128 devices in a mesh: group: 4 (over z), shard: 32 (over x, y, core).
Axes of the slice: x: 4, y: 4, z: 4, core: 2. Of those that a mesh axis runs over, the one named last changes fastest.
Arguments:
- embeddings: bfloat16 [49152, 768], P(('group', 'shard')), may hold values from -0.21875 to 0.21875
- members: int32 [49152], P(('group', 'shard')), may hold values from 0 to 8191, as said below
- counts: int32 [4, 32], replicated, may hold values from 96 to 384
Outputs:
- row_potential: float32 [49152], P(('group', 'shard'))
- col_potential: float32 [49152], P(('group', 'shard'))
- coarse_potential: float32 [8192], P(('group', 'shard'))
The draws below stay inside these ranges and needn't reach their ends.
Inputs may be any that keep to these rules, and one draw needn't show every extreme that they name: `members`: tracklets of shard index s (block b with b % 32 = s) name prototypes (k // (256 // 4)) * 32 * (256 // 4) + s * (256 // 4) + k % (256 // 4) for k below 256; every prototype is named by a tracklet at row r < 256 // 4 of some block.
All inputs are finite; a program needn't handle non-finite values.
Results may differ from the reference program's by a relative error of at most 0.0065.
Values may be sent and summed in bfloat16 or wider, within the bound.
No kernel may reach another device: no remote copies, remote signals or barrier semaphores. Data moves between devices by JAX's collectives and lax.ppermute only.
A program may use at most 128 MiB of HBM per device.

```python
import jax
import jax.numpy as jnp

D = 768
ROWS_DEV = 384
PROTO_BLOCK = 256
FINE_PRE = 2
FINE_POST = 1
COARSE = 2
TOKENS = 49152
PROTOS = 8192
N_GROUP = 4
N_SHARD = 32


def draw_members(key, part):
    key = jax.random.fold_in(key, 11)
    first, second = jax.random.split(key)
    quarter = PROTO_BLOCK // N_GROUP
    place = jnp.arange(TOKENS)
    grp = place // (ROWS_DEV * N_SHARD)
    shard_idx = place // ROWS_DEV % N_SHARD
    within = place % ROWS_DEV
    loose = jax.random.randint(first, (TOKENS,), 0, PROTO_BLOCK)
    perms = jax.vmap(lambda k: jax.random.permutation(k, PROTO_BLOCK))(jax.random.split(second, N_SHARD))
    fixed = perms[shard_idx, jnp.clip(grp * quarter + within, 0, PROTO_BLOCK - 1)]
    local = jnp.where(within < quarter, fixed, loose)
    return (local // quarter * N_SHARD * quarter + shard_idx * quarter + local % quarter).astype(jnp.int32)


def draw_counts(key, part):
    key = jax.random.fold_in(key, 23)
    first, second = jax.random.split(key)
    base = jax.random.randint(first, (N_GROUP * N_SHARD,), ROWS_DEV // 4, ROWS_DEV + 1)
    pick = jax.random.randint(second, (), 0, N_GROUP * N_SHARD)
    flat = jnp.where(jnp.arange(N_GROUP * N_SHARD) == pick, ROWS_DEV, base)
    return flat.reshape(N_GROUP, N_SHARD).astype(jnp.int32)


def levels(own_key, shape, shards, low, high):
    def one(axis_at, shards_of):
        steps = jax.random.uniform(jax.random.fold_in(jax.random.fold_in(own_key, 6), axis_at), (shards_of,), jnp.float32, low / len(shards), high / len(shards))
        return jnp.repeat(jnp.exp(steps), shape[axis_at] // shards_of).reshape((-1,) + (1,) * (len(shape) - axis_at - 1))

    loudness = one(*shards[0])
    for cut in shards[1:]:
        loudness = loudness * one(*cut)
    return loudness


def centred(rng, dims, width, reach, shards=(), held_as=jnp.bfloat16):
    result = jax.random.normal(rng, dims, jnp.float32) * width
    if len(shards) > 0:
        result = levels(rng, dims, shards, -0.22, 0.18) * result
    return jnp.clip(result, min=-reach, max=reach).astype(held_as)


def setup_inputs(seed: int = 0) -> dict:
    key_list = jax.random.split(jax.random.key(seed), 4)
    embeddings = centred(key_list[0], (TOKENS, D), D ** -0.5, 0.21875, ((0, 128),))
    members = draw_members(jax.random.fold_in(key_list[3], 71), 0)
    counts = draw_counts(jax.random.fold_in(key_list[3], 71), 0)
    return {"embeddings": embeddings, "members": members, "counts": counts}


EPS = 0.01
NEG = -1e30


def lse_update(cost, h, keep, log_mass, live):
    scores = jnp.where(keep, (h[None, :] - cost) / EPS, NEG)
    top = jnp.max(scores, axis=1)
    total = jnp.sum(jnp.exp(scores - top[:, None]), axis=1)
    out = EPS * log_mass - EPS * (top + jnp.log(total))
    return jnp.where(live, out, 0.0)


def reference(embeddings, members, counts):
    group_rows = ROWS_DEV * N_SHARD
    place = jnp.arange(TOKENS)
    valid = (place % ROWS_DEV) < counts.reshape(-1)[place // ROWS_DEV]
    costs = []
    keeps = []
    masses = []
    for grp in range(N_GROUP):
        block = embeddings[grp * group_rows:(grp + 1) * group_rows]
        costs.append(1.0 - jnp.dot(block, block.T, preferred_element_type=jnp.float32))
        live = valid[grp * group_rows:(grp + 1) * group_rows]
        idx = jnp.arange(group_rows)
        keeps.append(live[None, :] & (idx[:, None] != idx[None, :]))
        masses.append(-jnp.log(jnp.sum(live.astype(jnp.float32))))

    def fine(h):
        parts = []
        for grp in range(N_GROUP):
            sl = slice(grp * group_rows, (grp + 1) * group_rows)
            parts.append(lse_update(costs[grp], h[sl], keeps[grp], masses[grp], valid[sl]))
        return jnp.concatenate(parts)

    col_potential = jnp.zeros((TOKENS,), jnp.float32)
    row_potential = col_potential
    for step in range(FINE_PRE):
        row_potential = fine(col_potential)
        col_potential = fine(row_potential)
    weights = valid.astype(jnp.float32)
    sums = jax.ops.segment_sum(embeddings.astype(jnp.float32) * weights[:, None], members, PROTOS)
    sizes = jax.ops.segment_sum(weights, members, PROTOS)
    total = jnp.sum(weights)
    means = (sums / sizes[:, None]).astype(jnp.bfloat16)
    kcost = 1.0 - jnp.dot(means, means.T, preferred_element_type=jnp.float32)
    pidx = jnp.arange(PROTOS)
    pkeep = pidx[:, None] != pidx[None, :]
    plog = jnp.log(sizes / total)
    alive = jnp.ones((PROTOS,), bool)
    coarse_potential = jnp.zeros((PROTOS,), jnp.float32)
    for step in range(COARSE):
        upper = lse_update(kcost, coarse_potential, pkeep, plog, alive)
        coarse_potential = lse_update(kcost, upper, pkeep, plog, alive)
    row_potential = row_potential + jnp.where(valid, coarse_potential[members], 0.0)
    for step in range(FINE_POST):
        col_potential = fine(row_potential)
        row_potential = fine(col_potential)
    return row_potential, col_potential, coarse_potential
```

```python
import math

import jax
import jax.numpy as jnp
from jax import lax
from jax.experimental import pallas as pl
from jax.experimental.pallas import tpu as pltpu
from jax.sharding import Mesh, PartitionSpec as P


PROTO_BLOCK = 256
EPS = 0.01
SC = math.log2(math.e) / EPS
NEG = -1e30
LOW, HIGH = 2.0 ** -64, 2.0 ** 120
F32 = jnp.float32
BF16 = jnp.bfloat16
MIB = 2 ** 20
X, Y, Z = 4, 4, 4
PAD = 128

VMEM = pl.BlockSpec(memory_space=pltpu.VMEM)
SMEM = pl.BlockSpec(memory_space=pltpu.SMEM)
ANY = pl.BlockSpec(memory_space=pl.ANY)


def call(body, out_shape, in_specs, scratch=(), limit=24, name=None, flops=0, nbytes=0):
    return pl.pallas_call(
        body,
        out_shape=out_shape,
        in_specs=in_specs,
        out_specs=jax.tree.map(lambda _: VMEM, out_shape),
        scratch_shapes=list(scratch),
        compiler_params=pltpu.CompilerParams(vmem_limit_bytes=limit * MIB),
        cost_estimate=pl.CostEstimate(flops=flops, bytes_accessed=nbytes, transcendentals=0),
        name=name,
    )


def sds(shape, dtype=F32):
    return jax.ShapeDtypeStruct(shape, dtype)


def iota(shape, dim):
    return lax.broadcasted_iota(jnp.int32, shape, dim)


def to_lanes(col):
    n = col.shape[0]
    eye = iota((128, 128), 0) == iota((128, 128), 1)
    return jnp.concatenate(
        [
            jnp.sum(jnp.where(eye, col[k * 128:(k + 1) * 128], 0.0), axis=0, keepdims=True)
            for k in range(n // 128)
        ],
        axis=0,
    )


def to_rows(vals, out_ref):
    for k in range(vals.shape[0]):
        out_ref[k * 128:(k + 1) * 128, :] = jnp.transpose(
            jnp.broadcast_to(vals[k:k + 1, :], (128, 128))
        )


def lse2(parts):
    top = parts[0]
    for p in parts[1:]:
        top = jnp.maximum(top, p)
    total = jnp.exp2(parts[0] - top)
    for p in parts[1:]:
        total = total + jnp.exp2(p - top)
    return top + jnp.log2(total)


def in_range(total):
    return jnp.sum(jnp.where((total > LOW) & (total < HIGH), 0.0, 1.0)) == 0.0


def reduce_columns(tile, h, out_ref, wide_ref):
    rows, cols = tile.shape
    shift = jnp.max(h)
    lane, sub = iota((8, 128), 1), iota((8, 128), 0)

    def spread(by):
        for k in range(cols // 128):
            wide_ref[:, k * 128:(k + 1) * 128] = jnp.broadcast_to(h[k:k + 1, :] - by, (8, 128))

    spread(shift)

    def fast(r, _):
        acc = jnp.zeros((8, 128), F32)
        for g in range(16):
            s = tile[pl.ds(pl.multiple_of(r * 128 + g * 8, 8), 8), :] + wide_ref[...]
            part = jnp.sum(jnp.exp2(s), axis=1, keepdims=True)
            acc = acc + jnp.where(lane == sub + 8 * g, part, 0.0)
        out_ref[pl.ds(r, 1), :] = jnp.sum(acc, axis=0, keepdims=True)
        return 0

    lax.fori_loop(0, rows // 128, fast, 0, unroll=2)
    total = out_ref[0:rows // 128, :]
    good = in_range(total)

    @pl.when(good)
    def _():
        out_ref[0:rows // 128, :] = jnp.log2(total) + shift

    @pl.when(jnp.logical_not(good))
    def _():
        spread(0.0)

        def safe(r, _):
            acc = jnp.zeros((8, 128), F32)
            for g in range(16):
                s = tile[pl.ds(pl.multiple_of(r * 128 + g * 8, 8), 8), :] + wide_ref[...]
                top = jnp.max(s, axis=1, keepdims=True)
                part = top + jnp.log2(jnp.sum(jnp.exp2(s - top), axis=1, keepdims=True))
                acc = acc + jnp.where(lane == sub + 8 * g, part, 0.0)
            out_ref[pl.ds(r, 1), :] = jnp.sum(acc, axis=0, keepdims=True)
            return 0

        lax.fori_loop(0, rows // 128, safe, 0)


def safe_rows(tile, tall_ref, out_ref):
    rows, cols = tile.shape
    width, chunk = 128, 128
    for strip in range(cols // width):
        at = pl.ds(strip * width, width)

        def safe(c, carry):
            top, total = carry
            part = pl.ds(pl.multiple_of(c * chunk, chunk), chunk)
            s = (tile[part, at] + tall_ref[part, :]).reshape(chunk // 8, 8, width)
            now = jnp.maximum(top, jnp.max(s, axis=0))
            return now, total * jnp.exp2(top - now) + jnp.sum(jnp.exp2(s - now[None]), axis=0)

        top, total = lax.fori_loop(
            0, rows // chunk, safe, (jnp.full((8, width), NEG, F32), jnp.zeros((8, width), F32))
        )
        best = jnp.max(top, axis=0, keepdims=True)
        total = jnp.sum(total * jnp.exp2(top - best), axis=0, keepdims=True)
        out_ref[strip:strip + 1, :] = best + jnp.log2(total)


def reduce_rows(tile, h, out_ref, tall_ref):
    rows, cols = tile.shape
    shift = jnp.max(h)
    to_rows(h - shift, tall_ref)
    width = 256
    chunk = 64
    groups = width // 128
    for strip in range(cols // width):
        at = pl.ds(strip * width, width)

        def fast(c, acc):
            part = pl.ds(pl.multiple_of(c * chunk, chunk), chunk)
            add = tall_ref[part, :]
            s = tile[part, at] + jnp.concatenate([add] * groups, axis=1)
            return acc + jnp.sum(jnp.exp2(s).reshape(chunk // 8, 8, width), axis=0)

        acc = lax.fori_loop(0, rows // chunk, fast, jnp.zeros((8, width), F32), unroll=2)
        acc = jnp.sum(acc, axis=0, keepdims=True)
        for k in range(groups):
            row = strip * groups + k
            out_ref[row:row + 1, :] = acc[:, k * 128:(k + 1) * 128]
    total = out_ref[0:cols // 128, :]
    good = in_range(total)

    @pl.when(good)
    def _():
        out_ref[0:cols // 128, :] = jnp.log2(total) + shift

    @pl.when(jnp.logical_not(good))
    def _():
        to_rows(h, tall_ref)
        safe_rows(tile, tall_ref, out_ref)


def place(idx):
    return idx[0], idx[1], idx[2], idx[3]


def count_at(counts, z, x, y, c):
    return counts[z, (x * Y + y) * 2 + c]


def row_counts(counts, idx):
    z, x, y, c = place(idx)
    return [count_at(counts, z, x, lax.rem(y + dy, Y), lax.rem(c + dc, 2)) for dc in range(2) for dy in range(Y)]


def col_counts(counts, idx):
    z, x, y, c = place(idx)
    return [count_at(counts, z, lax.rem(x + dx, X), y, c) for dx in range(X)]


def group_total(counts, idx):
    n = counts[idx[0], 0]
    for s in range(1, X * Y * 2):
        n = n + counts[idx[0], s]
    return n


def live_mask(shape, block_counts, per):
    at = iota((per, 128), 0) * 128 + iota((per, 128), 1)
    return jnp.concatenate([jnp.where(at < n, 1.0, 0.0) for n in block_counts], axis=0) > 0.0


def log2_of(n):
    return jnp.log2(jnp.full((1, 128), n, jnp.int32).astype(F32))


def from_columns(parts, first, per):
    blocks = []
    for dx in range(X):
        blocks.append(
            lse2([p[first + (dx + k) % X * per:first + (dx + k) % X * per + per, :] for k, p in enumerate(parts)])
        )
    return jnp.concatenate(blocks, axis=0)


def gather_columns(parts, first, per):
    return jnp.concatenate([parts[(X - dx) % X][first:first + per, :] for dx in range(X)], axis=0)


def fold_y(parts, first, per):
    blocks = []
    for dc in range(2):
        for dy in range(Y):
            rows = [first + (dc * Y + (dy + k) % Y) * per for k in range(Y)]
            blocks.append(lse2([p[r:r + per, :] for p, r in zip(parts, rows)]))
    return jnp.concatenate(blocks, axis=0)


def fold_core(mine, other, first, per):
    half = Y * per
    return jnp.concatenate(
        [
            lse2([mine[first:first + half, :], other[first + half:first + 2 * half, :]]),
            lse2([mine[first + half:first + 2 * half, :], other[first:first + half, :]]),
        ],
        axis=0,
    )


def pool_kernel(counts, idx, emb, members, own, far1, far2, far3):
    z, x, y, c = place(idx)
    quarter = PROTO_BLOCK // Z
    ids = members[...]
    turn = lax.rem(lax.shift_right_logical(ids, 11) - z + Z, Z)
    local = turn * quarter + jnp.bitwise_and(ids, quarter - 1)
    rows = emb.shape[0]
    live = iota((1, rows), 1) < count_at(counts, z, x, y, c)
    hot = ((iota((PROTO_BLOCK, rows), 0) == local) & live).astype(BF16)
    sums = jnp.dot(hot, emb[...], preferred_element_type=F32)
    sizes = jnp.dot(hot, jnp.ones((rows, PAD), BF16), preferred_element_type=F32)
    d = emb.shape[1]
    own[:, 0:d] = sums[0:quarter]
    own[:, d:] = sizes[0:quarter]
    coded = code_sizes(sizes)
    for k, ref in ((1, far1), (2, far2), (3, far3)):
        ref[:, 0:d] = sums[k * quarter:(k + 1) * quarter].astype(BF16)
        ref[:, d:] = coded[k * quarter:(k + 1) * quarter]


def code_sizes(sizes):
    high = jnp.floor(sizes * (1.0 / 256.0))
    low = sizes - 256.0 * high
    return jnp.where(iota(sizes.shape, 1) < 64, high, low).astype(BF16)


def read_sizes(block, d):
    coded = block[:, d:].astype(F32)
    return coded[:, 0:1] * 256.0 + coded[:, 64:65]


def means_kernel(own, far1, far2, far3, out):
    d = own.shape[1] - PAD
    sums = own[:, 0:d]
    sizes = own[:, d:d + 1]
    for ref in (far1, far2, far3):
        block = ref[...]
        sums = sums + block[:, 0:d].astype(F32)
        sizes = sizes + read_sizes(block, d)
    out[:, 0:d] = (sums / sizes).astype(BF16)
    out[:, d:] = code_sizes(jnp.broadcast_to(sizes, (sizes.shape[0], PAD)))


def join_kernel(counts, own, far1, far2, far3, means, plog):
    d = own.shape[1] - PAD
    quarter = own.shape[0]
    total = counts[0, 0]
    for z in range(Z):
        for s in range(X * Y * 2):
            if z + s > 0:
                total = total + counts[z, s]
    sizes = []
    for k, ref in enumerate((own, far1, far2, far3)):
        block = ref[...]
        means[k * quarter:(k + 1) * quarter, :] = block[:, 0:d]
        sizes.append(jnp.broadcast_to(read_sizes(block, d), (quarter, 128)))
    plog[...] = jnp.zeros(plog.shape, F32)
    plog[0:2, :] = jnp.log2(to_lanes(jnp.concatenate(sizes, axis=0))) - log2_of(total)


def fetch(pieces, buf, sems):
    size = sum(p.shape[0] for p in pieces[0])
    for b, parts in enumerate(pieces):
        at = b * size
        for p in parts:
            n = p.shape[0]
            pltpu.make_async_copy(p, buf.at[pl.ds(at, n)], sems.at[b]).start()
            at += n

    def wait(b):
        into = buf.at[pl.ds(b * size, size)]
        pltpu.make_async_copy(into, into, sems.at[b]).wait()

    return wait


def tile_of(own, xs, ys, rows_buf, cols_buf, row_sems, col_sems):
    xa, xb, xc, xd = xs
    ya, yb, yc, yd, so, sa, sb, sc, sd = ys
    wait_cols = fetch([[own], [xb], [xc, xd], [xa]], cols_buf, col_sems)
    wait_rows = fetch([[own], [yb], [yc, yd], [ya], [so], [sb], [sc, sd], [sa]], rows_buf, row_sems)
    for b in range(X):
        wait_cols(b)
    for b in range(2 * Y):
        wait_rows(b)


def dot_t(a, b):
    return lax.dot_general(a, b, (((1,), (1,)), ((), ())), preferred_element_type=F32) * SC


def coarse_tile_kernel(own, *refs):
    xs, ys = refs[0:4], refs[4:13]
    plog, tile, payload, rows_buf, cols_buf, row_sems, col_sems, wide = refs[13:]
    tile_of(own, xs, ys, rows_buf, cols_buf, row_sems, col_sems)
    rows, cols = tile.shape
    step = 256

    def body(i, _):
        at = pl.ds(pl.multiple_of(i * step, step), step)
        tile[at, :] = dot_t(rows_buf[at, :], cols_buf[...])
        return 0

    lax.fori_loop(0, rows // step, body, 0)
    n = own.shape[0]
    eye = iota((n, n), 0) == iota((n, n), 1)
    tile[0:n, 0:n] = jnp.where(eye, NEG, tile[0:n, 0:n])
    payload[...] = jnp.zeros(payload.shape, F32)
    reduce_columns(tile, jnp.zeros((cols // 128, 128), F32), payload, wide)
    payload[rows // 128:rows // 128 + 2, :] = plog[0:2, :]


def fine_tile_kernel(counts, idx, own, *refs):
    xs, ys = refs[0:4], refs[4:13]
    tile, part, rows_buf, cols_buf, row_sems, col_sems, tall, acc = refs[13:]
    n = own.shape[0]
    for b, count in enumerate(row_counts(counts, idx)):
        tall[b * n:(b + 1) * n, :] = jnp.where(iota((n, 128), 0) < count, 0.0, NEG)
    tile_of(own, xs, ys, rows_buf, cols_buf, row_sems, col_sems)
    rows, cols = tile.shape
    step, wide = 256, 512
    acc[...] = jnp.zeros(acc.shape, F32)

    def body(i, _):
        at = pl.ds(pl.multiple_of(i * step, step), step)
        for j in range(cols // wide):
            across = pl.ds(j * wide, wide)
            s = dot_t(rows_buf[at, :], cols_buf[across, :])
            same = iota((step, wide), 0) + i * step == iota((step, wide), 1) + j * wide
            if j * wide < n:
                s = jnp.where(same & (iota((step, wide), 1) + j * wide < n), NEG, s)
            tile[at, across] = s
            s = s + jnp.concatenate([tall[at, :]] * (wide // 128), axis=1)
            acc[:, across] += jnp.sum(jnp.exp2(s).reshape(step // 8, 8, wide), axis=0)
        return 0

    lax.fori_loop(0, rows // step, body, 0)
    total = jnp.sum(acc[...], axis=0, keepdims=True)
    for k in range(cols // 128):
        part[k:k + 1, :] = total[:, k * 128:(k + 1) * 128]
    total = part[0:cols // 128, :]
    good = in_range(total)

    @pl.when(good)
    def _():
        part[0:cols // 128, :] = jnp.log2(total)

    @pl.when(jnp.logical_not(good))
    def _():
        safe_rows(tile, tall, part)


def fold_y_kernel(plan, *refs):
    parts, out = refs[0:Y], refs[Y]
    out[...] = jnp.zeros(out.shape, F32)
    for first, per in plan["lse"]:
        n = 2 * Y * per
        out[first:first + n, :] = fold_y(parts, first, per)
    if plan["plog"] is not None:
        first, into = plan["plog"]
        out[into:into + 2 * Y, :] = jnp.concatenate(
            [parts[(Y - dy) % Y][first:first + 2, :] for dy in range(Y)], axis=0
        )


def coarse2_kernel(mine, other, part, plog, members, tile, payload, plog_rows, tall):
    plog_rows[0:8, :] = mine[16:24, :]
    plog_rows[8:16, :] = other[16:24, :]
    h = plog_rows[...] + SC - fold_core(mine, other, 0, 2)
    payload[...] = jnp.zeros(payload.shape, F32)
    reduce_rows(tile, h, payload, tall)
    payload[8:20, :] = part[...]
    payload[20:22, :] = plog[0:2, :]
    payload[22:25, :] = members[...].astype(F32)


def fine_h(lse, counts, idx, block_counts, per):
    live = live_mask(lse.shape, block_counts, per)
    return live, SC - log2_of(group_total(counts, idx)) - lse


def step3_kernel(counts, idx, p0, p1, p2, p3, ktile, tile, payload, plog_cols, members, wide, kwide):
    parts = (p0, p1, p2, p3)
    plog_cols[...] = gather_columns(parts, 20, 2)
    members[...] = gather_columns(parts, 22, 3)
    payload[...] = jnp.zeros(payload.shape, F32)
    live, h = fine_h(from_columns(parts, 8, 3), counts, idx, col_counts(counts, idx), 3)
    reduce_columns(tile, jnp.where(live, h, NEG), payload.at[16:40, :], wide)
    h = plog_cols[...] + SC - from_columns(parts, 0, 2)
    reduce_columns(ktile, h, payload.at[0:16, :], kwide)


def step4_kernel(counts, idx, mine, other, plog_rows, ktile, tile, payload, tall, ktall):
    payload[...] = jnp.zeros(payload.shape, F32)
    h = plog_rows[...] + SC - fold_core(mine, other, 0, 2)
    reduce_rows(ktile, h, payload.at[0:8, :], ktall)
    live, h = fine_h(fold_core(mine, other, 16, 3), counts, idx, row_counts(counts, idx), 3)
    reduce_rows(tile, jnp.where(live, h, NEG), payload.at[8:20, :], tall)


def step5_kernel(counts, idx, p0, p1, p2, p3, plog_cols, members, tile, payload, coarse, tall, wide):
    z = idx[0]
    parts = (p0, p1, p2, p3)
    v = plog_cols[...] + SC - from_columns(parts, 0, 2)
    coarse[...] = v[0:1, :] * (1.0 / SC)
    to_rows(v, tall)
    ids = members[...].astype(jnp.int32)
    turn = lax.rem(z + Z - lax.shift_right_logical(ids, 11), Z)
    local = turn * (PROTO_BLOCK // Z) + jnp.bitwise_and(ids, PROTO_BLOCK // Z - 1)
    boost = []
    for k in range(X * 3):
        vals = tall[(k // 3) * PROTO_BLOCK:(k // 3 + 1) * PROTO_BLOCK, :]
        pick = iota((PROTO_BLOCK, 128), 0) == local[k:k + 1, :]
        boost.append(jnp.sum(jnp.where(pick, vals, 0.0), axis=0, keepdims=True))
    live, h = fine_h(from_columns(parts, 8, 3), counts, idx, col_counts(counts, idx), 3)
    h = jnp.where(live, h + jnp.concatenate(boost, axis=0), NEG)
    payload[...] = jnp.zeros(payload.shape, F32)
    reduce_columns(tile, h, payload, wide)


def step6_kernel(counts, idx, mine, other, tile, payload, out, tall):
    live, h = fine_h(fold_core(mine, other, 0, 3), counts, idx, row_counts(counts, idx), 3)
    out[...] = jnp.where(live, h, 0.0)[0:3, :] * (1.0 / SC)
    payload[...] = jnp.zeros(payload.shape, F32)
    reduce_rows(tile, jnp.where(live, h, NEG), payload, tall)


def last_kernel(counts, idx, p0, p1, p2, p3, out):
    parts = (p0, p1, p2, p3)
    live, h = fine_h(from_columns(parts, 0, 3), counts, idx, col_counts(counts, idx), 3)
    out[...] = jnp.where(live, h, 0.0)[0:3, :] * (1.0 / SC)


def hop(v, axis, k):
    n = {"x": X, "y": Y, "z": Z, "c": 2}[axis]
    return lax.ppermute(v, axis, [(i, (i + k) % n) for i in range(n)])


def spread_over(v, axis):
    return [v] + [hop(v, axis, k) for k in (1, 2, 3)]


def ring_start(v, axis):
    return hop(v, axis, 1), hop(v, axis, 3)


def ring_end(a, b, axis):
    half = a.shape[0] // 2
    return hop(a[:half], axis, 1), hop(b[half:], axis, 3)


def local(embeddings, members, counts):
    rows, d = embeddings.shape
    idx = jnp.stack([lax.axis_index(a) for a in ("z", "x", "y", "c")]).astype(jnp.int32)
    lanes = members.reshape(1, rows)
    lanes3 = members.reshape(rows // 128, 128)
    n_rows, n_cols = rows * Y * 2, rows * X
    k_rows, k_cols = PROTO_BLOCK * Y * 2, PROTO_BLOCK * X
    quarter = PROTO_BLOCK // Z

    xa, xb = ring_start(embeddings, "x")
    ya, yb = ring_start(embeddings, "y")
    so = hop(embeddings, "c", 1)
    own, far1, far2, far3 = call(
        pool_kernel,
        [sds((quarter, d + PAD))] + [sds((quarter, d + PAD), BF16)] * 3,
        [SMEM, SMEM, VMEM, VMEM],
        name="pool",
    )(counts, idx, embeddings, lanes)
    got = [hop(far1, "z", 1), hop(far2, "z", 2), hop(far3, "z", 3)]
    part = call(means_kernel, sds((quarter, d + PAD), BF16), [VMEM] * 4, name="means")(own, *got)
    means, plog = call(
        join_kernel, [sds((PROTO_BLOCK, d), BF16), sds((8, 128))], [SMEM] + [VMEM] * 4, name="join"
    )(counts, *spread_over(part, "z"))

    mxa, mxb = ring_start(means, "x")
    mya, myb = ring_start(means, "y")
    mso = hop(means, "c", 1)
    mxc, mxd = ring_end(mxa, mxb, "x")
    myc, myd = ring_end(mya, myb, "y")
    msa, msb, msc, msd = [hop(v, "c", 1) for v in (mya, myb, myc, myd)]

    xc, xd = ring_end(xa, xb, "x")
    yc, yd = ring_end(ya, yb, "y")
    sa, sb, sc, sd = [hop(v, "c", 1) for v in (ya, yb, yc, yd)]

    ktile, part = call(
        coarse_tile_kernel,
        [pltpu.VMEM((k_rows, k_cols), F32), sds((24, 128))],
        [ANY] * 14 + [VMEM],
        scratch=[
            pltpu.VMEM((k_rows, d), BF16),
            pltpu.VMEM((k_cols, d), BF16),
            pltpu.SemaphoreType.DMA((2 * Y,)),
            pltpu.SemaphoreType.DMA((X,)),
            pltpu.VMEM((8, k_cols), F32),
        ],
        name="coarse_tile",
        flops=2 * k_rows * k_cols * d,
    )(means, mxa, mxb, mxc, mxd, mya, myb, myc, myd, mso, msa, msb, msc, msd, plog)
    mine = call(
        lambda *r: fold_y_kernel({"lse": [(0, 2)], "plog": (16, 16)}, *r),
        sds((24, 128)),
        [VMEM] * 4,
        name="fold_y1",
    )(*spread_over(part, "y"))
    other = hop(mine, "c", 1)

    tile, upart = call(
        fine_tile_kernel,
        [pltpu.VMEM((n_rows, n_cols), F32), sds((n_cols // 128, 128))],
        [SMEM, SMEM] + [ANY] * 14,
        scratch=[
            pltpu.VMEM((n_rows, d), BF16),
            pltpu.VMEM((n_cols, d), BF16),
            pltpu.SemaphoreType.DMA((2 * Y,)),
            pltpu.SemaphoreType.DMA((X,)),
            pltpu.VMEM((n_rows, 128), F32),
            pltpu.VMEM((8, n_cols), F32),
        ],
        name="fine_tile",
        flops=2 * n_rows * n_cols * d,
    )(counts, idx, embeddings, xa, xb, xc, xd, ya, yb, yc, yd, so, sa, sb, sc, sd)

    tall = pltpu.VMEM((n_rows, 128), F32)
    wide = pltpu.VMEM((8, n_cols), F32)
    part, plog_rows = call(
        coarse2_kernel,
        [sds((32, 128)), sds((16, 128))],
        [VMEM] * 6,
        scratch=[pltpu.VMEM((k_rows, 128), F32)],
        name="coarse2",
    )(mine, other, upart, plog, lanes3, ktile)

    part, plog_cols, ids = call(
        step3_kernel,
        [sds((40, 128)), sds((8, 128)), sds((12, 128))],
        [SMEM, SMEM] + [VMEM] * 6,
        scratch=[wide, pltpu.VMEM((8, k_cols), F32)],
        name="step3",
    )(counts, idx, *spread_over(part, "x"), ktile, tile)
    mine = call(
        lambda *r: fold_y_kernel({"lse": [(0, 2), (16, 3)], "plog": None}, *r),
        sds((40, 128)),
        [VMEM] * 4,
        name="fold_y2",
    )(*spread_over(part, "y"))
    other = hop(mine, "c", 1)

    part = call(
        step4_kernel,
        sds((24, 128)),
        [SMEM, SMEM] + [VMEM] * 5,
        scratch=[tall, pltpu.VMEM((k_rows, 128), F32)],
        name="step4",
    )(counts, idx, mine, other, plog_rows, ktile, tile)

    part, coarse = call(
        step5_kernel,
        [sds((24, 128)), sds((1, 128))],
        [SMEM, SMEM] + [VMEM] * 7,
        scratch=[pltpu.VMEM((k_cols, 128), F32), wide],
        name="step5",
    )(counts, idx, *spread_over(part, "x"), plog_cols, ids, tile)
    mine = call(
        lambda *r: fold_y_kernel({"lse": [(0, 3)], "plog": None}, *r),
        sds((24, 128)),
        [VMEM] * 4,
        name="fold_y3",
    )(*spread_over(part, "y"))
    other = hop(mine, "c", 1)

    part, col = call(
        step6_kernel,
        [sds((16, 128)), sds((3, 128))],
        [SMEM, SMEM] + [VMEM] * 3,
        scratch=[tall],
        name="step6",
    )(counts, idx, mine, other, tile)
    row = call(last_kernel, sds((3, 128)), [SMEM, SMEM] + [VMEM] * 4, name="last")(
        counts, idx, *spread_over(part, "x")
    )
    return row.reshape(rows), col.reshape(rows), coarse[0, :quarter]


def solution(mesh):
    split = Mesh(mesh.devices.reshape(Z, X, Y, 2), ("z", "x", "y", "c"))
    every = P(("z", "x", "y", "c"))
    return jax.shard_map(
        local,
        mesh=split,
        in_specs=(P(("z", "x", "y", "c"), None), every, P()),
        out_specs=(every, every, every),
        check_vma=False,
    )
```

```python
import math

import jax
import jax.numpy as jnp
from jax import lax
from jax.experimental import pallas as pl
from jax.experimental.pallas import tpu as pltpu
from jax.sharding import Mesh, PartitionSpec as P


PROTO_BLOCK = 256
EPS = 0.01
SC = math.log2(math.e) / EPS
NEG = -1e30
LOW, HIGH, PEAK = 2.0 ** -48, 2.0 ** 120, 2.0 ** 40
STEP = 256
F32 = jnp.float32
BF16 = jnp.bfloat16
MIB = 2 ** 20
X, Y, Z = 4, 4, 4
PAD = 128

VMEM = pl.BlockSpec(memory_space=pltpu.VMEM)
SMEM = pl.BlockSpec(memory_space=pltpu.SMEM)
ANY = pl.BlockSpec(memory_space=pl.ANY)


HBM = pltpu.MemorySpace.HBM
IN_HBM = pl.BlockSpec(memory_space=HBM)


def call(body, out_shape, in_specs, scratch=(), out_specs=None, limit=6, name=None, flops=0, nbytes=0):
    return pl.pallas_call(
        body,
        out_shape=out_shape,
        in_specs=in_specs,
        out_specs=out_specs or jax.tree.map(lambda _: VMEM, out_shape),
        scratch_shapes=list(scratch),
        compiler_params=pltpu.CompilerParams(vmem_limit_bytes=limit * MIB),
        cost_estimate=pl.CostEstimate(flops=flops, bytes_accessed=nbytes, transcendentals=0),
        name=name,
    )


def sds(shape, dtype=F32):
    return jax.ShapeDtypeStruct(shape, dtype)


def iota(shape, dim):
    return lax.broadcasted_iota(jnp.int32, shape, dim)


def to_lanes(col):
    n = col.shape[0]
    eye = iota((128, 128), 0) == iota((128, 128), 1)
    return jnp.concatenate(
        [
            jnp.sum(jnp.where(eye, col[k * 128:(k + 1) * 128], 0.0), axis=0, keepdims=True)
            for k in range(n // 128)
        ],
        axis=0,
    )


def to_rows(vals, out_ref):
    for k in range(vals.shape[0]):
        out_ref[k * 128:(k + 1) * 128, :] = jnp.transpose(
            jnp.broadcast_to(vals[k:k + 1, :], (128, 128))
        )


def lse2(parts):
    top = parts[0]
    for p in parts[1:]:
        top = jnp.maximum(top, p)
    total = jnp.exp2(parts[0] - top)
    for p in parts[1:]:
        total = total + jnp.exp2(p - top)
    return top + jnp.log2(total)


def in_range(total, peak):
    outside = jnp.sum(jnp.where((total > LOW) & (total < HIGH), 0.0, 1.0))
    return (outside == 0.0) & (peak <= PEAK)


def spread(vals, wide_ref):
    for k in range(vals.shape[0]):
        wide_ref[:, k * 128:(k + 1) * 128] = jnp.broadcast_to(vals[k:k + 1, :], (8, 128))


def store_lse(total, shift, peak, out_ref, safe):
    n = total.shape[0]
    good = in_range(total, peak)

    @pl.when(good)
    def _():
        out_ref[0:n, :] = jnp.log2(total) + shift

    @pl.when(jnp.logical_not(good))
    def _():
        safe()


def reduce_columns(tile, h, guard, out_ref, wide_ref, backup):
    rows, cols = tile.shape
    shift = jnp.max(h)
    spread(jnp.exp2(h - shift), wide_ref)
    lane, sub = iota((8, 128), 1), iota((8, 128), 0)

    def body(r, _):
        acc = jnp.zeros((8, 128), F32)
        for g in range(16):
            s = tile[pl.ds(pl.multiple_of(r * 128 + g * 8, 8), 8), :] * wide_ref[...]
            part = jnp.sum(s, axis=1, keepdims=True)
            acc = acc + jnp.where(lane == sub + 8 * g, part, 0.0)
        out_ref[pl.ds(r, 1), :] = jnp.sum(acc, axis=0, keepdims=True)
        return 0

    lax.fori_loop(0, rows // 128, body, 0, unroll=4)
    store_lse(
        out_ref[0:rows // 128, :], shift, jnp.max(guard[...]), out_ref,
        lambda: safe_columns(backup, h, out_ref),
    )


def reduce_rows(tile, h, guard, out_ref, tall_ref, backup):
    rows, cols = tile.shape
    shift = jnp.max(h)
    to_rows(jnp.exp2(h - shift), tall_ref)
    width, chunk = 512, 64
    groups = width // 128
    for strip in range(cols // width):
        at = pl.ds(strip * width, width)

        def body(c, acc):
            part = pl.ds(pl.multiple_of(c * chunk, chunk), chunk)
            s = tile[part, at] * jnp.concatenate([tall_ref[part, :]] * groups, axis=1)
            return acc + jnp.sum(s.reshape(chunk // 8, 8, width), axis=0)

        acc = lax.fori_loop(0, rows // chunk, body, jnp.zeros((8, width), F32), unroll=2)
        acc = jnp.sum(acc, axis=0, keepdims=True)
        for k in range(groups):
            row = strip * groups + k
            out_ref[row:row + 1, :] = acc[:, k * 128:(k + 1) * 128]
    store_lse(
        out_ref[0:cols // 128, :], shift, jnp.max(guard[...]), out_ref,
        lambda: safe_rows(backup, h, out_ref, tall_ref),
    )


def block_scores(backup, ci, cj):
    rows_hbm, cols_hbm, own, a_buf, b_buf, sem = backup
    for src, at, buf in ((rows_hbm, ci, a_buf), (cols_hbm, cj, b_buf)):
        copy = pltpu.make_async_copy(src.at[pl.ds(pl.multiple_of(at * STEP, STEP), STEP)], buf, sem)
        copy.start()
        copy.wait()
    s = dot_t(a_buf[...], b_buf[...])
    i, j = iota((STEP, STEP), 0) + ci * STEP, iota((STEP, STEP), 1) + cj * STEP
    return jnp.where((i == j) & (j < own), NEG, s)


def safe_columns(backup, h, out_ref):
    n, m = backup[0].shape[0] // STEP, backup[1].shape[0] // STEP

    def by_rows(ci, _):
        top, total = jnp.full((STEP, 1), NEG, F32), jnp.zeros((STEP, 1), F32)
        for cj in range(m):
            add = jnp.concatenate([h[2 * cj:2 * cj + 1, :], h[2 * cj + 1:2 * cj + 2, :]], axis=1)
            s = block_scores(backup, ci, cj) + add
            now = jnp.maximum(top, jnp.max(s, axis=1, keepdims=True))
            total = total * jnp.exp2(top - now) + jnp.sum(jnp.exp2(s - now), axis=1, keepdims=True)
            top = now
        lanes = to_lanes(jnp.broadcast_to(top + jnp.log2(total), (STEP, 128)))
        for k in range(STEP // 128):
            out_ref[pl.ds(ci * (STEP // 128) + k, 1), :] = lanes[k:k + 1, :]
        return 0

    lax.fori_loop(0, n, by_rows, 0)


def safe_rows(backup, h, out_ref, tall_ref):
    n, m = backup[0].shape[0] // STEP, backup[1].shape[0] // STEP
    to_rows(h, tall_ref)
    for cj in range(m):

        def by_rows(ci, carry):
            top, total = carry
            add = tall_ref[pl.ds(pl.multiple_of(ci * STEP, STEP), STEP), :]
            s = block_scores(backup, ci, cj) + jnp.concatenate([add] * (STEP // 128), axis=1)
            now = jnp.maximum(top, jnp.max(s, axis=0, keepdims=True))
            return now, total * jnp.exp2(top - now) + jnp.sum(jnp.exp2(s - now), axis=0, keepdims=True)

        top, total = lax.fori_loop(
            0, n, by_rows, (jnp.full((1, STEP), NEG, F32), jnp.zeros((1, STEP), F32))
        )
        lse = top + jnp.log2(total)
        for k in range(STEP // 128):
            row = cj * (STEP // 128) + k
            out_ref[row:row + 1, :] = lse[:, k * 128:(k + 1) * 128]


def info_place(info):
    return info[Z, 0], info[Z, 1], info[Z, 2], info[Z, 3]


def count_at(counts, z, x, y, c):
    return counts[z, (x * Y + y) * 2 + c]


def behind(at, c, k, n):
    return lax.rem(at + jnp.where(c == 0, n - k, k), n)


def row_counts(counts, idx):
    z, x, y, c = idx
    return [
        count_at(counts, z, x, behind(y, (c + dc) % 2, k, Y), (c + dc) % 2) for dc in range(2) for k in range(Y)
    ]


def col_counts(counts, idx):
    z, x, y, c = idx
    return [count_at(counts, z, behind(x, c, k, X), y, c) for k in range(X)]


def live_mask(block_counts, per):
    at = iota((per, 128), 0) * 128 + iota((per, 128), 1)
    return jnp.concatenate([jnp.where(at < n, 1.0, 0.0) for n in block_counts], axis=0)


def log2_of(n):
    return jnp.log2(jnp.full((1, 128), n, jnp.int32).astype(F32))


def from_columns(parts, first, per):
    blocks = []
    for j in range(X):
        rows = [first + (j - k) % X * per for k in range(X)]
        blocks.append(lse2([p[r:r + per, :] for p, r in zip(parts, rows)]))
    return jnp.concatenate(blocks, axis=0)


def gather_columns(parts, first, per):
    return jnp.concatenate([p[first:first + per, :] for p in parts], axis=0)


def fold_y(parts, first, per):
    blocks = []
    for dc in range(2):
        for j in range(Y):
            rows = [first + (dc * Y + (j - k if dc == 0 else j + k) % Y) * per for k in range(Y)]
            blocks.append(lse2([p[r:r + per, :] for p, r in zip(parts, rows)]))
    return jnp.concatenate(blocks, axis=0)


def fold_core(mine, other, first, per):
    half = Y * per
    return jnp.concatenate(
        [
            lse2([mine[first:first + half, :], other[first + half:first + 2 * half, :]]),
            lse2([mine[first + half:first + 2 * half, :], other[first:first + half, :]]),
        ],
        axis=0,
    )


def pool_kernel(info, emb, members, sums, live_rows, live_cols, seat, logs):
    idx = info_place(info)
    z, x, y, c = idx
    quarter = PROTO_BLOCK // Z
    per = members.shape[0]
    ids = members[...]
    which = lax.shift_right_logical(ids, 11)
    within = jnp.bitwise_and(ids, quarter - 1)
    seat[...] = (lax.rem(z - which + Z, Z) * quarter + within).astype(F32)
    local = jnp.concatenate([(which * quarter + within)[k:k + 1, :] for k in range(per)], axis=1)
    rows, d = emb.shape
    live = iota((1, rows), 1) < count_at(info, z, x, y, c)
    hot = ((iota((PROTO_BLOCK, rows), 0) == local) & live).astype(BF16)
    sums[:, 0:d] = jnp.dot(hot, emb[...], preferred_element_type=F32)
    sums[:, d:] = jnp.dot(hot, jnp.ones((rows, PAD), BF16), preferred_element_type=F32)
    live_rows[...] = live_mask(row_counts(info, idx), per)
    live_cols[...] = live_mask(col_counts(info, idx), per)
    mine, total = 0, 0
    for g in range(Z):
        n = info[g, 0]
        for s in range(1, X * Y * 2):
            n = n + info[g, s]
        mine = mine + jnp.where(g == z, n, 0)
        total = total + n
    logs[...] = jnp.concatenate([log2_of(mine), log2_of(total), jnp.zeros((6, 128), F32)], axis=0)


def code_sizes(sizes):
    high = jnp.floor(sizes * (1.0 / 256.0))
    low = sizes - 256.0 * high
    return jnp.where(iota(sizes.shape, 1) < 64, high, low).astype(BF16)


def read_sizes(block, d):
    coded = block[:, d:].astype(F32)
    return coded[:, 0:1] * 256.0 + coded[:, 64:65]


def means_kernel(got, out):
    quarter, width = out.shape
    d = width - PAD
    sums = got[0:quarter, :]
    for k in range(1, Z):
        sums = sums + got[k * quarter:(k + 1) * quarter, :]
    sizes = sums[:, d:]
    out[:, 0:d] = (sums[:, 0:d] / sizes[:, 0:1]).astype(BF16)
    out[:, d:] = code_sizes(sizes)


def join_kernel(logs, p0, p1, p2, p3, means, plog):
    quarter, width = p0.shape
    d = width - PAD
    sizes = []
    for k, ref in enumerate((p0, p1, p2, p3)):
        block = ref[...]
        means[k * quarter:(k + 1) * quarter, :] = block[:, 0:d]
        sizes.append(jnp.broadcast_to(read_sizes(block, d), (quarter, 128)))
    plog[...] = jnp.zeros(plog.shape, F32)
    plog[0:2, :] = jnp.log2(to_lanes(jnp.concatenate(sizes, axis=0))) - logs[1:2, :]


def fetch(pieces, buf, sems):
    size = pieces[0].shape[0]
    for b, p in enumerate(pieces):
        pltpu.make_async_copy(p, buf.at[pl.ds(b * size, size)], sems.at[b]).start()

    def wait(b):
        into = buf.at[pl.ds(pl.multiple_of(b * size, size), size)]
        pltpu.make_async_copy(into, into, sems.at[b]).wait()

    return wait


def gathered(own, xs, ys, swapped, rows_buf, cols_buf, row_sems, col_sems):
    wait_cols = fetch([own, *xs], cols_buf, col_sems)
    wait_rows = fetch([own, *ys, *swapped], rows_buf, row_sems)
    for b in range(X):
        wait_cols(b)
    return wait_rows


def saved(rows_buf, cols_buf, rows_out, cols_out, sems):
    copies = [
        pltpu.make_async_copy(rows_buf, rows_out, sems.at[0]),
        pltpu.make_async_copy(cols_buf, cols_out, sems.at[1]),
    ]
    for copy in copies:
        copy.start()

    def wait():
        for copy in copies:
            copy.wait()

    return wait


def dot_t(a, b):
    return lax.dot_general(a, b, (((1,), (1,)), ((), ())), preferred_element_type=F32) * SC


def fill_tile(tile, own, rows_buf, cols_buf, wait_rows, peak, acc, live):
    rows, cols = tile.shape
    step, wide = 2 * own, 512
    peak[...] = jnp.zeros(peak.shape, F32)
    if acc is not None:
        acc[...] = jnp.zeros(acc.shape, F32)

    def body(i, _):
        wait_rows(2 * i)
        wait_rows(2 * i + 1)
        at = pl.ds(pl.multiple_of(i * step, step), step)
        for j in range(cols // wide):
            across = pl.ds(j * wide, wide)
            s = dot_t(rows_buf[at, :], cols_buf[across, :])
            if j * wide < own:
                col = iota((step, wide), 1) + j * wide
                s = jnp.where((iota((step, wide), 0) + i * step == col) & (col < own), NEG, s)
            s = jnp.exp2(s)
            tile[at, across] = s
            parts = s.reshape(step // 8, 8, wide)
            most = jnp.max(parts, axis=0)
            for k in range(wide // 128):
                peak[...] = jnp.maximum(peak[...], most[:, k * 128:(k + 1) * 128])
            if acc is not None:
                s = s * jnp.concatenate([live[at, :]] * (wide // 128), axis=1)
                acc[:, across] += jnp.sum(s.reshape(step // 8, 8, wide), axis=0)
        return 0

    lax.fori_loop(0, rows // step, body, 0)


def coarse_tile_kernel(own, x1, x2, x3, y1, y2, y3, s0, s1, s2, s3, plog, tile, payload, peak, rows_out, cols_out,
                       rows_buf, cols_buf, row_sems, col_sems, out_sems, wide, a_buf, b_buf, sem):
    n = own.shape[0]
    wait_rows = gathered(own, (x1, x2, x3), (y1, y2, y3), (s0, s1, s2, s3), rows_buf, cols_buf, row_sems, col_sems)
    fill_tile(tile, n, rows_buf, cols_buf, wait_rows, peak, None, None)
    wait = saved(rows_buf, cols_buf, rows_out, cols_out, out_sems)
    rows, cols = tile.shape
    payload[...] = jnp.zeros(payload.shape, F32)
    backup = (rows_out, cols_out, n, a_buf, b_buf, sem)
    wait()
    reduce_columns(tile, jnp.zeros((cols // 128, 128), F32), peak, payload, wide, backup)
    payload[rows // 128:rows // 128 + 2, :] = plog[0:2, :]


def fine_tile_kernel(info, live_rows, own, x1, x2, x3, y1, y2, y3, s0, s1, s2, s3, tile, part, peak, rows_out,
                     cols_out, rows_buf, cols_buf, row_sems, col_sems, out_sems, tall, acc, a_buf, b_buf, sem):
    n = own.shape[0]
    wait_rows = gathered(own, (x1, x2, x3), (y1, y2, y3), (s0, s1, s2, s3), rows_buf, cols_buf, row_sems, col_sems)
    for b, count in enumerate(row_counts(info, info_place(info))):
        tall[b * n:(b + 1) * n, :] = jnp.where(iota((n, 128), 0) < count, 1.0, 0.0)
    fill_tile(tile, n, rows_buf, cols_buf, wait_rows, peak, acc, tall)
    wait = saved(rows_buf, cols_buf, rows_out, cols_out, out_sems)
    rows, cols = tile.shape
    total = jnp.sum(acc[...], axis=0, keepdims=True)
    for k in range(cols // 128):
        part[k:k + 1, :] = total[:, k * 128:(k + 1) * 128]
    wait()
    h = jnp.where(live_rows[...] > 0.0, 0.0, NEG)
    store_lse(
        part[...], 0.0, jnp.max(peak[...]), part,
        lambda: safe_rows((rows_out, cols_out, n, a_buf, b_buf, sem), h, part, tall),
    )


def fold_y_kernel(plan, *refs):
    parts, out = refs[0:Y], refs[Y]
    out[...] = jnp.zeros(out.shape, F32)
    for first, per in plan["lse"]:
        n = 2 * Y * per
        out[first:first + n, :] = fold_y(parts, first, per)
    if plan["plog"] is not None:
        first, into = plan["plog"]
        out[into:into + 2 * Y, :] = jnp.concatenate(
            [p[first:first + 2, :] for p in parts], axis=0
        )


def coarse2_kernel(mine, other, part, plog, seat, tile, peak, rows_hbm, cols_hbm, payload, plog_rows, tall, *bufs):
    plog_rows[0:8, :] = mine[16:24, :]
    plog_rows[8:16, :] = other[16:24, :]
    h = plog_rows[...] + SC - fold_core(mine, other, 0, 2)
    payload[...] = jnp.zeros(payload.shape, F32)
    reduce_rows(tile, h, peak, payload, tall, (rows_hbm, cols_hbm, PROTO_BLOCK, *bufs))
    payload[8:20, :] = part[...]
    payload[20:22, :] = plog[0:2, :]
    payload[22:25, :] = seat[...]


def fine_h(lse, logs, live, boost=0.0):
    return jnp.where(live[...] > 0.0, SC - logs[0:1, :] - lse + boost, NEG)


def step3_kernel(logs, live_cols, p0, p1, p2, p3, ktile, kpeak, krows, kcols, tile, peak, rows_hbm, cols_hbm,
                 payload, plog_cols, seats, wide, kwide, *bufs):
    parts = (p0, p1, p2, p3)
    plog_cols[...] = gather_columns(parts, 20, 2)
    seats[...] = gather_columns(parts, 22, 3)
    payload[...] = jnp.zeros(payload.shape, F32)
    h = fine_h(from_columns(parts, 8, 3), logs, live_cols)
    backup = (rows_hbm, cols_hbm, tile.shape[1] // X, *bufs)
    reduce_columns(tile, h, peak, payload.at[16:40, :], wide, backup)
    h = plog_cols[...] + SC - from_columns(parts, 0, 2)
    reduce_columns(ktile, h, kpeak, payload.at[0:16, :], kwide, (krows, kcols, PROTO_BLOCK, *bufs))


def step4_kernel(logs, live_rows, mine, other, plog_rows, ktile, kpeak, krows, kcols, tile, peak, rows_hbm, cols_hbm,
                 payload, tall, ktall, *bufs):
    payload[...] = jnp.zeros(payload.shape, F32)
    h = plog_rows[...] + SC - fold_core(mine, other, 0, 2)
    reduce_rows(ktile, h, kpeak, payload.at[0:8, :], ktall, (krows, kcols, PROTO_BLOCK, *bufs))
    h = fine_h(fold_core(mine, other, 16, 3), logs, live_rows)
    backup = (rows_hbm, cols_hbm, tile.shape[1] // X, *bufs)
    reduce_rows(tile, h, peak, payload.at[8:20, :], tall, backup)


def step5_kernel(logs, live_cols, p0, p1, p2, p3, plog_cols, seats, tile, peak, rows_hbm, cols_hbm,
                 payload, coarse, tall, wide, *bufs):
    parts = (p0, p1, p2, p3)
    v = plog_cols[...] + SC - from_columns(parts, 0, 2)
    coarse[...] = v[0:1, :] * (1.0 / SC)
    to_rows(v, tall)
    local = seats[...].astype(jnp.int32)
    boost = []
    for k in range(X * 3):
        vals = tall[(k // 3) * PROTO_BLOCK:(k // 3 + 1) * PROTO_BLOCK, :]
        pick = iota((PROTO_BLOCK, 128), 0) == local[k:k + 1, :]
        boost.append(jnp.sum(jnp.where(pick, vals, 0.0), axis=0, keepdims=True))
    h = fine_h(from_columns(parts, 8, 3), logs, live_cols, jnp.concatenate(boost, axis=0))
    payload[...] = jnp.zeros(payload.shape, F32)
    reduce_columns(tile, h, peak, payload, wide, (rows_hbm, cols_hbm, tile.shape[1] // X, *bufs))


def potential(h):
    return jnp.where(h == NEG, 0.0, h)[0:3, :] * (1.0 / SC)


def step6_kernel(logs, live_rows, mine, other, tile, peak, rows_hbm, cols_hbm, payload, out, tall, *bufs):
    h = fine_h(fold_core(mine, other, 0, 3), logs, live_rows)
    out[...] = potential(h)
    payload[...] = jnp.zeros(payload.shape, F32)
    backup = (rows_hbm, cols_hbm, tile.shape[1] // X, *bufs)
    reduce_rows(tile, h, peak, payload, tall, backup)


def last_kernel(logs, live_cols, p0, p1, p2, p3, out):
    out[...] = potential(fine_h(from_columns((p0, p1, p2, p3), 0, 3), logs, live_cols))


def swap(v, axis, bit):
    n = {"z": Z, "c": 2}[axis]
    return lax.ppermute(v, axis, [(i, i ^ bit) for i in range(n)])


def ahead(v, axis, k):
    n = {"z": Z}[axis]
    return lax.ppermute(v, axis, [(i, (i + k) % n) for i in range(n)])


def turn(v, axis, k):
    n = {"x": X, "y": Y}[axis]
    return lax.ppermute(
        v, (axis, "c"), [(i * 2 + c, (i + (k if c == 0 else n - k)) % n * 2 + c) for i in range(n) for c in range(2)]
    )


def spread_over(v, axis):
    return [v] + [turn(v, axis, k) for k in (1, 2, 3)]


def vmem(v):
    return pltpu.with_memory_space_constraint(v, pltpu.VMEM)


def held(tile, peak, rows, cols):
    return [vmem(tile), peak, *[pltpu.with_memory_space_constraint(v, HBM) for v in (rows, cols)]]


def local(embeddings, members, counts):
    rows, d = embeddings.shape
    here = jnp.stack([lax.axis_index(a) for a in ("z", "x", "y", "c")]).astype(jnp.int32)
    info = jnp.concatenate([counts, jnp.pad(here[None], ((0, 0), (0, counts.shape[1] - 4)))], axis=0)
    per = rows // 128
    n_rows, n_cols = rows * Y * 2, rows * X
    k_rows, k_cols = PROTO_BLOCK * Y * 2, PROTO_BLOCK * X
    quarter = PROTO_BLOCK // Z
    width = d + PAD

    def first(own):
        return turn(own, "x", 1), turn(own, "x", 3), turn(own, "y", 1), turn(own, "y", 3)

    x1, x3, y1, y3 = first(embeddings)
    sums, live_rows, live_cols, seat, logs = call(
        pool_kernel,
        [
            sds((PROTO_BLOCK, width)), sds((n_rows // 128, 128)), sds((n_cols // 128, 128)),
            sds((per, 128)), sds((8, 128)),
        ],
        [SMEM, VMEM, VMEM],
        name="pool",
    )(info, embeddings, members.reshape(per, 128))
    got = lax.all_to_all(sums, "z", 0, 0, tiled=True)
    x1, x3, y1, y3, got = lax.optimization_barrier((x1, x3, y1, y3, got))
    x2, y2 = turn(x1, "x", 1), turn(y1, "y", 1)
    s0, s1, s3 = swap(embeddings, "c", 1), swap(y1, "c", 1), swap(y3, "c", 1)
    part = call(means_kernel, sds((quarter, width), BF16), [VMEM], name="means")(got)
    means, plog = call(
        join_kernel, [sds((PROTO_BLOCK, d), BF16), sds((8, 128))], [VMEM] * 5, name="join"
    )(logs, part, *[ahead(part, "z", k) for k in (1, 2, 3)])
    x2, y2, s0, s1, s3, means = lax.optimization_barrier((x2, y2, s0, s1, s3, means))
    s2 = swap(y2, "c", 1)
    vectors = [embeddings, x1, x2, x3, y1, y2, y3, s0, s1, s2, s3]

    bufs = [pltpu.VMEM((STEP, d), BF16), pltpu.VMEM((STEP, d), BF16), pltpu.SemaphoreType.DMA]

    def tile_call(body, n, m, part_rows, specs, extra, name):
        out = [pltpu.VMEM((n, m), F32), sds((part_rows, 128)), sds((8, 128)), HBM((n, d), BF16), HBM((m, d), BF16)]
        return call(
            body,
            out,
            specs,
            scratch=[
                pltpu.VMEM((n, d), BF16),
                pltpu.VMEM((m, d), BF16),
                pltpu.SemaphoreType.DMA((2 * Y,)),
                pltpu.SemaphoreType.DMA((X,)),
                pltpu.SemaphoreType.DMA((2,)),
                *extra,
                *bufs,
            ],
            out_specs=[VMEM, VMEM, VMEM, IN_HBM, IN_HBM],
            limit=14,
            name=name,
            flops=2 * n * m * d,
        )

    tall = pltpu.VMEM((n_rows, 128), F32)
    wide = pltpu.VMEM((8, n_cols), F32)
    mx1, mx3, my1, my3 = first(means)
    t0 = swap(means, "c", 1)
    tile, upart, *back = tile_call(
        fine_tile_kernel, n_rows, n_cols, n_cols // 128, [SMEM, VMEM] + [ANY] * 11, [tall, wide], "fine_tile"
    )(info, live_rows, *vectors)
    upart, mx1, mx3, my1, my3, t0 = lax.optimization_barrier((upart, mx1, mx3, my1, my3, t0))
    mx2, my2 = turn(mx1, "x", 1), turn(my1, "y", 1)
    t1, t3, t2 = swap(my1, "c", 1), swap(my3, "c", 1), swap(my2, "c", 1)
    back = held(tile, *back)

    ktile, part, *kback = tile_call(
        coarse_tile_kernel, k_rows, k_cols, 24, [ANY] * 11 + [VMEM], [pltpu.VMEM((8, k_cols), F32)], "coarse_tile"
    )(means, mx1, mx2, mx3, my1, my2, my3, t0, t1, t2, t3, plog)
    kback = held(ktile, *kback)
    kspecs = [VMEM, VMEM, IN_HBM, IN_HBM]
    mine = call(
        lambda *r: fold_y_kernel({"lse": [(0, 2)], "plog": (16, 16)}, *r),
        sds((24, 128)),
        [VMEM] * 4,
        name="fold_y1",
    )(*spread_over(part, "y"))
    other = swap(mine, "c", 1)

    part, plog_rows = call(
        coarse2_kernel,
        [sds((32, 128)), sds((16, 128))],
        [VMEM] * 5 + kspecs,
        scratch=[pltpu.VMEM((k_rows, 128), F32), *bufs],
        name="coarse2",
    )(mine, other, upart, plog, seat, *kback)

    part, plog_cols, seats = call(
        step3_kernel,
        [sds((40, 128)), sds((8, 128)), sds((12, 128))],
        [VMEM, VMEM] + [VMEM] * 4 + kspecs * 2,
        scratch=[wide, pltpu.VMEM((8, k_cols), F32), *bufs],
        name="step3",
    )(logs, live_cols, *spread_over(part, "x"), *kback, *back)
    mine = call(
        lambda *r: fold_y_kernel({"lse": [(0, 2), (16, 3)], "plog": None}, *r),
        sds((40, 128)),
        [VMEM] * 4,
        name="fold_y2",
    )(*spread_over(part, "y"))
    other = swap(mine, "c", 1)

    part = call(
        step4_kernel,
        sds((24, 128)),
        [VMEM, VMEM] + [VMEM] * 3 + kspecs * 2,
        scratch=[tall, pltpu.VMEM((k_rows, 128), F32), *bufs],
        name="step4",
    )(logs, live_rows, mine, other, plog_rows, *kback, *back)

    part, coarse = call(
        step5_kernel,
        [sds((24, 128)), sds((1, 128))],
        [VMEM, VMEM] + [VMEM] * 6 + kspecs,
        scratch=[pltpu.VMEM((k_cols, 128), F32), wide, *bufs],
        name="step5",
    )(logs, live_cols, *spread_over(part, "x"), plog_cols, seats, *back)
    mine = call(
        lambda *r: fold_y_kernel({"lse": [(0, 3)], "plog": None}, *r),
        sds((24, 128)),
        [VMEM] * 4,
        name="fold_y3",
    )(*spread_over(part, "y"))
    other = swap(mine, "c", 1)

    part, col = call(
        step6_kernel,
        [sds((16, 128)), sds((3, 128))],
        [VMEM, VMEM] + [VMEM] * 2 + kspecs,
        scratch=[tall, *bufs],
        name="step6",
    )(logs, live_rows, mine, other, *back)
    row = call(last_kernel, sds((3, 128)), [VMEM, VMEM] + [VMEM] * 4, name="last")(
        logs, live_cols, *spread_over(part, "x")
    )
    return row.reshape(rows), col.reshape(rows), coarse[0, :quarter]


def solution(mesh):
    split = Mesh(mesh.devices.reshape(Z, X, Y, 2), ("z", "x", "y", "c"))
    every = P(("z", "x", "y", "c"))
    return jax.shard_map(
        local,
        mesh=split,
        in_specs=(P(("z", "x", "y", "c"), None), every, P()),
        out_specs=(every, every, every),
        check_vma=False,
    )
```

```python
import math

import jax
import jax.numpy as jnp
from jax import lax
from jax.experimental import pallas as pl
from jax.experimental.pallas import tpu as pltpu
from jax.sharding import Mesh, PartitionSpec as P


PROTO_BLOCK = 256
EPS = 0.01
SC = math.log2(math.e) / EPS
NEG = -1e30
LOW, HIGH, PEAK = 2.0 ** -48, 2.0 ** 120, 2.0 ** 40
STEP = 256
F32 = jnp.float32
BF16 = jnp.bfloat16
MIB = 2 ** 20
X, Y, Z = 4, 4, 4
PAD = 128

VMEM = pl.BlockSpec(memory_space=pltpu.VMEM)
SMEM = pl.BlockSpec(memory_space=pltpu.SMEM)
ANY = pl.BlockSpec(memory_space=pl.ANY)


HBM = pltpu.MemorySpace.HBM
IN_HBM = pl.BlockSpec(memory_space=HBM)


def call(body, out_shape, in_specs, scratch=(), out_specs=None, limit=6, name=None, flops=0, nbytes=0):
    return pl.pallas_call(
        body,
        out_shape=out_shape,
        in_specs=in_specs,
        out_specs=out_specs or jax.tree.map(lambda _: VMEM, out_shape),
        scratch_shapes=list(scratch),
        compiler_params=pltpu.CompilerParams(vmem_limit_bytes=limit * MIB),
        cost_estimate=pl.CostEstimate(flops=flops, bytes_accessed=nbytes, transcendentals=0),
        name=name,
    )


def sds(shape, dtype=F32):
    return jax.ShapeDtypeStruct(shape, dtype)


def iota(shape, dim):
    return lax.broadcasted_iota(jnp.int32, shape, dim)


def to_lanes(col):
    n = col.shape[0]
    eye = iota((128, 128), 0) == iota((128, 128), 1)
    return jnp.concatenate(
        [
            jnp.sum(jnp.where(eye, col[k * 128:(k + 1) * 128], 0.0), axis=0, keepdims=True)
            for k in range(n // 128)
        ],
        axis=0,
    )


def to_rows(vals, out_ref):
    for k in range(vals.shape[0]):
        out_ref[k * 128:(k + 1) * 128, :] = jnp.transpose(
            jnp.broadcast_to(vals[k:k + 1, :], (128, 128))
        )


def lse2(parts):
    top = parts[0]
    for p in parts[1:]:
        top = jnp.maximum(top, p)
    total = jnp.exp2(parts[0] - top)
    for p in parts[1:]:
        total = total + jnp.exp2(p - top)
    return top + jnp.log2(total)


def in_range(total, peak):
    outside = jnp.sum(jnp.where((total > LOW) & (total < HIGH), 0.0, 1.0))
    return (outside == 0.0) & (peak <= PEAK)


def spread(vals, wide_ref):
    for k in range(vals.shape[0]):
        wide_ref[:, k * 128:(k + 1) * 128] = jnp.broadcast_to(vals[k:k + 1, :], (8, 128))


def store_lse(total, shift, peak, out_ref, safe):
    n = total.shape[0]
    good = in_range(total, peak)

    @pl.when(good)
    def _():
        out_ref[0:n, :] = jnp.log2(total) + shift

    @pl.when(jnp.logical_not(good))
    def _():
        safe()


def reduce_columns(tile, h, guard, out_ref, wide_ref, backup):
    rows, cols = tile.shape
    shift = jnp.max(h)
    spread(jnp.exp2(h - shift), wide_ref)
    lane, sub = iota((8, 128), 1), iota((8, 128), 0)

    def body(r, _):
        acc = jnp.zeros((8, 128), F32)
        for g in range(16):
            s = tile[pl.ds(pl.multiple_of(r * 128 + g * 8, 8), 8), :] * wide_ref[...]
            part = jnp.sum(s, axis=1, keepdims=True)
            acc = acc + jnp.where(lane == sub + 8 * g, part, 0.0)
        out_ref[pl.ds(r, 1), :] = jnp.sum(acc, axis=0, keepdims=True)
        return 0

    lax.fori_loop(0, rows // 128, body, 0, unroll=4)
    store_lse(
        out_ref[0:rows // 128, :], shift, jnp.max(guard[...]), out_ref,
        lambda: safe_columns(backup, h, out_ref, wide_ref),
    )


def reduce_rows(tile, h, guard, out_ref, tall_ref, backup):
    rows, cols = tile.shape
    shift = jnp.max(h)
    to_rows(jnp.exp2(h - shift), tall_ref)
    width, chunk = 512, 64
    groups = width // 128
    for strip in range(cols // width):
        at = pl.ds(strip * width, width)

        def body(c, acc):
            part = pl.ds(pl.multiple_of(c * chunk, chunk), chunk)
            s = tile[part, at] * jnp.concatenate([tall_ref[part, :]] * groups, axis=1)
            return acc + jnp.sum(s.reshape(chunk // 8, 8, width), axis=0)

        acc = lax.fori_loop(0, rows // chunk, body, jnp.zeros((8, width), F32), unroll=2)
        acc = jnp.sum(acc, axis=0, keepdims=True)
        for k in range(groups):
            row = strip * groups + k
            out_ref[row:row + 1, :] = acc[:, k * 128:(k + 1) * 128]
    store_lse(
        out_ref[0:cols // 128, :], shift, jnp.max(guard[...]), out_ref,
        lambda: safe_rows(backup, h, out_ref, tall_ref),
    )


def block_scores(backup, ci, cj):
    rows_hbm, cols_hbm, own, a_buf, b_buf, sem = backup
    for src, at, buf in ((rows_hbm, ci, a_buf), (cols_hbm, cj, b_buf)):
        copy = pltpu.make_async_copy(src.at[pl.ds(pl.multiple_of(at * STEP, STEP), STEP)], buf, sem)
        copy.start()
        copy.wait()
    s = dot_t(a_buf[...], b_buf[...])
    i, j = iota((STEP, STEP), 0) + ci * STEP, iota((STEP, STEP), 1) + cj * STEP
    return jnp.where((i == j) & (j < own), NEG, s)


def safe_columns(backup, h, out_ref, wide_ref):
    n, m = backup[0].shape[0] // STEP, backup[1].shape[0] // STEP
    spread(h, wide_ref)

    def by_rows(ci, _):
        def by_cols(cj, carry):
            top, total = carry
            s = block_scores(backup, ci, cj)
            s = s + wide_ref[0:1, pl.ds(pl.multiple_of(cj * STEP, STEP), STEP)]
            now = jnp.maximum(top, jnp.max(s, axis=1, keepdims=True))
            return now, total * jnp.exp2(top - now) + jnp.sum(jnp.exp2(s - now), axis=1, keepdims=True)

        top, total = lax.fori_loop(
            0, m, by_cols, (jnp.full((STEP, 1), NEG, F32), jnp.zeros((STEP, 1), F32))
        )
        lanes = to_lanes(jnp.broadcast_to(top + jnp.log2(total), (STEP, 128)))
        for k in range(STEP // 128):
            out_ref[pl.ds(ci * (STEP // 128) + k, 1), :] = lanes[k:k + 1, :]
        return 0

    lax.fori_loop(0, n, by_rows, 0)


def safe_rows(backup, h, out_ref, tall_ref):
    n, m = backup[0].shape[0] // STEP, backup[1].shape[0] // STEP
    to_rows(h, tall_ref)

    def by_cols(cj, _):
        def by_rows(ci, carry):
            top, total = carry
            add = tall_ref[pl.ds(pl.multiple_of(ci * STEP, STEP), STEP), :]
            s = block_scores(backup, ci, cj) + jnp.concatenate([add] * (STEP // 128), axis=1)
            now = jnp.maximum(top, jnp.max(s, axis=0, keepdims=True))
            return now, total * jnp.exp2(top - now) + jnp.sum(jnp.exp2(s - now), axis=0, keepdims=True)

        top, total = lax.fori_loop(
            0, n, by_rows, (jnp.full((1, STEP), NEG, F32), jnp.zeros((1, STEP), F32))
        )
        lse = top + jnp.log2(total)
        for k in range(STEP // 128):
            out_ref[pl.ds(cj * (STEP // 128) + k, 1), :] = lse[:, k * 128:(k + 1) * 128]
        return 0

    lax.fori_loop(0, m, by_cols, 0)


def info_place(info):
    return info[Z, 0], info[Z, 1], info[Z, 2], info[Z, 3]


def count_at(counts, z, x, y, c):
    return counts[z, (x * Y + y) * 2 + c]


def behind(at, c, k, n):
    return lax.rem(at + jnp.where(c == 0, n - k, k), n)


def row_counts(counts, idx):
    z, x, y, c = idx
    return [
        count_at(counts, z, x, behind(y, (c + dc) % 2, k, Y), (c + dc) % 2) for dc in range(2) for k in range(Y)
    ]


def col_counts(counts, idx):
    z, x, y, c = idx
    return [count_at(counts, z, behind(x, c, k, X), y, c) for k in range(X)]


def live_mask(block_counts, per):
    at = iota((per, 128), 0) * 128 + iota((per, 128), 1)
    return jnp.concatenate([jnp.where(at < n, 1.0, 0.0) for n in block_counts], axis=0)


def log2_of(n):
    return jnp.log2(jnp.full((1, 128), n, jnp.int32).astype(F32))


def from_columns(parts, first, per):
    blocks = []
    for j in range(X):
        rows = [first + (j - k) % X * per for k in range(X)]
        blocks.append(lse2([p[r:r + per, :] for p, r in zip(parts, rows)]))
    return jnp.concatenate(blocks, axis=0)


def gather_columns(parts, first, per):
    return jnp.concatenate([p[first:first + per, :] for p in parts], axis=0)


def fold_y(parts, first, per):
    blocks = []
    for dc in range(2):
        for j in range(Y):
            rows = [first + (dc * Y + (j - k if dc == 0 else j + k) % Y) * per for k in range(Y)]
            blocks.append(lse2([p[r:r + per, :] for p, r in zip(parts, rows)]))
    return jnp.concatenate(blocks, axis=0)


def fold_core(mine, other, first, per):
    half = Y * per
    return jnp.concatenate(
        [
            lse2([mine[first:first + half, :], other[first + half:first + 2 * half, :]]),
            lse2([mine[first + half:first + 2 * half, :], other[first:first + half, :]]),
        ],
        axis=0,
    )


def pool_kernel(info, emb, members, keep, send, live_rows, live_cols, seat, logs):
    idx = info_place(info)
    z, x, y, c = idx
    quarter = PROTO_BLOCK // Z
    per = members.shape[0]
    ids = members[...]
    which = lax.shift_right_logical(ids, 11)
    within = jnp.bitwise_and(ids, quarter - 1)
    seat[...] = (lax.rem(z - which + Z, Z) * quarter + within).astype(F32)
    turn = jnp.bitwise_xor(which, z)
    slot = jnp.where(turn == 0, 0, jnp.where(turn == 3, 1, turn + 1)) * quarter + within
    local = jnp.concatenate([slot[k:k + 1, :] for k in range(per)], axis=1)
    rows, d = emb.shape
    live = iota((1, rows), 1) < count_at(info, z, x, y, c)
    hot = ((iota((PROTO_BLOCK, rows), 0) == local) & live).astype(BF16)
    sums = jnp.dot(hot, emb[...], preferred_element_type=F32)
    sizes = jnp.dot(hot, jnp.ones((rows, PAD), BF16), preferred_element_type=F32)
    half = 2 * quarter
    keep[:, 0:d] = sums[0:half]
    keep[:, d:] = sizes[0:half]
    send[:, 0:d] = sums[half:]
    send[:, d:] = sizes[half:]
    live_rows[...] = live_mask(row_counts(info, idx), per)
    live_cols[...] = live_mask(col_counts(info, idx), per)
    mine, total = 0, 0
    for g in range(Z):
        n = info[g, 0]
        for s in range(1, X * Y * 2):
            n = n + info[g, s]
        mine = mine + jnp.where(g == z, n, 0)
        total = total + n
    logs[...] = jnp.concatenate([log2_of(mine), log2_of(total), jnp.zeros((6, 128), F32)], axis=0)


def code_sizes(sizes):
    high = jnp.floor(sizes * (1.0 / 256.0))
    low = sizes - 256.0 * high
    return jnp.where(iota(sizes.shape, 1) < 64, high, low).astype(BF16)


def read_sizes(block, d):
    coded = block[:, d:].astype(F32)
    return coded[:, 0:1] * 256.0 + coded[:, 64:65]


def pool2_kernel(mine, got, keep, send):
    quarter = mine.shape[0] // 2
    keep[...] = mine[0:quarter, :] + got[0:quarter, :]
    send[...] = mine[quarter:, :] + got[quarter:, :]


def means_kernel(mine, got, out):
    d = mine.shape[1] - PAD
    sums = mine[...] + got[...]
    sizes = sums[:, d:]
    out[:, 0:d] = (sums[:, 0:d] / sizes[:, 0:1]).astype(BF16)
    out[:, d:] = code_sizes(sizes)


def join_kernel(logs, p0, p1, p2, p3, means, plog):
    quarter, width = p0.shape
    d = width - PAD
    sizes = []
    for k, ref in enumerate((p0, p1, p2, p3)):
        block = ref[...]
        means[k * quarter:(k + 1) * quarter, :] = block[:, 0:d]
        sizes.append(jnp.broadcast_to(read_sizes(block, d), (quarter, 128)))
    plog[...] = jnp.zeros(plog.shape, F32)
    plog[0:2, :] = jnp.log2(to_lanes(jnp.concatenate(sizes, axis=0))) - logs[1:2, :]


def fetch(pieces, buf, sems):
    size = pieces[0].shape[0]
    for b, p in enumerate(pieces):
        pltpu.make_async_copy(p, buf.at[pl.ds(b * size, size)], sems.at[b]).start()

    def wait(b):
        into = buf.at[pl.ds(pl.multiple_of(b * size, size), size)]
        pltpu.make_async_copy(into, into, sems.at[b]).wait()

    return wait


def gathered(own, xs, ys, swapped, rows_buf, cols_buf, row_sems, col_sems):
    wait_cols = fetch([own, *xs], cols_buf, col_sems)
    wait_rows = fetch([own, *ys, *swapped], rows_buf, row_sems)
    for b in range(X):
        wait_cols(b)
    return wait_rows


def dot_t(a, b):
    return lax.dot_general(a, b, (((1,), (1,)), ((), ())), preferred_element_type=F32) * SC


def fill_tile(tile, own, rows_buf, cols_buf, wait_rows, rows_out, cols_out, out_sems, peak, acc, live):
    rows, cols = tile.shape
    step, wide = 2 * own, 512
    save_cols = pltpu.make_async_copy(cols_buf, cols_out, out_sems.at[1])
    save_cols.start()
    peak[...] = jnp.zeros(peak.shape, F32)
    if acc is not None:
        acc[...] = jnp.zeros(acc.shape, F32)

    def body(i, _):
        wait_rows(2 * i)
        wait_rows(2 * i + 1)
        at = pl.ds(pl.multiple_of(i * step, step), step)
        pltpu.make_async_copy(rows_buf.at[at], rows_out.at[at], out_sems.at[0]).start()
        for j in range(cols // wide):
            across = pl.ds(j * wide, wide)
            s = dot_t(rows_buf[at, :], cols_buf[across, :])
            if j * wide < own:
                col = iota((step, wide), 1) + j * wide
                s = jnp.where((iota((step, wide), 0) + i * step == col) & (col < own), NEG, s)
            s = jnp.exp2(s)
            tile[at, across] = s
            parts = s.reshape(step // 8, 8, wide)
            most = jnp.max(parts, axis=0)
            for k in range(wide // 128):
                peak[...] = jnp.maximum(peak[...], most[:, k * 128:(k + 1) * 128])
            if acc is not None:
                s = s * jnp.concatenate([live[at, :]] * (wide // 128), axis=1)
                acc[:, across] += jnp.sum(s.reshape(step // 8, 8, wide), axis=0)
        return 0

    lax.fori_loop(0, rows // step, body, 0)
    save_cols.wait()
    pltpu.make_async_copy(rows_buf, rows_out, out_sems.at[0]).wait()


def coarse_tile_kernel(own, x1, x2, x3, y1, y2, y3, s0, s1, s2, s3, plog, tile, payload, peak, rows_out, cols_out,
                       rows_buf, cols_buf, row_sems, col_sems, out_sems, wide, a_buf, b_buf, sem):
    n = own.shape[0]
    wait_rows = gathered(own, (x1, x2, x3), (y1, y2, y3), (s0, s1, s2, s3), rows_buf, cols_buf, row_sems, col_sems)
    fill_tile(tile, n, rows_buf, cols_buf, wait_rows, rows_out, cols_out, out_sems, peak, None, None)
    rows, cols = tile.shape
    payload[...] = jnp.zeros(payload.shape, F32)
    backup = (rows_out, cols_out, n, a_buf, b_buf, sem)
    reduce_columns(tile, jnp.zeros((cols // 128, 128), F32), peak, payload, wide, backup)
    payload[rows // 128:rows // 128 + 2, :] = plog[0:2, :]


def fine_tile_kernel(info, live_rows, own, x1, x2, x3, y1, y2, y3, s0, s1, s2, s3, tile, part, peak, rows_out,
                     cols_out, rows_buf, cols_buf, row_sems, col_sems, out_sems, tall, acc, a_buf, b_buf, sem):
    n = own.shape[0]
    wait_rows = gathered(own, (x1, x2, x3), (y1, y2, y3), (s0, s1, s2, s3), rows_buf, cols_buf, row_sems, col_sems)
    for b, count in enumerate(row_counts(info, info_place(info))):
        tall[b * n:(b + 1) * n, :] = jnp.where(iota((n, 128), 0) < count, 1.0, 0.0)
    fill_tile(tile, n, rows_buf, cols_buf, wait_rows, rows_out, cols_out, out_sems, peak, acc, tall)
    rows, cols = tile.shape
    total = jnp.sum(acc[...], axis=0, keepdims=True)
    for k in range(cols // 128):
        part[k:k + 1, :] = total[:, k * 128:(k + 1) * 128]
    h = jnp.where(live_rows[...] > 0.0, 0.0, NEG)
    store_lse(
        part[...], 0.0, jnp.max(peak[...]), part,
        lambda: safe_rows((rows_out, cols_out, n, a_buf, b_buf, sem), h, part, tall),
    )


def fold_y_kernel(plan, *refs):
    parts, out = refs[0:Y], refs[Y]
    out[...] = jnp.zeros(out.shape, F32)
    for first, per in plan["lse"]:
        n = 2 * Y * per
        out[first:first + n, :] = fold_y(parts, first, per)
    if plan["plog"] is not None:
        first, into = plan["plog"]
        out[into:into + 2 * Y, :] = jnp.concatenate(
            [p[first:first + 2, :] for p in parts], axis=0
        )


def coarse2_kernel(mine, other, part, plog, seat, tile, peak, rows_hbm, cols_hbm, payload, plog_rows, tall, *bufs):
    plog_rows[0:8, :] = mine[16:24, :]
    plog_rows[8:16, :] = other[16:24, :]
    h = plog_rows[...] + SC - fold_core(mine, other, 0, 2)
    payload[...] = jnp.zeros(payload.shape, F32)
    reduce_rows(tile, h, peak, payload, tall, (rows_hbm, cols_hbm, PROTO_BLOCK, *bufs))
    payload[8:20, :] = part[...]
    payload[20:22, :] = plog[0:2, :]
    payload[22:25, :] = seat[...]


def fine_h(lse, logs, live, boost=0.0):
    return jnp.where(live[...] > 0.0, SC - logs[0:1, :] - lse + boost, NEG)


def step3_kernel(logs, live_cols, p0, p1, p2, p3, ktile, kpeak, krows, kcols, tile, peak, rows_hbm, cols_hbm,
                 payload, plog_cols, seats, wide, kwide, *bufs):
    parts = (p0, p1, p2, p3)
    plog_cols[...] = gather_columns(parts, 20, 2)
    seats[...] = gather_columns(parts, 22, 3)
    payload[...] = jnp.zeros(payload.shape, F32)
    h = fine_h(from_columns(parts, 8, 3), logs, live_cols)
    backup = (rows_hbm, cols_hbm, tile.shape[1] // X, *bufs)
    reduce_columns(tile, h, peak, payload.at[16:40, :], wide, backup)
    h = plog_cols[...] + SC - from_columns(parts, 0, 2)
    reduce_columns(ktile, h, kpeak, payload.at[0:16, :], kwide, (krows, kcols, PROTO_BLOCK, *bufs))


def step4_kernel(logs, live_rows, mine, other, plog_rows, ktile, kpeak, krows, kcols, tile, peak, rows_hbm, cols_hbm,
                 payload, tall, ktall, *bufs):
    payload[...] = jnp.zeros(payload.shape, F32)
    h = plog_rows[...] + SC - fold_core(mine, other, 0, 2)
    reduce_rows(ktile, h, kpeak, payload.at[0:8, :], ktall, (krows, kcols, PROTO_BLOCK, *bufs))
    h = fine_h(fold_core(mine, other, 16, 3), logs, live_rows)
    backup = (rows_hbm, cols_hbm, tile.shape[1] // X, *bufs)
    reduce_rows(tile, h, peak, payload.at[8:20, :], tall, backup)


def step5_kernel(logs, live_cols, p0, p1, p2, p3, plog_cols, seats, tile, peak, rows_hbm, cols_hbm,
                 payload, coarse, tall, wide, *bufs):
    parts = (p0, p1, p2, p3)
    v = plog_cols[...] + SC - from_columns(parts, 0, 2)
    coarse[...] = v[0:1, :] * (1.0 / SC)
    to_rows(v, tall)
    local = seats[...].astype(jnp.int32)
    boost = []
    for k in range(X * 3):
        vals = tall[(k // 3) * PROTO_BLOCK:(k // 3 + 1) * PROTO_BLOCK, :]
        pick = iota((PROTO_BLOCK, 128), 0) == local[k:k + 1, :]
        boost.append(jnp.sum(jnp.where(pick, vals, 0.0), axis=0, keepdims=True))
    h = fine_h(from_columns(parts, 8, 3), logs, live_cols, jnp.concatenate(boost, axis=0))
    payload[...] = jnp.zeros(payload.shape, F32)
    reduce_columns(tile, h, peak, payload, wide, (rows_hbm, cols_hbm, tile.shape[1] // X, *bufs))


def potential(h):
    return jnp.where(h == NEG, 0.0, h)[0:3, :] * (1.0 / SC)


def step6_kernel(logs, live_rows, mine, other, tile, peak, rows_hbm, cols_hbm, payload, out, tall, *bufs):
    h = fine_h(fold_core(mine, other, 0, 3), logs, live_rows)
    out[...] = potential(h)
    payload[...] = jnp.zeros(payload.shape, F32)
    backup = (rows_hbm, cols_hbm, tile.shape[1] // X, *bufs)
    reduce_rows(tile, h, peak, payload, tall, backup)


def last_kernel(logs, live_cols, p0, p1, p2, p3, out):
    out[...] = potential(fine_h(from_columns((p0, p1, p2, p3), 0, 3), logs, live_cols))


def swap(v, axis, bit):
    n = {"z": Z, "c": 2}[axis]
    return lax.ppermute(v, axis, [(i, i ^ bit) for i in range(n)])


def ahead(v, axis, k):
    n = {"z": Z}[axis]
    return lax.ppermute(v, axis, [(i, (i + k) % n) for i in range(n)])


def turn(v, axis, k):
    n = {"x": X, "y": Y}[axis]
    return lax.ppermute(
        v, (axis, "c"), [(i * 2 + c, (i + (k if c == 0 else n - k)) % n * 2 + c) for i in range(n) for c in range(2)]
    )


def spread_over(v, axis):
    return [v] + [turn(v, axis, k) for k in (1, 2, 3)]


def vmem(v):
    return pltpu.with_memory_space_constraint(v, pltpu.VMEM)


def held(tile, peak, rows, cols):
    return [vmem(tile), peak, *[pltpu.with_memory_space_constraint(v, HBM) for v in (rows, cols)]]


def local(embeddings, members, counts):
    rows, d = embeddings.shape
    here = jnp.stack([lax.axis_index(a) for a in ("z", "x", "y", "c")]).astype(jnp.int32)
    info = jnp.concatenate([counts, jnp.pad(here[None], ((0, 0), (0, counts.shape[1] - 4)))], axis=0)
    per = rows // 128
    n_rows, n_cols = rows * Y * 2, rows * X
    k_rows, k_cols = PROTO_BLOCK * Y * 2, PROTO_BLOCK * X
    quarter = PROTO_BLOCK // Z
    width = d + PAD

    def first(own):
        return turn(own, "x", 1), turn(own, "x", 3), turn(own, "y", 1), turn(own, "y", 3)

    x1, x3, y1, y3 = first(embeddings)
    keep, send, live_rows, live_cols, seat, logs = call(
        pool_kernel,
        [
            sds((2 * quarter, width)), sds((2 * quarter, width)), sds((n_rows // 128, 128)),
            sds((n_cols // 128, 128)), sds((per, 128)), sds((8, 128)),
        ],
        [SMEM, VMEM, VMEM],
        name="pool",
    )(info, embeddings, members.reshape(per, 128))
    got = swap(send, "z", 1)
    x1, x3, y1, y3, got = lax.optimization_barrier((x1, x3, y1, y3, got))
    x2, y2 = turn(x1, "x", 1), turn(y1, "y", 1)
    s0, s1, s3 = swap(embeddings, "c", 1), swap(y1, "c", 1), swap(y3, "c", 1)
    keep, send = call(
        pool2_kernel, [sds((quarter, width)), sds((quarter, width))], [VMEM] * 2, name="pool2"
    )(keep, got)
    got = swap(send, "z", 3)
    x2, y2, s0, s1, s3, got = lax.optimization_barrier((x2, y2, s0, s1, s3, got))
    part = call(means_kernel, sds((quarter, width), BF16), [VMEM] * 2, name="means")(keep, got)
    means, plog = call(
        join_kernel, [sds((PROTO_BLOCK, d), BF16), sds((8, 128))], [VMEM] * 5, name="join"
    )(logs, part, *[ahead(part, "z", k) for k in (1, 2, 3)])
    s2 = swap(y2, "c", 1)
    s0, s1, s2, s3, means = lax.optimization_barrier((s0, s1, s2, s3, means))
    vectors = [embeddings, x1, x2, x3, y1, y2, y3, s0, s1, s2, s3]

    bufs = [pltpu.VMEM((STEP, d), BF16), pltpu.VMEM((STEP, d), BF16), pltpu.SemaphoreType.DMA]

    def tile_call(body, n, m, part_rows, specs, extra, name):
        out = [pltpu.VMEM((n, m), F32), sds((part_rows, 128)), sds((8, 128)), HBM((n, d), BF16), HBM((m, d), BF16)]
        return call(
            body,
            out,
            specs,
            scratch=[
                pltpu.VMEM((n, d), BF16),
                pltpu.VMEM((m, d), BF16),
                pltpu.SemaphoreType.DMA((2 * Y,)),
                pltpu.SemaphoreType.DMA((X,)),
                pltpu.SemaphoreType.DMA((2,)),
                *extra,
                *bufs,
            ],
            out_specs=[VMEM, VMEM, VMEM, IN_HBM, IN_HBM],
            limit=14,
            name=name,
            flops=2 * n * m * d,
        )

    tall = pltpu.VMEM((n_rows, 128), F32)
    wide = pltpu.VMEM((8, n_cols), F32)
    mx1, mx3, my1, my3 = first(means)
    t0 = swap(means, "c", 1)
    tile, upart, *back = tile_call(
        fine_tile_kernel, n_rows, n_cols, n_cols // 128, [SMEM, VMEM] + [ANY] * 11, [tall, wide], "fine_tile"
    )(info, live_rows, *vectors)
    upart, mx1, mx3, my1, my3, t0 = lax.optimization_barrier((upart, mx1, mx3, my1, my3, t0))
    mx2, my2 = turn(mx1, "x", 1), turn(my1, "y", 1)
    t1, t3, t2 = swap(my1, "c", 1), swap(my3, "c", 1), swap(my2, "c", 1)
    back = held(tile, *back)

    ktile, part, *kback = tile_call(
        coarse_tile_kernel, k_rows, k_cols, 24, [ANY] * 11 + [VMEM], [pltpu.VMEM((8, k_cols), F32)], "coarse_tile"
    )(means, mx1, mx2, mx3, my1, my2, my3, t0, t1, t2, t3, plog)
    kback = held(ktile, *kback)
    kspecs = [VMEM, VMEM, IN_HBM, IN_HBM]
    mine = call(
        lambda *r: fold_y_kernel({"lse": [(0, 2)], "plog": (16, 16)}, *r),
        sds((24, 128)),
        [VMEM] * 4,
        name="fold_y1",
    )(*spread_over(part, "y"))
    other = swap(mine, "c", 1)

    part, plog_rows = call(
        coarse2_kernel,
        [sds((32, 128)), sds((16, 128))],
        [VMEM] * 5 + kspecs,
        scratch=[pltpu.VMEM((k_rows, 128), F32), *bufs],
        name="coarse2",
    )(mine, other, upart, plog, seat, *kback)

    part, plog_cols, seats = call(
        step3_kernel,
        [sds((40, 128)), sds((8, 128)), sds((12, 128))],
        [VMEM, VMEM] + [VMEM] * 4 + kspecs * 2,
        scratch=[wide, pltpu.VMEM((8, k_cols), F32), *bufs],
        name="step3",
    )(logs, live_cols, *spread_over(part, "x"), *kback, *back)
    mine = call(
        lambda *r: fold_y_kernel({"lse": [(0, 2), (16, 3)], "plog": None}, *r),
        sds((40, 128)),
        [VMEM] * 4,
        name="fold_y2",
    )(*spread_over(part, "y"))
    other = swap(mine, "c", 1)

    part = call(
        step4_kernel,
        sds((24, 128)),
        [VMEM, VMEM] + [VMEM] * 3 + kspecs * 2,
        scratch=[tall, pltpu.VMEM((k_rows, 128), F32), *bufs],
        name="step4",
    )(logs, live_rows, mine, other, plog_rows, *kback, *back)

    part, coarse = call(
        step5_kernel,
        [sds((24, 128)), sds((1, 128))],
        [VMEM, VMEM] + [VMEM] * 6 + kspecs,
        scratch=[pltpu.VMEM((k_cols, 128), F32), wide, *bufs],
        name="step5",
    )(logs, live_cols, *spread_over(part, "x"), plog_cols, seats, *back)
    mine = call(
        lambda *r: fold_y_kernel({"lse": [(0, 3)], "plog": None}, *r),
        sds((24, 128)),
        [VMEM] * 4,
        name="fold_y3",
    )(*spread_over(part, "y"))
    other = swap(mine, "c", 1)

    part, col = call(
        step6_kernel,
        [sds((16, 128)), sds((3, 128))],
        [VMEM, VMEM] + [VMEM] * 2 + kspecs,
        scratch=[tall, *bufs],
        name="step6",
    )(logs, live_rows, mine, other, *back)
    row = call(last_kernel, sds((3, 128)), [VMEM, VMEM] + [VMEM] * 4, name="last")(
        logs, live_cols, *spread_over(part, "x")
    )
    return row.reshape(rows), col.reshape(rows), coarse[0, :quarter]


def solution(mesh):
    split = Mesh(mesh.devices.reshape(Z, X, Y, 2), ("z", "x", "y", "c"))
    every = P(("z", "x", "y", "c"))
    return jax.shard_map(
        local,
        mesh=split,
        in_specs=(P(("z", "x", "y", "c"), None), every, P()),
        out_specs=(every, every, every),
        check_vma=False,
    )
```

```python
import math

import jax
import jax.numpy as jnp
from jax import lax
from jax.experimental import pallas as pl
from jax.experimental.pallas import tpu as pltpu
from jax.sharding import Mesh, PartitionSpec as P


PROTO_BLOCK = 256
EPS = 0.01
SC = math.log2(math.e) / EPS
NEG = -1e30
LOW, HIGH, PEAK = 2.0 ** -48, 2.0 ** 120, 2.0 ** 40
STEP = 256
F32 = jnp.float32
BF16 = jnp.bfloat16
MIB = 2 ** 20
X, Y, Z = 4, 4, 4
PAD = 128

VMEM = pl.BlockSpec(memory_space=pltpu.VMEM)
SMEM = pl.BlockSpec(memory_space=pltpu.SMEM)
ANY = pl.BlockSpec(memory_space=pl.ANY)


HBM = pltpu.MemorySpace.HBM
IN_HBM = pl.BlockSpec(memory_space=HBM)


def call(body, out_shape, in_specs, scratch=(), out_specs=None, limit=6, name=None, flops=0, nbytes=0):
    return pl.pallas_call(
        body,
        out_shape=out_shape,
        in_specs=in_specs,
        out_specs=out_specs or jax.tree.map(lambda _: VMEM, out_shape),
        scratch_shapes=list(scratch),
        compiler_params=pltpu.CompilerParams(vmem_limit_bytes=limit * MIB),
        cost_estimate=pl.CostEstimate(flops=flops, bytes_accessed=nbytes, transcendentals=0),
        name=name,
    )


def sds(shape, dtype=F32):
    return jax.ShapeDtypeStruct(shape, dtype)


def iota(shape, dim):
    return lax.broadcasted_iota(jnp.int32, shape, dim)


def to_lanes(col):
    n = col.shape[0]
    eye = iota((128, 128), 0) == iota((128, 128), 1)
    return jnp.concatenate(
        [
            jnp.sum(jnp.where(eye, col[k * 128:(k + 1) * 128], 0.0), axis=0, keepdims=True)
            for k in range(n // 128)
        ],
        axis=0,
    )


def to_rows(vals, out_ref):
    for k in range(vals.shape[0]):
        out_ref[k * 128:(k + 1) * 128, :] = jnp.transpose(
            jnp.broadcast_to(vals[k:k + 1, :], (128, 128))
        )


def lse2(parts):
    top = parts[0]
    for p in parts[1:]:
        top = jnp.maximum(top, p)
    total = jnp.exp2(parts[0] - top)
    for p in parts[1:]:
        total = total + jnp.exp2(p - top)
    return top + jnp.log2(total)


def in_range(total, peak):
    outside = jnp.sum(jnp.where((total > LOW) & (total < HIGH), 0.0, 1.0))
    return (outside == 0.0) & (peak <= PEAK)


def spread(vals, wide_ref):
    for k in range(vals.shape[0]):
        wide_ref[:, k * 128:(k + 1) * 128] = jnp.broadcast_to(vals[k:k + 1, :], (8, 128))


def store_lse(total, shift, peak, out_ref, safe):
    n = total.shape[0]
    good = in_range(total, peak)

    @pl.when(good)
    def _():
        out_ref[0:n, :] = jnp.log2(total) + shift

    @pl.when(jnp.logical_not(good))
    def _():
        safe()


def reduce_columns(tile, h, guard, out_ref, wide_ref, backup):
    rows, cols = tile.shape
    shift = jnp.max(h)
    spread(jnp.exp2(h - shift), wide_ref)
    lane, sub = iota((8, 128), 1), iota((8, 128), 0)

    def body(r, _):
        acc = jnp.zeros((8, 128), F32)
        for g in range(16):
            s = tile[pl.ds(pl.multiple_of(r * 128 + g * 8, 8), 8), :] * wide_ref[...]
            part = jnp.sum(s, axis=1, keepdims=True)
            acc = acc + jnp.where(lane == sub + 8 * g, part, 0.0)
        out_ref[pl.ds(r, 1), :] = jnp.sum(acc, axis=0, keepdims=True)
        return 0

    lax.fori_loop(0, rows // 128, body, 0, unroll=4)
    store_lse(
        out_ref[0:rows // 128, :], shift, jnp.max(guard[...]), out_ref,
        lambda: safe_columns(backup, h, out_ref, wide_ref),
    )


def reduce_rows(tile, h, guard, out_ref, tall_ref, backup):
    rows, cols = tile.shape
    shift = jnp.max(h)
    to_rows(jnp.exp2(h - shift), tall_ref)
    width, chunk = 512, 64
    groups = width // 128
    for strip in range(cols // width):
        at = pl.ds(strip * width, width)

        def body(c, acc):
            part = pl.ds(pl.multiple_of(c * chunk, chunk), chunk)
            s = tile[part, at] * jnp.concatenate([tall_ref[part, :]] * groups, axis=1)
            return acc + jnp.sum(s.reshape(chunk // 8, 8, width), axis=0)

        acc = lax.fori_loop(0, rows // chunk, body, jnp.zeros((8, width), F32), unroll=2)
        acc = jnp.sum(acc, axis=0, keepdims=True)
        for k in range(groups):
            row = strip * groups + k
            out_ref[row:row + 1, :] = acc[:, k * 128:(k + 1) * 128]
    store_lse(
        out_ref[0:cols // 128, :], shift, jnp.max(guard[...]), out_ref,
        lambda: safe_rows(backup, h, out_ref, tall_ref),
    )


def block_scores(backup, ci, cj):
    rows_hbm, cols_hbm, own, a_buf, b_buf, sem = backup
    for src, at, buf in ((rows_hbm, ci, a_buf), (cols_hbm, cj, b_buf)):
        copy = pltpu.make_async_copy(src.at[pl.ds(pl.multiple_of(at * STEP, STEP), STEP)], buf, sem)
        copy.start()
        copy.wait()
    s = dot_t(a_buf[...], b_buf[...])
    i, j = iota((STEP, STEP), 0) + ci * STEP, iota((STEP, STEP), 1) + cj * STEP
    return jnp.where((i == j) & (j < own), NEG, s)


def safe_columns(backup, h, out_ref, wide_ref):
    n, m = backup[0].shape[0] // STEP, backup[1].shape[0] // STEP
    spread(h, wide_ref)

    def by_rows(ci, _):
        def by_cols(cj, carry):
            top, total = carry
            s = block_scores(backup, ci, cj)
            s = s + wide_ref[0:1, pl.ds(pl.multiple_of(cj * STEP, STEP), STEP)]
            now = jnp.maximum(top, jnp.max(s, axis=1, keepdims=True))
            return now, total * jnp.exp2(top - now) + jnp.sum(jnp.exp2(s - now), axis=1, keepdims=True)

        top, total = lax.fori_loop(
            0, m, by_cols, (jnp.full((STEP, 1), NEG, F32), jnp.zeros((STEP, 1), F32))
        )
        lanes = to_lanes(jnp.broadcast_to(top + jnp.log2(total), (STEP, 128)))
        for k in range(STEP // 128):
            out_ref[pl.ds(ci * (STEP // 128) + k, 1), :] = lanes[k:k + 1, :]
        return 0

    lax.fori_loop(0, n, by_rows, 0)


def safe_rows(backup, h, out_ref, tall_ref):
    n, m = backup[0].shape[0] // STEP, backup[1].shape[0] // STEP
    to_rows(h, tall_ref)

    def by_cols(cj, _):
        def by_rows(ci, carry):
            top, total = carry
            add = tall_ref[pl.ds(pl.multiple_of(ci * STEP, STEP), STEP), :]
            s = block_scores(backup, ci, cj) + jnp.concatenate([add] * (STEP // 128), axis=1)
            now = jnp.maximum(top, jnp.max(s, axis=0, keepdims=True))
            return now, total * jnp.exp2(top - now) + jnp.sum(jnp.exp2(s - now), axis=0, keepdims=True)

        top, total = lax.fori_loop(
            0, n, by_rows, (jnp.full((1, STEP), NEG, F32), jnp.zeros((1, STEP), F32))
        )
        lse = top + jnp.log2(total)
        for k in range(STEP // 128):
            out_ref[pl.ds(cj * (STEP // 128) + k, 1), :] = lse[:, k * 128:(k + 1) * 128]
        return 0

    lax.fori_loop(0, m, by_cols, 0)


def info_place(info):
    return info[Z, 0], info[Z, 1], info[Z, 2], info[Z, 3]


def count_at(counts, z, x, y, c):
    return counts[z, (x * Y + y) * 2 + c]


def behind(at, c, k, n):
    return lax.rem(at + jnp.where(c == 0, n - k, k), n)


def row_counts(counts, idx):
    z, x, y, c = idx
    return [
        count_at(counts, z, x, behind(y, (c + dc) % 2, k, Y), (c + dc) % 2) for dc in range(2) for k in range(Y)
    ]


def col_counts(counts, idx):
    z, x, y, c = idx
    return [count_at(counts, z, behind(x, c, k, X), y, c) for k in range(X)]


def live_mask(block_counts, per):
    at = iota((per, 128), 0) * 128 + iota((per, 128), 1)
    return jnp.concatenate([jnp.where(at < n, 1.0, 0.0) for n in block_counts], axis=0)


def log2_of(n):
    return jnp.log2(jnp.full((1, 128), n, jnp.int32).astype(F32))


def from_columns(parts, first, per):
    blocks = []
    for j in range(X):
        rows = [first + (j - k) % X * per for k in range(X)]
        blocks.append(lse2([p[r:r + per, :] for p, r in zip(parts, rows)]))
    return jnp.concatenate(blocks, axis=0)


def gather_columns(parts, first, per):
    return jnp.concatenate([p[first:first + per, :] for p in parts], axis=0)


def fold_y(parts, first, per):
    blocks = []
    for dc in range(2):
        for j in range(Y):
            rows = [first + (dc * Y + (j - k if dc == 0 else j + k) % Y) * per for k in range(Y)]
            blocks.append(lse2([p[r:r + per, :] for p, r in zip(parts, rows)]))
    return jnp.concatenate(blocks, axis=0)


def fold_core(mine, other, first, per):
    half = Y * per
    return jnp.concatenate(
        [
            lse2([mine[first:first + half, :], other[first + half:first + 2 * half, :]]),
            lse2([mine[first + half:first + 2 * half, :], other[first:first + half, :]]),
        ],
        axis=0,
    )


def pool_kernel(info, emb, members, keep, send, live_rows, live_cols, seat, logs):
    idx = info_place(info)
    z, x, y, c = idx
    quarter = PROTO_BLOCK // Z
    per = members.shape[0]
    ids = members[...]
    which = lax.shift_right_logical(ids, 11)
    within = jnp.bitwise_and(ids, quarter - 1)
    turn = jnp.bitwise_xor(which, z)
    seat[...] = (turn * quarter + within).astype(F32)
    slot = jnp.where(turn == 0, 0, jnp.where(turn == 3, 1, turn + 1)) * quarter + within
    local = jnp.concatenate([slot[k:k + 1, :] for k in range(per)], axis=1)
    rows, d = emb.shape
    live = iota((1, rows), 1) < count_at(info, z, x, y, c)
    hot = ((iota((PROTO_BLOCK, rows), 0) == local) & live).astype(BF16)
    sums = jnp.dot(hot, emb[...], preferred_element_type=F32)
    sizes = jnp.dot(hot, jnp.ones((rows, PAD), BF16), preferred_element_type=F32)
    half = 2 * quarter
    keep[:, 0:d] = sums[0:half]
    keep[:, d:] = sizes[0:half]
    send[:, 0:d] = sums[half:]
    send[:, d:] = sizes[half:]
    live_rows[...] = live_mask(row_counts(info, idx), per)
    live_cols[...] = live_mask(col_counts(info, idx), per)
    mine, total = 0, 0
    for g in range(Z):
        n = info[g, 0]
        for s in range(1, X * Y * 2):
            n = n + info[g, s]
        mine = mine + jnp.where(g == z, n, 0)
        total = total + n
    logs[...] = jnp.concatenate([log2_of(mine), log2_of(total), jnp.zeros((6, 128), F32)], axis=0)


def code_sizes(sizes):
    high = jnp.floor(sizes * (1.0 / 256.0))
    low = sizes - 256.0 * high
    return jnp.where(iota(sizes.shape, 1) < 64, high, low).astype(BF16)


def read_sizes(block, d):
    coded = block[:, d:].astype(F32)
    return coded[:, 0:1] * 256.0 + coded[:, 64:65]


def pool2_kernel(mine, got, keep, send):
    quarter = mine.shape[0] // 2
    keep[...] = mine[0:quarter, :] + got[0:quarter, :]
    send[...] = mine[quarter:, :] + got[quarter:, :]


def means_kernel(mine, got, out):
    d = mine.shape[1] - PAD
    sums = mine[...] + got[...]
    sizes = sums[:, d:]
    out[:, 0:d] = (sums[:, 0:d] / sizes[:, 0:1]).astype(BF16)
    out[:, d:] = code_sizes(sizes)


def pair_kernel(mine, got, out):
    quarter = mine.shape[0]
    out[0:quarter, :] = mine[...]
    out[quarter:, :] = got[...]


def join_kernel(logs, mine, got, means, plog):
    quarter, width = mine.shape[0] // 2, mine.shape[1]
    d = width - PAD
    sizes = []
    for k, ref in enumerate((mine, got, got, mine)):
        block = ref[k // 2 * quarter:(k // 2 + 1) * quarter, :]
        means[k * quarter:(k + 1) * quarter, :] = block[:, 0:d]
        sizes.append(jnp.broadcast_to(read_sizes(block, d), (quarter, 128)))
    plog[...] = jnp.zeros(plog.shape, F32)
    plog[0:2, :] = jnp.log2(to_lanes(jnp.concatenate(sizes, axis=0))) - logs[1:2, :]


def fetch(pieces, buf, sems):
    size = pieces[0].shape[0]
    for b, p in enumerate(pieces):
        pltpu.make_async_copy(p, buf.at[pl.ds(b * size, size)], sems.at[b]).start()

    def wait(b):
        into = buf.at[pl.ds(pl.multiple_of(b * size, size), size)]
        pltpu.make_async_copy(into, into, sems.at[b]).wait()

    return wait


def gathered(own, xs, ys, swapped, rows_buf, cols_buf, row_sems, col_sems):
    wait_cols = fetch([own, *xs], cols_buf, col_sems)
    wait_rows = fetch([own, *ys, *swapped], rows_buf, row_sems)
    for b in range(X):
        wait_cols(b)
    return wait_rows


def dot_t(a, b):
    return lax.dot_general(a, b, (((1,), (1,)), ((), ())), preferred_element_type=F32) * SC


def fill_tile(tile, own, rows_buf, cols_buf, wait_rows, rows_out, cols_out, out_sems, peak, acc, live):
    rows, cols = tile.shape
    step, wide = 2 * own, 512
    save_cols = pltpu.make_async_copy(cols_buf, cols_out, out_sems.at[1])
    save_cols.start()
    peak[...] = jnp.zeros(peak.shape, F32)
    if acc is not None:
        acc[...] = jnp.zeros(acc.shape, F32)

    def body(i, _):
        wait_rows(2 * i)
        wait_rows(2 * i + 1)
        at = pl.ds(pl.multiple_of(i * step, step), step)
        pltpu.make_async_copy(rows_buf.at[at], rows_out.at[at], out_sems.at[0]).start()
        for j in range(cols // wide):
            across = pl.ds(j * wide, wide)
            s = dot_t(rows_buf[at, :], cols_buf[across, :])
            if j * wide < own:
                col = iota((step, wide), 1) + j * wide
                s = jnp.where((iota((step, wide), 0) + i * step == col) & (col < own), NEG, s)
            s = jnp.exp2(s)
            tile[at, across] = s
            parts = s.reshape(step // 8, 8, wide)
            most = jnp.max(parts, axis=0)
            for k in range(wide // 128):
                peak[...] = jnp.maximum(peak[...], most[:, k * 128:(k + 1) * 128])
            if acc is not None:
                s = s * jnp.concatenate([live[at, :]] * (wide // 128), axis=1)
                acc[:, across] += jnp.sum(s.reshape(step // 8, 8, wide), axis=0)
        return 0

    lax.fori_loop(0, rows // step, body, 0)
    save_cols.wait()
    pltpu.make_async_copy(rows_buf, rows_out, out_sems.at[0]).wait()


def coarse_tile_kernel(own, x1, x2, x3, y1, y2, y3, s0, s1, s2, s3, plog, tile, payload, peak, rows_out, cols_out,
                       rows_buf, cols_buf, row_sems, col_sems, out_sems, wide, a_buf, b_buf, sem):
    n = own.shape[0]
    wait_rows = gathered(own, (x1, x2, x3), (y1, y2, y3), (s0, s1, s2, s3), rows_buf, cols_buf, row_sems, col_sems)
    fill_tile(tile, n, rows_buf, cols_buf, wait_rows, rows_out, cols_out, out_sems, peak, None, None)
    rows, cols = tile.shape
    payload[...] = jnp.zeros(payload.shape, F32)
    backup = (rows_out, cols_out, n, a_buf, b_buf, sem)
    reduce_columns(tile, jnp.zeros((cols // 128, 128), F32), peak, payload, wide, backup)
    payload[rows // 128:rows // 128 + 2, :] = plog[0:2, :]


def fine_tile_kernel(info, live_rows, own, x1, x2, x3, y1, y2, y3, s0, s1, s2, s3, tile, part, peak, rows_out,
                     cols_out, rows_buf, cols_buf, row_sems, col_sems, out_sems, tall, acc, a_buf, b_buf, sem):
    n = own.shape[0]
    wait_rows = gathered(own, (x1, x2, x3), (y1, y2, y3), (s0, s1, s2, s3), rows_buf, cols_buf, row_sems, col_sems)
    for b, count in enumerate(row_counts(info, info_place(info))):
        tall[b * n:(b + 1) * n, :] = jnp.where(iota((n, 128), 0) < count, 1.0, 0.0)
    fill_tile(tile, n, rows_buf, cols_buf, wait_rows, rows_out, cols_out, out_sems, peak, acc, tall)
    rows, cols = tile.shape
    total = jnp.sum(acc[...], axis=0, keepdims=True)
    for k in range(cols // 128):
        part[k:k + 1, :] = total[:, k * 128:(k + 1) * 128]
    h = jnp.where(live_rows[...] > 0.0, 0.0, NEG)
    store_lse(
        part[...], 0.0, jnp.max(peak[...]), part,
        lambda: safe_rows((rows_out, cols_out, n, a_buf, b_buf, sem), h, part, tall),
    )


def fold_y_kernel(plan, *refs):
    parts, out = refs[0:Y], refs[Y]
    out[...] = jnp.zeros(out.shape, F32)
    for first, per in plan["lse"]:
        n = 2 * Y * per
        out[first:first + n, :] = fold_y(parts, first, per)
    if plan["plog"] is not None:
        first, into = plan["plog"]
        out[into:into + 2 * Y, :] = jnp.concatenate(
            [p[first:first + 2, :] for p in parts], axis=0
        )


def coarse2_kernel(mine, other, part, plog, seat, tile, peak, rows_hbm, cols_hbm, payload, plog_rows, tall, *bufs):
    plog_rows[0:8, :] = mine[16:24, :]
    plog_rows[8:16, :] = other[16:24, :]
    h = plog_rows[...] + SC - fold_core(mine, other, 0, 2)
    payload[...] = jnp.zeros(payload.shape, F32)
    reduce_rows(tile, h, peak, payload, tall, (rows_hbm, cols_hbm, PROTO_BLOCK, *bufs))
    payload[8:20, :] = part[...]
    payload[20:22, :] = plog[0:2, :]
    payload[22:25, :] = seat[...]


def fine_h(lse, logs, live, boost=0.0):
    return jnp.where(live[...] > 0.0, SC - logs[0:1, :] - lse + boost, NEG)


def step3_kernel(logs, live_cols, p0, p1, p2, p3, ktile, kpeak, krows, kcols, tile, peak, rows_hbm, cols_hbm,
                 payload, plog_cols, seats, wide, kwide, *bufs):
    parts = (p0, p1, p2, p3)
    plog_cols[...] = gather_columns(parts, 20, 2)
    seats[...] = gather_columns(parts, 22, 3)
    payload[...] = jnp.zeros(payload.shape, F32)
    h = fine_h(from_columns(parts, 8, 3), logs, live_cols)
    backup = (rows_hbm, cols_hbm, tile.shape[1] // X, *bufs)
    reduce_columns(tile, h, peak, payload.at[16:40, :], wide, backup)
    h = plog_cols[...] + SC - from_columns(parts, 0, 2)
    reduce_columns(ktile, h, kpeak, payload.at[0:16, :], kwide, (krows, kcols, PROTO_BLOCK, *bufs))


def step4_kernel(logs, live_rows, mine, other, plog_rows, ktile, kpeak, krows, kcols, tile, peak, rows_hbm, cols_hbm,
                 payload, tall, ktall, *bufs):
    payload[...] = jnp.zeros(payload.shape, F32)
    h = plog_rows[...] + SC - fold_core(mine, other, 0, 2)
    reduce_rows(ktile, h, kpeak, payload.at[0:8, :], ktall, (krows, kcols, PROTO_BLOCK, *bufs))
    h = fine_h(fold_core(mine, other, 16, 3), logs, live_rows)
    backup = (rows_hbm, cols_hbm, tile.shape[1] // X, *bufs)
    reduce_rows(tile, h, peak, payload.at[8:20, :], tall, backup)


def step5_kernel(logs, live_cols, p0, p1, p2, p3, plog_cols, seats, tile, peak, rows_hbm, cols_hbm,
                 payload, coarse, tall, wide, *bufs):
    parts = (p0, p1, p2, p3)
    v = plog_cols[...] + SC - from_columns(parts, 0, 2)
    coarse[...] = v[0:1, :] * (1.0 / SC)
    to_rows(v, tall)
    local = seats[...].astype(jnp.int32)
    boost = []
    for k in range(X * 3):
        vals = tall[(k // 3) * PROTO_BLOCK:(k // 3 + 1) * PROTO_BLOCK, :]
        pick = iota((PROTO_BLOCK, 128), 0) == local[k:k + 1, :]
        boost.append(jnp.sum(jnp.where(pick, vals, 0.0), axis=0, keepdims=True))
    h = fine_h(from_columns(parts, 8, 3), logs, live_cols, jnp.concatenate(boost, axis=0))
    payload[...] = jnp.zeros(payload.shape, F32)
    reduce_columns(tile, h, peak, payload, wide, (rows_hbm, cols_hbm, tile.shape[1] // X, *bufs))


def potential(h):
    return jnp.where(h == NEG, 0.0, h)[0:3, :] * (1.0 / SC)


def step6_kernel(logs, live_rows, mine, other, tile, peak, rows_hbm, cols_hbm, payload, out, tall, *bufs):
    h = fine_h(fold_core(mine, other, 0, 3), logs, live_rows)
    out[...] = potential(h)
    payload[...] = jnp.zeros(payload.shape, F32)
    backup = (rows_hbm, cols_hbm, tile.shape[1] // X, *bufs)
    reduce_rows(tile, h, peak, payload, tall, backup)


def last_kernel(logs, live_cols, p0, p1, p2, p3, out):
    out[...] = potential(fine_h(from_columns((p0, p1, p2, p3), 0, 3), logs, live_cols))


def swap(v, axis, bit):
    n = {"z": Z, "c": 2}[axis]
    return lax.ppermute(v, axis, [(i, i ^ bit) for i in range(n)])


def turn(v, axis, k):
    n = {"x": X, "y": Y}[axis]
    return lax.ppermute(
        v, (axis, "c"), [(i * 2 + c, (i + (k if c == 0 else n - k)) % n * 2 + c) for i in range(n) for c in range(2)]
    )


def spread_over(v, axis):
    return [v] + [turn(v, axis, k) for k in (1, 2, 3)]


def vmem(v):
    return pltpu.with_memory_space_constraint(v, pltpu.VMEM)


def held(tile, peak, rows, cols):
    return [vmem(tile), peak, *[pltpu.with_memory_space_constraint(v, HBM) for v in (rows, cols)]]


def local(embeddings, members, counts):
    rows, d = embeddings.shape
    here = jnp.stack([lax.axis_index(a) for a in ("z", "x", "y", "c")]).astype(jnp.int32)
    info = jnp.concatenate([counts, jnp.pad(here[None], ((0, 0), (0, counts.shape[1] - 4)))], axis=0)
    per = rows // 128
    n_rows, n_cols = rows * Y * 2, rows * X
    k_rows, k_cols = PROTO_BLOCK * Y * 2, PROTO_BLOCK * X
    quarter = PROTO_BLOCK // Z
    width = d + PAD

    def first(own):
        return turn(own, "x", 1), turn(own, "x", 3), turn(own, "y", 1), turn(own, "y", 3)

    x1, x3, y1, y3 = first(embeddings)
    x1, x3 = lax.optimization_barrier((x1, x3))
    y1, y3 = lax.optimization_barrier((y1, y3))
    x2, y2 = turn(x1, "x", 1), turn(y1, "y", 1)
    s0, s1, s3 = swap(embeddings, "c", 1), swap(y1, "c", 1), swap(y3, "c", 1)
    keep, send, live_rows, live_cols, seat, logs = call(
        pool_kernel,
        [
            sds((2 * quarter, width)), sds((2 * quarter, width)), sds((n_rows // 128, 128)),
            sds((n_cols // 128, 128)), sds((per, 128)), sds((8, 128)),
        ],
        [SMEM, VMEM, VMEM],
        name="pool",
    )(info, embeddings, members.reshape(per, 128))
    keep, send = call(
        pool2_kernel, [sds((quarter, width)), sds((quarter, width))], [VMEM] * 2, name="pool2"
    )(keep, swap(send, "z", 1))
    part = call(means_kernel, sds((quarter, width), BF16), [VMEM] * 2, name="means")(keep, swap(send, "z", 3))
    part = call(pair_kernel, sds((2 * quarter, width), BF16), [VMEM] * 2, name="pair")(part, swap(part, "z", 3))
    got = swap(part, "z", 1)
    x2, y2, s0, s1, s3, got = lax.optimization_barrier((x2, y2, s0, s1, s3, got))
    means, plog = call(
        join_kernel, [sds((PROTO_BLOCK, d), BF16), sds((8, 128))], [VMEM] * 3, name="join"
    )(logs, part, got)
    s2 = swap(y2, "c", 1)
    vectors = [embeddings, x1, x2, x3, y1, y2, y3, s0, s1, s2, s3]

    bufs = [pltpu.VMEM((STEP, d), BF16), pltpu.VMEM((STEP, d), BF16), pltpu.SemaphoreType.DMA]

    def tile_call(body, n, m, part_rows, specs, extra, name):
        out = [pltpu.VMEM((n, m), F32), sds((part_rows, 128)), sds((8, 128)), HBM((n, d), BF16), HBM((m, d), BF16)]
        return call(
            body,
            out,
            specs,
            scratch=[
                pltpu.VMEM((n, d), BF16),
                pltpu.VMEM((m, d), BF16),
                pltpu.SemaphoreType.DMA((2 * Y,)),
                pltpu.SemaphoreType.DMA((X,)),
                pltpu.SemaphoreType.DMA((2,)),
                *extra,
                *bufs,
            ],
            out_specs=[VMEM, VMEM, VMEM, IN_HBM, IN_HBM],
            limit=14,
            name=name,
            flops=2 * n * m * d,
        )

    tall = pltpu.VMEM((n_rows, 128), F32)
    wide = pltpu.VMEM((8, n_cols), F32)
    mx1, mx3, my1, my3 = first(means)
    t0 = swap(means, "c", 1)
    tile, upart, *back = tile_call(
        fine_tile_kernel, n_rows, n_cols, n_cols // 128, [SMEM, VMEM] + [ANY] * 11, [tall, wide], "fine_tile"
    )(info, live_rows, *vectors)
    upart, mx1, mx3, my1, my3, t0 = lax.optimization_barrier((upart, mx1, mx3, my1, my3, t0))
    mx2, my2 = turn(mx1, "x", 1), turn(my1, "y", 1)
    t1, t3, t2 = swap(my1, "c", 1), swap(my3, "c", 1), swap(my2, "c", 1)
    back = held(tile, *back)

    ktile, part, *kback = tile_call(
        coarse_tile_kernel, k_rows, k_cols, 24, [ANY] * 11 + [VMEM], [pltpu.VMEM((8, k_cols), F32)], "coarse_tile"
    )(means, mx1, mx2, mx3, my1, my2, my3, t0, t1, t2, t3, plog)
    kback = held(ktile, *kback)
    kspecs = [VMEM, VMEM, IN_HBM, IN_HBM]
    mine = call(
        lambda *r: fold_y_kernel({"lse": [(0, 2)], "plog": (16, 16)}, *r),
        sds((24, 128)),
        [VMEM] * 4,
        name="fold_y1",
    )(*spread_over(part, "y"))
    other = swap(mine, "c", 1)

    part, plog_rows = call(
        coarse2_kernel,
        [sds((32, 128)), sds((16, 128))],
        [VMEM] * 5 + kspecs,
        scratch=[pltpu.VMEM((k_rows, 128), F32), *bufs],
        name="coarse2",
    )(mine, other, upart, plog, seat, *kback)

    part, plog_cols, seats = call(
        step3_kernel,
        [sds((40, 128)), sds((8, 128)), sds((12, 128))],
        [VMEM, VMEM] + [VMEM] * 4 + kspecs * 2,
        scratch=[wide, pltpu.VMEM((8, k_cols), F32), *bufs],
        name="step3",
    )(logs, live_cols, *spread_over(part, "x"), *kback, *back)
    mine = call(
        lambda *r: fold_y_kernel({"lse": [(0, 2), (16, 3)], "plog": None}, *r),
        sds((40, 128)),
        [VMEM] * 4,
        name="fold_y2",
    )(*spread_over(part, "y"))
    other = swap(mine, "c", 1)

    part = call(
        step4_kernel,
        sds((24, 128)),
        [VMEM, VMEM] + [VMEM] * 3 + kspecs * 2,
        scratch=[tall, pltpu.VMEM((k_rows, 128), F32), *bufs],
        name="step4",
    )(logs, live_rows, mine, other, plog_rows, *kback, *back)

    part, coarse = call(
        step5_kernel,
        [sds((24, 128)), sds((1, 128))],
        [VMEM, VMEM] + [VMEM] * 6 + kspecs,
        scratch=[pltpu.VMEM((k_cols, 128), F32), wide, *bufs],
        name="step5",
    )(logs, live_cols, *spread_over(part, "x"), plog_cols, seats, *back)
    mine = call(
        lambda *r: fold_y_kernel({"lse": [(0, 3)], "plog": None}, *r),
        sds((24, 128)),
        [VMEM] * 4,
        name="fold_y3",
    )(*spread_over(part, "y"))
    other = swap(mine, "c", 1)

    part, col = call(
        step6_kernel,
        [sds((16, 128)), sds((3, 128))],
        [VMEM, VMEM] + [VMEM] * 2 + kspecs,
        scratch=[tall, *bufs],
        name="step6",
    )(logs, live_rows, mine, other, *back)
    row = call(last_kernel, sds((3, 128)), [VMEM, VMEM] + [VMEM] * 4, name="last")(
        logs, live_cols, *spread_over(part, "x")
    )
    return row.reshape(rows), col.reshape(rows), coarse[0, :quarter]


def solution(mesh):
    split = Mesh(mesh.devices.reshape(Z, X, Y, 2), ("z", "x", "y", "c"))
    every = P(("z", "x", "y", "c"))
    return jax.shard_map(
        local,
        mesh=split,
        in_specs=(P(("z", "x", "y", "c"), None), every, P()),
        out_specs=(every, every, every),
        check_vma=False,
    )
```

```python
import math

import jax
import jax.numpy as jnp
from jax import lax
from jax.experimental import pallas as pl
from jax.experimental.pallas import tpu as pltpu
from jax.sharding import Mesh, PartitionSpec as P


PROTO_BLOCK = 256
EPS = 0.01
SC = math.log2(math.e) / EPS
NEG = -1e30
LOW, HIGH, PEAK = 2.0 ** -25, 2.0 ** 120, 2.0 ** 64
STEP = 256
F32 = jnp.float32
BF16 = jnp.bfloat16
MIB = 2 ** 20
X, Y, Z = 4, 4, 4
PAD = 128

VMEM = pl.BlockSpec(memory_space=pltpu.VMEM)
SMEM = pl.BlockSpec(memory_space=pltpu.SMEM)
ANY = pl.BlockSpec(memory_space=pl.ANY)


HBM = pltpu.MemorySpace.HBM
IN_HBM = pl.BlockSpec(memory_space=HBM)


def call(body, out_shape, in_specs, scratch=(), out_specs=None, limit=6, name=None, flops=0, nbytes=0):
    return pl.pallas_call(
        body,
        out_shape=out_shape,
        in_specs=in_specs,
        out_specs=out_specs or jax.tree.map(lambda _: VMEM, out_shape),
        scratch_shapes=list(scratch),
        compiler_params=pltpu.CompilerParams(vmem_limit_bytes=limit * MIB),
        cost_estimate=pl.CostEstimate(flops=flops, bytes_accessed=nbytes, transcendentals=0),
        name=name,
    )


def sds(shape, dtype=F32):
    return jax.ShapeDtypeStruct(shape, dtype)


def iota(shape, dim):
    return lax.broadcasted_iota(jnp.int32, shape, dim)


def to_lanes(col):
    n = col.shape[0]
    eye = iota((128, 128), 0) == iota((128, 128), 1)
    return jnp.concatenate(
        [
            jnp.sum(jnp.where(eye, col[k * 128:(k + 1) * 128], 0.0), axis=0, keepdims=True)
            for k in range(n // 128)
        ],
        axis=0,
    )


def to_rows(vals, out_ref):
    for k in range(vals.shape[0]):
        out_ref[k * 128:(k + 1) * 128, :] = jnp.transpose(
            jnp.broadcast_to(vals[k:k + 1, :], (128, 128))
        )


def lse2(parts):
    top = parts[0]
    for p in parts[1:]:
        top = jnp.maximum(top, p)
    total = jnp.exp2(parts[0] - top)
    for p in parts[1:]:
        total = total + jnp.exp2(p - top)
    return top + jnp.log2(total)


def in_range(total, peak):
    outside = jnp.sum(jnp.where((total > LOW) & (total < HIGH), 0.0, 1.0))
    return (outside == 0.0) & (peak <= PEAK)


def spread(vals, wide_ref):
    for k in range(vals.shape[0]):
        wide_ref[:, k * 128:(k + 1) * 128] = jnp.broadcast_to(vals[k:k + 1, :], (8, 128))


def store_lse(total, shift, peak, out_ref, safe):
    n = total.shape[0]
    good = in_range(total, peak)

    @pl.when(good)
    def _():
        out_ref[0:n, :] = jnp.log2(total) + shift

    @pl.when(jnp.logical_not(good))
    def _():
        safe()


def reduce_columns(tile, h, guard, out_ref, wide_ref, backup):
    rows, cols = tile.shape
    shift = jnp.max(h)
    spread(jnp.exp2(h - shift), wide_ref)
    lane, sub = iota((8, 128), 1), iota((8, 128), 0)

    def body(r, _):
        acc = jnp.zeros((8, 128), F32)
        for g in range(16):
            s = tile[pl.ds(pl.multiple_of(r * 128 + g * 8, 8), 8), :] * wide_ref[...]
            part = jnp.sum(s, axis=1, keepdims=True)
            acc = acc + jnp.where(lane == sub + 8 * g, part, 0.0)
        out_ref[pl.ds(r, 1), :] = jnp.sum(acc, axis=0, keepdims=True)
        return 0

    lax.fori_loop(0, rows // 128, body, 0, unroll=4)
    store_lse(
        out_ref[0:rows // 128, :], shift, jnp.max(guard[...]), out_ref,
        lambda: safe_columns(backup, h, out_ref, wide_ref),
    )


def reduce_rows(tile, h, guard, out_ref, tall_ref, backup):
    rows, cols = tile.shape
    shift = jnp.max(h)
    to_rows(jnp.exp2(h - shift), tall_ref)
    width, chunk = 512, 64
    groups = width // 128
    for strip in range(cols // width):
        at = pl.ds(strip * width, width)

        def body(c, acc):
            part = pl.ds(pl.multiple_of(c * chunk, chunk), chunk)
            s = tile[part, at] * jnp.concatenate([tall_ref[part, :]] * groups, axis=1)
            return acc + jnp.sum(s.reshape(chunk // 8, 8, width), axis=0)

        acc = lax.fori_loop(0, rows // chunk, body, jnp.zeros((8, width), F32), unroll=2)
        acc = jnp.sum(acc, axis=0, keepdims=True)
        for k in range(groups):
            row = strip * groups + k
            out_ref[row:row + 1, :] = acc[:, k * 128:(k + 1) * 128]
    store_lse(
        out_ref[0:cols // 128, :], shift, jnp.max(guard[...]), out_ref,
        lambda: safe_rows(backup, h, out_ref, tall_ref),
    )


def block_scores(backup, ci, cj):
    rows_hbm, cols_hbm, own, a_buf, b_buf, sem = backup
    for src, at, buf in ((rows_hbm, ci, a_buf), (cols_hbm, cj, b_buf)):
        copy = pltpu.make_async_copy(src.at[pl.ds(pl.multiple_of(at * STEP, STEP), STEP)], buf, sem)
        copy.start()
        copy.wait()
    s = dot_t(a_buf[...], b_buf[...])
    i, j = iota((STEP, STEP), 0) + ci * STEP, iota((STEP, STEP), 1) + cj * STEP
    return jnp.where((i == j) & (j < own), NEG, s)


def safe_columns(backup, h, out_ref, wide_ref):
    n, m = backup[0].shape[0] // STEP, backup[1].shape[0] // STEP
    spread(h, wide_ref)

    def by_rows(ci, _):
        def by_cols(cj, carry):
            top, total = carry
            s = block_scores(backup, ci, cj)
            s = s + wide_ref[0:1, pl.ds(pl.multiple_of(cj * STEP, STEP), STEP)]
            now = jnp.maximum(top, jnp.max(s, axis=1, keepdims=True))
            return now, total * jnp.exp2(top - now) + jnp.sum(jnp.exp2(s - now), axis=1, keepdims=True)

        top, total = lax.fori_loop(
            0, m, by_cols, (jnp.full((STEP, 1), NEG, F32), jnp.zeros((STEP, 1), F32))
        )
        lanes = to_lanes(jnp.broadcast_to(top + jnp.log2(total), (STEP, 128)))
        for k in range(STEP // 128):
            out_ref[pl.ds(ci * (STEP // 128) + k, 1), :] = lanes[k:k + 1, :]
        return 0

    lax.fori_loop(0, n, by_rows, 0)


def safe_rows(backup, h, out_ref, tall_ref):
    n, m = backup[0].shape[0] // STEP, backup[1].shape[0] // STEP
    to_rows(h, tall_ref)

    def by_cols(cj, _):
        def by_rows(ci, carry):
            top, total = carry
            add = tall_ref[pl.ds(pl.multiple_of(ci * STEP, STEP), STEP), :]
            s = block_scores(backup, ci, cj) + jnp.concatenate([add] * (STEP // 128), axis=1)
            now = jnp.maximum(top, jnp.max(s, axis=0, keepdims=True))
            return now, total * jnp.exp2(top - now) + jnp.sum(jnp.exp2(s - now), axis=0, keepdims=True)

        top, total = lax.fori_loop(
            0, n, by_rows, (jnp.full((1, STEP), NEG, F32), jnp.zeros((1, STEP), F32))
        )
        lse = top + jnp.log2(total)
        for k in range(STEP // 128):
            out_ref[pl.ds(cj * (STEP // 128) + k, 1), :] = lse[:, k * 128:(k + 1) * 128]
        return 0

    lax.fori_loop(0, m, by_cols, 0)


def info_place(info):
    return info[Z, 0], info[Z, 1], info[Z, 2], info[Z, 3]


def count_at(counts, z, x, y, c):
    return counts[z, (x * Y + y) * 2 + c]


def behind(at, c, k, n):
    return lax.rem(at + jnp.where(c == 0, n - k, k), n)


def row_counts(counts, idx):
    z, x, y, c = idx
    return [
        count_at(counts, z, x, behind(y, (c + dc) % 2, k, Y), (c + dc) % 2) for dc in range(2) for k in range(Y)
    ]


def col_counts(counts, idx):
    z, x, y, c = idx
    return [count_at(counts, z, behind(x, c, k, X), y, c) for k in range(X)]


def live_mask(block_counts, per):
    at = iota((per, 128), 0) * 128 + iota((per, 128), 1)
    return jnp.concatenate([jnp.where(at < n, 1.0, 0.0) for n in block_counts], axis=0)


def log2_of(n):
    return jnp.log2(jnp.full((1, 128), n, jnp.int32).astype(F32))


def from_columns(parts, first, per):
    blocks = []
    for j in range(X):
        rows = [first + (j - k) % X * per for k in range(X)]
        blocks.append(lse2([p[r:r + per, :] for p, r in zip(parts, rows)]))
    return jnp.concatenate(blocks, axis=0)


def gather_columns(parts, first, per):
    return jnp.concatenate([p[first:first + per, :] for p in parts], axis=0)


def fold_y(parts, first, per):
    blocks = []
    for dc in range(2):
        for j in range(Y):
            rows = [first + (dc * Y + (j - k if dc == 0 else j + k) % Y) * per for k in range(Y)]
            blocks.append(lse2([p[r:r + per, :] for p, r in zip(parts, rows)]))
    return jnp.concatenate(blocks, axis=0)


def fold_core(mine, other, first, per):
    half = Y * per
    return jnp.concatenate(
        [
            lse2([mine[first:first + half, :], other[first + half:first + 2 * half, :]]),
            lse2([mine[first + half:first + 2 * half, :], other[first:first + half, :]]),
        ],
        axis=0,
    )


def pool_kernel(info, emb, members, keep, send, live_rows, live_cols, seat, logs):
    idx = info_place(info)
    z, x, y, c = idx
    quarter = PROTO_BLOCK // Z
    per = members.shape[0]
    ids = members[...]
    which = lax.shift_right_logical(ids, 11)
    within = jnp.bitwise_and(ids, quarter - 1)
    turn = jnp.bitwise_xor(which, z)
    seat[...] = (turn * quarter + within).astype(F32)
    slot = jnp.where(turn == 0, 0, jnp.where(turn == 3, 1, turn + 1)) * quarter + within
    local = jnp.concatenate([slot[k:k + 1, :] for k in range(per)], axis=1)
    rows, d = emb.shape
    live = iota((1, rows), 1) < count_at(info, z, x, y, c)
    hot = ((iota((PROTO_BLOCK, rows), 0) == local) & live).astype(BF16)
    sums = jnp.dot(hot, emb[...], preferred_element_type=F32)
    sizes = jnp.dot(hot, jnp.ones((rows, PAD), BF16), preferred_element_type=F32)
    half = 2 * quarter
    keep[:, 0:d] = sums[0:half]
    keep[:, d:] = sizes[0:half]
    send[:, 0:d] = sums[half:]
    send[:, d:] = sizes[half:]
    live_rows[...] = live_mask(row_counts(info, idx), per)
    live_cols[...] = live_mask(col_counts(info, idx), per)
    mine, total = 0, 0
    for g in range(Z):
        n = info[g, 0]
        for s in range(1, X * Y * 2):
            n = n + info[g, s]
        mine = mine + jnp.where(g == z, n, 0)
        total = total + n
    logs[...] = jnp.concatenate([log2_of(mine), log2_of(total), jnp.zeros((6, 128), F32)], axis=0)


def code_sizes(sizes):
    high = jnp.floor(sizes * (1.0 / 256.0))
    low = sizes - 256.0 * high
    return jnp.where(iota(sizes.shape, 1) < 64, high, low).astype(BF16)


def read_sizes(block, d):
    coded = block[:, d:].astype(F32)
    return coded[:, 0:1] * 256.0 + coded[:, 64:65]


def pool2_kernel(mine, got, keep, send):
    quarter = mine.shape[0] // 2
    keep[...] = mine[0:quarter, :] + got[0:quarter, :]
    send[...] = mine[quarter:, :] + got[quarter:, :]


def means_kernel(mine, got, out):
    d = mine.shape[1] - PAD
    sums = mine[...] + got[...]
    sizes = sums[:, d:]
    out[:, 0:d] = (sums[:, 0:d] / sizes[:, 0:1]).astype(BF16)
    out[:, d:] = code_sizes(sizes)


def pair_kernel(mine, got, out):
    quarter = mine.shape[0]
    out[0:quarter, :] = mine[...]
    out[quarter:, :] = got[...]


def join_kernel(logs, mine, got, means, plog):
    quarter, width = mine.shape[0] // 2, mine.shape[1]
    d = width - PAD
    sizes = []
    for k, ref in enumerate((mine, got, got, mine)):
        block = ref[k // 2 * quarter:(k // 2 + 1) * quarter, :]
        means[k * quarter:(k + 1) * quarter, :] = block[:, 0:d]
        sizes.append(jnp.broadcast_to(read_sizes(block, d), (quarter, 128)))
    plog[...] = jnp.zeros(plog.shape, F32)
    plog[0:2, :] = jnp.log2(to_lanes(jnp.concatenate(sizes, axis=0))) - logs[1:2, :]


def fetch(pieces, buf, sems):
    size = pieces[0].shape[0]
    for b, p in enumerate(pieces):
        pltpu.make_async_copy(p, buf.at[pl.ds(b * size, size)], sems.at[b]).start()

    def wait(b):
        into = buf.at[pl.ds(pl.multiple_of(b * size, size), size)]
        pltpu.make_async_copy(into, into, sems.at[b]).wait()

    return wait


def gathered(own, xs, ys, swapped, rows_buf, cols_buf, row_sems, col_sems):
    wait_cols = fetch([own, *xs], cols_buf, col_sems)
    wait_rows = fetch([own, *ys, *swapped], rows_buf, row_sems)
    for b in range(X):
        wait_cols(b)
    return wait_rows


def dot_t(a, b):
    return lax.dot_general(a, b, (((1,), (1,)), ((), ())), preferred_element_type=F32) * SC


def fill_tile(tile, own, rows_buf, cols_buf, wait_rows, rows_out, cols_out, out_sems, peak, acc, live):
    rows, cols = tile.shape
    step, wide = 2 * own, 512
    save_cols = pltpu.make_async_copy(cols_buf, cols_out, out_sems.at[1])
    save_cols.start()
    peak[...] = jnp.zeros(peak.shape, F32)
    if acc is not None:
        acc[...] = jnp.zeros(acc.shape, F32)

    def body(i, _):
        wait_rows(2 * i)
        wait_rows(2 * i + 1)
        at = pl.ds(pl.multiple_of(i * step, step), step)
        pltpu.make_async_copy(rows_buf.at[at], rows_out.at[at], out_sems.at[0]).start()
        for j in range(cols // wide):
            across = pl.ds(j * wide, wide)
            s = dot_t(rows_buf[at, :], cols_buf[across, :])
            if j * wide < own:
                col = iota((step, wide), 1) + j * wide
                s = jnp.where((iota((step, wide), 0) + i * step == col) & (col < own), NEG, s)
            s = jnp.exp2(s)
            tile[at, across] = s
            parts = s.reshape(step // 8, 8, wide)
            most = jnp.max(parts, axis=0)
            for k in range(wide // 128):
                peak[...] = jnp.maximum(peak[...], most[:, k * 128:(k + 1) * 128])
            if acc is not None:
                s = s * jnp.concatenate([live[at, :]] * (wide // 128), axis=1)
                acc[:, across] += jnp.sum(s.reshape(step // 8, 8, wide), axis=0)
        return 0

    lax.fori_loop(0, rows // step, body, 0)
    save_cols.wait()
    pltpu.make_async_copy(rows_buf, rows_out, out_sems.at[0]).wait()


def coarse_tile_kernel(own, x1, x2, x3, y1, y2, y3, s0, s1, s2, s3, plog, tile, payload, peak, rows_out, cols_out,
                       rows_buf, cols_buf, row_sems, col_sems, out_sems, wide, a_buf, b_buf, sem):
    n = own.shape[0]
    wait_rows = gathered(own, (x1, x2, x3), (y1, y2, y3), (s0, s1, s2, s3), rows_buf, cols_buf, row_sems, col_sems)
    fill_tile(tile, n, rows_buf, cols_buf, wait_rows, rows_out, cols_out, out_sems, peak, None, None)
    rows, cols = tile.shape
    payload[...] = jnp.zeros(payload.shape, F32)
    backup = (rows_out, cols_out, n, a_buf, b_buf, sem)
    reduce_columns(tile, jnp.zeros((cols // 128, 128), F32), peak, payload, wide, backup)
    payload[rows // 128:rows // 128 + 2, :] = plog[0:2, :]


def fine_tile_kernel(info, live_rows, own, x1, x2, x3, y1, y2, y3, s0, s1, s2, s3, tile, part, peak, rows_out,
                     cols_out, rows_buf, cols_buf, row_sems, col_sems, out_sems, tall, acc, a_buf, b_buf, sem):
    n = own.shape[0]
    wait_rows = gathered(own, (x1, x2, x3), (y1, y2, y3), (s0, s1, s2, s3), rows_buf, cols_buf, row_sems, col_sems)
    for b, count in enumerate(row_counts(info, info_place(info))):
        tall[b * n:(b + 1) * n, :] = jnp.where(iota((n, 128), 0) < count, 1.0, 0.0)
    fill_tile(tile, n, rows_buf, cols_buf, wait_rows, rows_out, cols_out, out_sems, peak, acc, tall)
    rows, cols = tile.shape
    total = jnp.sum(acc[...], axis=0, keepdims=True)
    for k in range(cols // 128):
        part[k:k + 1, :] = total[:, k * 128:(k + 1) * 128]
    h = jnp.where(live_rows[...] > 0.0, 0.0, NEG)
    store_lse(
        part[...], 0.0, jnp.max(peak[...]), part,
        lambda: safe_rows((rows_out, cols_out, n, a_buf, b_buf, sem), h, part, tall),
    )


def fold_y_kernel(plan, *refs):
    parts, out = refs[0:Y], refs[Y]
    out[...] = jnp.zeros(out.shape, F32)
    for first, per in plan["lse"]:
        n = 2 * Y * per
        out[first:first + n, :] = fold_y(parts, first, per)
    if plan["plog"] is not None:
        first, into = plan["plog"]
        out[into:into + 2 * Y, :] = jnp.concatenate(
            [p[first:first + 2, :] for p in parts], axis=0
        )


def coarse2_kernel(mine, other, part, plog, seat, tile, peak, rows_hbm, cols_hbm, payload, plog_rows, tall, *bufs):
    plog_rows[0:8, :] = mine[16:24, :]
    plog_rows[8:16, :] = other[16:24, :]
    h = plog_rows[...] + SC - fold_core(mine, other, 0, 2)
    payload[...] = jnp.zeros(payload.shape, F32)
    reduce_rows(tile, h, peak, payload, tall, (rows_hbm, cols_hbm, PROTO_BLOCK, *bufs))
    payload[8:20, :] = part[...]
    payload[20:22, :] = plog[0:2, :]
    payload[22:25, :] = seat[...]


def fine_h(lse, logs, live, boost=0.0):
    return jnp.where(live[...] > 0.0, SC - logs[0:1, :] - lse + boost, NEG)


def step3_kernel(logs, live_cols, p0, p1, p2, p3, ktile, kpeak, krows, kcols, tile, peak, rows_hbm, cols_hbm,
                 payload, plog_cols, seats, wide, kwide, *bufs):
    parts = (p0, p1, p2, p3)
    plog_cols[...] = gather_columns(parts, 20, 2)
    seats[...] = gather_columns(parts, 22, 3)
    payload[...] = jnp.zeros(payload.shape, F32)
    h = fine_h(from_columns(parts, 8, 3), logs, live_cols)
    backup = (rows_hbm, cols_hbm, tile.shape[1] // X, *bufs)
    reduce_columns(tile, h, peak, payload.at[16:40, :], wide, backup)
    h = plog_cols[...] + SC - from_columns(parts, 0, 2)
    reduce_columns(ktile, h, kpeak, payload.at[0:16, :], kwide, (krows, kcols, PROTO_BLOCK, *bufs))


def step4_kernel(logs, live_rows, mine, other, plog_rows, ktile, kpeak, krows, kcols, tile, peak, rows_hbm, cols_hbm,
                 payload, tall, ktall, *bufs):
    payload[...] = jnp.zeros(payload.shape, F32)
    h = plog_rows[...] + SC - fold_core(mine, other, 0, 2)
    reduce_rows(ktile, h, kpeak, payload.at[0:8, :], ktall, (krows, kcols, PROTO_BLOCK, *bufs))
    h = fine_h(fold_core(mine, other, 16, 3), logs, live_rows)
    backup = (rows_hbm, cols_hbm, tile.shape[1] // X, *bufs)
    reduce_rows(tile, h, peak, payload.at[8:20, :], tall, backup)


def step5_kernel(logs, live_cols, p0, p1, p2, p3, plog_cols, seats, tile, peak, rows_hbm, cols_hbm,
                 payload, coarse, tall, wide, *bufs):
    parts = (p0, p1, p2, p3)
    v = plog_cols[...] + SC - from_columns(parts, 0, 2)
    coarse[...] = v[0:1, :] * (1.0 / SC)
    to_rows(v, tall)
    local = seats[...].astype(jnp.int32)
    boost = []
    for k in range(X * 3):
        vals = tall[(k // 3) * PROTO_BLOCK:(k // 3 + 1) * PROTO_BLOCK, :]
        pick = iota((PROTO_BLOCK, 128), 0) == local[k:k + 1, :]
        boost.append(jnp.sum(jnp.where(pick, vals, 0.0), axis=0, keepdims=True))
    h = fine_h(from_columns(parts, 8, 3), logs, live_cols, jnp.concatenate(boost, axis=0))
    payload[...] = jnp.zeros(payload.shape, F32)
    reduce_columns(tile, h, peak, payload, wide, (rows_hbm, cols_hbm, tile.shape[1] // X, *bufs))


def potential(h):
    return jnp.where(h == NEG, 0.0, h)[0:3, :] * (1.0 / SC)


def step6_kernel(logs, live_rows, mine, other, tile, peak, rows_hbm, cols_hbm, payload, out, tall, *bufs):
    h = fine_h(fold_core(mine, other, 0, 3), logs, live_rows)
    out[...] = potential(h)
    payload[...] = jnp.zeros(payload.shape, F32)
    backup = (rows_hbm, cols_hbm, tile.shape[1] // X, *bufs)
    reduce_rows(tile, h, peak, payload, tall, backup)


def last_kernel(logs, live_cols, p0, p1, p2, p3, out):
    out[...] = potential(fine_h(from_columns((p0, p1, p2, p3), 0, 3), logs, live_cols))


def swap(v, axis, bit):
    n = {"z": Z, "c": 2}[axis]
    return lax.ppermute(v, axis, [(i, i ^ bit) for i in range(n)])


def turn(v, axis, k):
    n = {"x": X, "y": Y}[axis]
    return lax.ppermute(
        v, (axis, "c"), [(i * 2 + c, (i + (k if c == 0 else n - k)) % n * 2 + c) for i in range(n) for c in range(2)]
    )


def spread_over(v, axis):
    return [v] + [turn(v, axis, k) for k in (1, 2, 3)]


def vmem(v):
    return pltpu.with_memory_space_constraint(v, pltpu.VMEM)


def held(tile, peak, rows, cols):
    return [vmem(tile), peak, *[pltpu.with_memory_space_constraint(v, HBM) for v in (rows, cols)]]


def local(embeddings, members, counts):
    rows, d = embeddings.shape
    here = jnp.stack([lax.axis_index(a) for a in ("z", "x", "y", "c")]).astype(jnp.int32)
    info = jnp.concatenate([counts, jnp.pad(here[None], ((0, 0), (0, counts.shape[1] - 4)))], axis=0)
    per = rows // 128
    n_rows, n_cols = rows * Y * 2, rows * X
    k_rows, k_cols = PROTO_BLOCK * Y * 2, PROTO_BLOCK * X
    quarter = PROTO_BLOCK // Z
    width = d + PAD

    def first(own):
        return turn(own, "x", 1), turn(own, "x", 3), turn(own, "y", 1), turn(own, "y", 3)

    x1, x3, y1, y3 = first(embeddings)
    x1, x3 = lax.optimization_barrier((x1, x3))
    y1, y3 = lax.optimization_barrier((y1, y3))
    x2, y2 = turn(x1, "x", 1), turn(y1, "y", 1)
    s0, s1, s3 = swap(embeddings, "c", 1), swap(y1, "c", 1), swap(y3, "c", 1)
    keep, send, live_rows, live_cols, seat, logs = call(
        pool_kernel,
        [
            sds((2 * quarter, width)), sds((2 * quarter, width)), sds((n_rows // 128, 128)),
            sds((n_cols // 128, 128)), sds((per, 128)), sds((8, 128)),
        ],
        [SMEM, VMEM, VMEM],
        name="pool",
    )(info, embeddings, members.reshape(per, 128))
    keep, send = call(
        pool2_kernel, [sds((quarter, width)), sds((quarter, width))], [VMEM] * 2, name="pool2"
    )(keep, swap(send, "z", 1))
    part = call(means_kernel, sds((quarter, width), BF16), [VMEM] * 2, name="means")(keep, swap(send, "z", 3))
    part = call(pair_kernel, sds((2 * quarter, width), BF16), [VMEM] * 2, name="pair")(part, swap(part, "z", 3))
    got = swap(part, "z", 1)
    x2, y2, s0, s1, s3, got = lax.optimization_barrier((x2, y2, s0, s1, s3, got))
    means, plog = call(
        join_kernel, [sds((PROTO_BLOCK, d), BF16), sds((8, 128))], [VMEM] * 3, name="join"
    )(logs, part, got)
    s2 = swap(y2, "c", 1)
    vectors = [embeddings, x1, x2, x3, y1, y2, y3, s0, s1, s2, s3]

    bufs = [pltpu.VMEM((STEP, d), BF16), pltpu.VMEM((STEP, d), BF16), pltpu.SemaphoreType.DMA]

    def tile_call(body, n, m, part_rows, specs, extra, name):
        out = [pltpu.VMEM((n, m), F32), sds((part_rows, 128)), sds((8, 128)), HBM((n, d), BF16), HBM((m, d), BF16)]
        return call(
            body,
            out,
            specs,
            scratch=[
                pltpu.VMEM((n, d), BF16),
                pltpu.VMEM((m, d), BF16),
                pltpu.SemaphoreType.DMA((2 * Y,)),
                pltpu.SemaphoreType.DMA((X,)),
                pltpu.SemaphoreType.DMA((2,)),
                *extra,
                *bufs,
            ],
            out_specs=[VMEM, VMEM, VMEM, IN_HBM, IN_HBM],
            limit=14,
            name=name,
            flops=2 * n * m * d,
        )

    tall = pltpu.VMEM((n_rows, 128), F32)
    wide = pltpu.VMEM((8, n_cols), F32)
    mx1, mx3, my1, my3 = first(means)
    t0 = swap(means, "c", 1)
    tile, upart, *back = tile_call(
        fine_tile_kernel, n_rows, n_cols, n_cols // 128, [SMEM, VMEM] + [ANY] * 11, [tall, wide], "fine_tile"
    )(info, live_rows, *vectors)
    upart, mx1, mx3, my1, my3, t0 = lax.optimization_barrier((upart, mx1, mx3, my1, my3, t0))
    mx2, my2 = turn(mx1, "x", 1), turn(my1, "y", 1)
    t1, t3, t2 = swap(my1, "c", 1), swap(my3, "c", 1), swap(my2, "c", 1)
    back = held(tile, *back)

    ktile, part, *kback = tile_call(
        coarse_tile_kernel, k_rows, k_cols, 24, [ANY] * 11 + [VMEM], [pltpu.VMEM((8, k_cols), F32)], "coarse_tile"
    )(means, mx1, mx2, mx3, my1, my2, my3, t0, t1, t2, t3, plog)
    kback = held(ktile, *kback)
    kspecs = [VMEM, VMEM, IN_HBM, IN_HBM]
    mine = call(
        lambda *r: fold_y_kernel({"lse": [(0, 2)], "plog": (16, 16)}, *r),
        sds((24, 128)),
        [VMEM] * 4,
        name="fold_y1",
    )(*spread_over(part, "y"))
    other = swap(mine, "c", 1)

    part, plog_rows = call(
        coarse2_kernel,
        [sds((32, 128)), sds((16, 128))],
        [VMEM] * 5 + kspecs,
        scratch=[pltpu.VMEM((k_rows, 128), F32), *bufs],
        name="coarse2",
    )(mine, other, upart, plog, seat, *kback)

    part, plog_cols, seats = call(
        step3_kernel,
        [sds((40, 128)), sds((8, 128)), sds((12, 128))],
        [VMEM, VMEM] + [VMEM] * 4 + kspecs * 2,
        scratch=[wide, pltpu.VMEM((8, k_cols), F32), *bufs],
        name="step3",
    )(logs, live_cols, *spread_over(part, "x"), *kback, *back)
    mine = call(
        lambda *r: fold_y_kernel({"lse": [(0, 2), (16, 3)], "plog": None}, *r),
        sds((40, 128)),
        [VMEM] * 4,
        name="fold_y2",
    )(*spread_over(part, "y"))
    other = swap(mine, "c", 1)

    part = call(
        step4_kernel,
        sds((24, 128)),
        [VMEM, VMEM] + [VMEM] * 3 + kspecs * 2,
        scratch=[tall, pltpu.VMEM((k_rows, 128), F32), *bufs],
        name="step4",
    )(logs, live_rows, mine, other, plog_rows, *kback, *back)

    part, coarse = call(
        step5_kernel,
        [sds((24, 128)), sds((1, 128))],
        [VMEM, VMEM] + [VMEM] * 6 + kspecs,
        scratch=[pltpu.VMEM((k_cols, 128), F32), wide, *bufs],
        name="step5",
    )(logs, live_cols, *spread_over(part, "x"), plog_cols, seats, *back)
    mine = call(
        lambda *r: fold_y_kernel({"lse": [(0, 3)], "plog": None}, *r),
        sds((24, 128)),
        [VMEM] * 4,
        name="fold_y3",
    )(*spread_over(part, "y"))
    other = swap(mine, "c", 1)

    part, col = call(
        step6_kernel,
        [sds((16, 128)), sds((3, 128))],
        [VMEM, VMEM] + [VMEM] * 2 + kspecs,
        scratch=[tall, *bufs],
        name="step6",
    )(logs, live_rows, mine, other, *back)
    row = call(last_kernel, sds((3, 128)), [VMEM, VMEM] + [VMEM] * 4, name="last")(
        logs, live_cols, *spread_over(part, "x")
    )
    return row.reshape(rows), col.reshape(rows), coarse[0, :quarter]


def solution(mesh):
    split = Mesh(mesh.devices.reshape(Z, X, Y, 2), ("z", "x", "y", "c"))
    every = P(("z", "x", "y", "c"))
    return jax.shard_map(
        local,
        mesh=split,
        in_specs=(P(("z", "x", "y", "c"), None), every, P()),
        out_specs=(every, every, every),
        check_vma=False,
    )
```

```python
import math

import jax
import jax.numpy as jnp
from jax import lax
from jax.experimental import pallas as pl
from jax.experimental.pallas import tpu as pltpu
from jax.sharding import Mesh, PartitionSpec as P


PROTO_BLOCK = 256
EPS = 0.01
SC = math.log2(math.e) / EPS
NEG = -1e30
LOW, HIGH, PEAK = 2.0 ** -25, 2.0 ** 120, 2.0 ** 64
STEP = 256
F32 = jnp.float32
BF16 = jnp.bfloat16
MIB = 2 ** 20
X, Y, Z = 4, 4, 4
PAD = 128

VMEM = pl.BlockSpec(memory_space=pltpu.VMEM)
SMEM = pl.BlockSpec(memory_space=pltpu.SMEM)
ANY = pl.BlockSpec(memory_space=pl.ANY)


HBM = pltpu.MemorySpace.HBM
IN_HBM = pl.BlockSpec(memory_space=HBM)


def call(body, out_shape, in_specs, scratch=(), out_specs=None, limit=6, name=None, flops=0, nbytes=0):
    return pl.pallas_call(
        body,
        out_shape=out_shape,
        in_specs=in_specs,
        out_specs=out_specs or jax.tree.map(lambda _: VMEM, out_shape),
        scratch_shapes=list(scratch),
        compiler_params=pltpu.CompilerParams(vmem_limit_bytes=limit * MIB),
        cost_estimate=pl.CostEstimate(flops=flops, bytes_accessed=nbytes, transcendentals=0),
        name=name,
    )


def sds(shape, dtype=F32):
    return jax.ShapeDtypeStruct(shape, dtype)


def iota(shape, dim):
    return lax.broadcasted_iota(jnp.int32, shape, dim)


def to_lanes(col):
    n = col.shape[0]
    eye = iota((128, 128), 0) == iota((128, 128), 1)
    return jnp.concatenate(
        [
            jnp.sum(jnp.where(eye, col[k * 128:(k + 1) * 128], 0.0), axis=0, keepdims=True)
            for k in range(n // 128)
        ],
        axis=0,
    )


def to_rows(vals, out_ref):
    for k in range(vals.shape[0]):
        out_ref[k * 128:(k + 1) * 128, :] = jnp.transpose(
            jnp.broadcast_to(vals[k:k + 1, :], (128, 128))
        )


def lse2(parts):
    top = parts[0]
    for p in parts[1:]:
        top = jnp.maximum(top, p)
    total = jnp.exp2(parts[0] - top)
    for p in parts[1:]:
        total = total + jnp.exp2(p - top)
    return top + jnp.log2(total)


def in_range(total, peak):
    outside = jnp.sum(jnp.where((total > LOW) & (total < HIGH), 0.0, 1.0))
    return (outside == 0.0) & (peak <= PEAK)


def spread(vals, wide_ref):
    for k in range(vals.shape[0]):
        wide_ref[:, k * 128:(k + 1) * 128] = jnp.broadcast_to(vals[k:k + 1, :], (8, 128))


def store_lse(total, shift, peak, out_ref, safe):
    n = total.shape[0]
    good = in_range(total, peak)

    @pl.when(good)
    def _():
        out_ref[0:n, :] = jnp.log2(total) + shift

    @pl.when(jnp.logical_not(good))
    def _():
        safe()


def reduce_columns(tile, h, guard, out_ref, wide_ref, backup, live=None):
    rows, cols = tile.shape
    shift = jnp.max(h)
    spread(jnp.exp2(h - shift), wide_ref)
    lane, sub = iota((8, 128), 1), iota((8, 128), 0)

    def body(r, _):
        acc = jnp.zeros((8, 128), F32)
        for g in range(16):
            s = tile[pl.ds(pl.multiple_of(r * 128 + g * 8, 8), 8), :] * wide_ref[...]
            part = jnp.sum(s, axis=1, keepdims=True)
            acc = acc + jnp.where(lane == sub + 8 * g, part, 0.0)
        out_ref[pl.ds(r, 1), :] = jnp.sum(acc, axis=0, keepdims=True)
        return 0

    lax.fori_loop(0, rows // 128, body, 0, unroll=4)
    total = out_ref[0:rows // 128, :]
    if live is not None:
        total = jnp.where(live[...] > 0.0, total, 1.0)
    store_lse(total, shift, jnp.max(guard[...]), out_ref, lambda: safe_columns(backup, h, out_ref, wide_ref))


def reduce_rows(tile, h, guard, out_ref, tall_ref, backup):
    rows, cols = tile.shape
    shift = jnp.max(h)
    to_rows(jnp.exp2(h - shift), tall_ref)
    width, chunk = 512, 64
    groups = width // 128
    for strip in range(cols // width):
        at = pl.ds(strip * width, width)

        def body(c, acc):
            part = pl.ds(pl.multiple_of(c * chunk, chunk), chunk)
            s = tile[part, at] * jnp.concatenate([tall_ref[part, :]] * groups, axis=1)
            return acc + jnp.sum(s.reshape(chunk // 8, 8, width), axis=0)

        acc = lax.fori_loop(0, rows // chunk, body, jnp.zeros((8, width), F32), unroll=2)
        acc = jnp.sum(acc, axis=0, keepdims=True)
        for k in range(groups):
            row = strip * groups + k
            out_ref[row:row + 1, :] = acc[:, k * 128:(k + 1) * 128]
    store_lse(
        out_ref[0:cols // 128, :], shift, jnp.max(guard[...]), out_ref,
        lambda: safe_rows(backup, h, out_ref, tall_ref),
    )


def block_scores(backup, ci, cj):
    rows_hbm, cols_hbm, own, a_buf, b_buf, sem = backup
    for src, at, buf in ((rows_hbm, ci, a_buf), (cols_hbm, cj, b_buf)):
        copy = pltpu.make_async_copy(src.at[pl.ds(pl.multiple_of(at * STEP, STEP), STEP)], buf, sem)
        copy.start()
        copy.wait()
    s = dot_t(a_buf[...], b_buf[...])
    i, j = iota((STEP, STEP), 0) + ci * STEP, iota((STEP, STEP), 1) + cj * STEP
    return jnp.where((i == j) & (j < own), NEG, s)


def safe_columns(backup, h, out_ref, wide_ref):
    n, m = backup[0].shape[0] // STEP, backup[1].shape[0] // STEP
    spread(h, wide_ref)

    def by_rows(ci, _):
        def by_cols(cj, carry):
            top, total = carry
            s = block_scores(backup, ci, cj)
            s = s + wide_ref[0:1, pl.ds(pl.multiple_of(cj * STEP, STEP), STEP)]
            now = jnp.maximum(top, jnp.max(s, axis=1, keepdims=True))
            return now, total * jnp.exp2(top - now) + jnp.sum(jnp.exp2(s - now), axis=1, keepdims=True)

        top, total = lax.fori_loop(
            0, m, by_cols, (jnp.full((STEP, 1), NEG, F32), jnp.zeros((STEP, 1), F32))
        )
        lanes = to_lanes(jnp.broadcast_to(top + jnp.log2(total), (STEP, 128)))
        for k in range(STEP // 128):
            out_ref[pl.ds(ci * (STEP // 128) + k, 1), :] = lanes[k:k + 1, :]
        return 0

    lax.fori_loop(0, n, by_rows, 0)


def safe_rows(backup, h, out_ref, tall_ref):
    n, m = backup[0].shape[0] // STEP, backup[1].shape[0] // STEP
    to_rows(h, tall_ref)

    def by_cols(cj, _):
        def by_rows(ci, carry):
            top, total = carry
            add = tall_ref[pl.ds(pl.multiple_of(ci * STEP, STEP), STEP), :]
            s = block_scores(backup, ci, cj) + jnp.concatenate([add] * (STEP // 128), axis=1)
            now = jnp.maximum(top, jnp.max(s, axis=0, keepdims=True))
            return now, total * jnp.exp2(top - now) + jnp.sum(jnp.exp2(s - now), axis=0, keepdims=True)

        top, total = lax.fori_loop(
            0, n, by_rows, (jnp.full((1, STEP), NEG, F32), jnp.zeros((1, STEP), F32))
        )
        lse = top + jnp.log2(total)
        for k in range(STEP // 128):
            out_ref[pl.ds(cj * (STEP // 128) + k, 1), :] = lse[:, k * 128:(k + 1) * 128]
        return 0

    lax.fori_loop(0, m, by_cols, 0)


def info_place(info):
    return info[Z, 0], info[Z, 1], info[Z, 2], info[Z, 3]


def count_at(counts, z, x, y, c):
    return counts[z, (x * Y + y) * 2 + c]


def behind(at, c, k, n):
    return lax.rem(at + jnp.where(c == 0, n - k, k), n)


def row_counts(counts, idx):
    z, x, y, c = idx
    return [
        count_at(counts, z, x, behind(y, (c + dc) % 2, k, Y), (c + dc) % 2) for dc in range(2) for k in range(Y)
    ]


def col_counts(counts, idx):
    z, x, y, c = idx
    return [count_at(counts, z, behind(x, c, k, X), y, c) for k in range(X)]


def live_mask(block_counts, per):
    at = iota((per, 128), 0) * 128 + iota((per, 128), 1)
    return jnp.concatenate([jnp.where(at < n, 1.0, 0.0) for n in block_counts], axis=0)


def log2_of(n):
    return jnp.log2(jnp.full((1, 128), n, jnp.int32).astype(F32))


def from_columns(parts, first, per):
    blocks = []
    for j in range(X):
        rows = [first + (j - k) % X * per for k in range(X)]
        blocks.append(lse2([p[r:r + per, :] for p, r in zip(parts, rows)]))
    return jnp.concatenate(blocks, axis=0)


def gather_columns(parts, first, per):
    return jnp.concatenate([p[first:first + per, :] for p in parts], axis=0)


def fold_y(parts, first, per):
    blocks = []
    for dc in range(2):
        for j in range(Y):
            rows = [first + (dc * Y + (j - k if dc == 0 else j + k) % Y) * per for k in range(Y)]
            blocks.append(lse2([p[r:r + per, :] for p, r in zip(parts, rows)]))
    return jnp.concatenate(blocks, axis=0)


def fold_core(mine, other, first, per):
    half = Y * per
    return jnp.concatenate(
        [
            lse2([mine[first:first + half, :], other[first + half:first + 2 * half, :]]),
            lse2([mine[first + half:first + 2 * half, :], other[first:first + half, :]]),
        ],
        axis=0,
    )


def pool_kernel(info, emb, members, keep, send, live_rows, live_cols, seat, logs):
    idx = info_place(info)
    z, x, y, c = idx
    quarter = PROTO_BLOCK // Z
    per = members.shape[0]
    ids = members[...]
    which = lax.shift_right_logical(ids, 11)
    within = jnp.bitwise_and(ids, quarter - 1)
    turn = jnp.bitwise_xor(which, z)
    seat[...] = (turn * quarter + within).astype(F32)
    slot = jnp.where(turn == 0, 0, jnp.where(turn == 3, 1, turn + 1)) * quarter + within
    local = jnp.concatenate([slot[k:k + 1, :] for k in range(per)], axis=1)
    rows, d = emb.shape
    live = iota((1, rows), 1) < count_at(info, z, x, y, c)
    hot = ((iota((PROTO_BLOCK, rows), 0) == local) & live).astype(BF16)
    sums = jnp.dot(hot, emb[...], preferred_element_type=F32)
    sizes = jnp.dot(hot, jnp.ones((rows, PAD), BF16), preferred_element_type=F32)
    half = 2 * quarter
    keep[:, 0:d] = sums[0:half]
    keep[:, d:] = sizes[0:half]
    send[:, 0:d] = sums[half:]
    send[:, d:] = sizes[half:]
    live_rows[...] = live_mask(row_counts(info, idx), per)
    live_cols[...] = live_mask(col_counts(info, idx), per)
    mine, total = 0, 0
    for g in range(Z):
        n = info[g, 0]
        for s in range(1, X * Y * 2):
            n = n + info[g, s]
        mine = mine + jnp.where(g == z, n, 0)
        total = total + n
    logs[...] = jnp.concatenate([log2_of(mine), log2_of(total), jnp.zeros((6, 128), F32)], axis=0)


def code_sizes(sizes):
    high = jnp.floor(sizes * (1.0 / 256.0))
    low = sizes - 256.0 * high
    return jnp.where(iota(sizes.shape, 1) < 64, high, low).astype(BF16)


def read_sizes(block, d):
    coded = block[:, d:].astype(F32)
    return coded[:, 0:1] * 256.0 + coded[:, 64:65]


def pool2_kernel(mine, got, keep, send):
    quarter = mine.shape[0] // 2
    keep[...] = mine[0:quarter, :] + got[0:quarter, :]
    send[...] = mine[quarter:, :] + got[quarter:, :]


def means_kernel(mine, got, out):
    d = mine.shape[1] - PAD
    sums = mine[...] + got[...]
    sizes = sums[:, d:]
    out[:, 0:d] = (sums[:, 0:d] / sizes[:, 0:1]).astype(BF16)
    out[:, d:] = code_sizes(sizes)


def join_kernel(logs, p0, p1, p2, p3, means, plog):
    quarter, width = p0.shape
    d = width - PAD
    sizes = []
    for k, ref in enumerate((p0, p1, p2, p3)):
        block = ref[...]
        means[k * quarter:(k + 1) * quarter, :] = block[:, 0:d]
        sizes.append(jnp.broadcast_to(read_sizes(block, d), (quarter, 128)))
    plog[...] = jnp.zeros(plog.shape, F32)
    plog[0:2, :] = jnp.log2(to_lanes(jnp.concatenate(sizes, axis=0))) - logs[1:2, :]


def fetch(row_blocks, col_blocks, rows_buf, cols_buf, row_sems, col_sems):
    size = row_blocks[0].shape[0]

    def start(blocks, buf, sems, b):
        pltpu.make_async_copy(blocks[b], buf.at[pl.ds(b * size, size)], sems.at[b]).start()

    for b in range(X):
        start(col_blocks, cols_buf, col_sems, b)
    for b in range(2 * Y):
        start(row_blocks, rows_buf, row_sems, b)

    def wait(buf, sems, b):
        into = buf.at[pl.ds(pl.multiple_of(b * size, size), size)]
        pltpu.make_async_copy(into, into, sems.at[b]).wait()

    return lambda b: wait(rows_buf, row_sems, b), lambda b: wait(cols_buf, col_sems, b)


def dot_t(a, b):
    return lax.dot_general(a, b, (((1,), (1,)), ((), ())), preferred_element_type=F32) * SC


def fill_tile(tile, size, waits, rows_buf, cols_buf, rows_out, cols_out, out_sems, acc, live, sums):
    rows, cols = tile.shape
    wait_rows, wait_cols = waits
    step, wide = 2 * size, 512
    for b in range(X):
        wait_cols(b)
    save_cols = pltpu.make_async_copy(cols_buf, cols_out, out_sems.at[1])
    save_cols.start()
    if acc is not None:
        acc[...] = jnp.zeros(acc.shape, F32)

    def body(i, _):
        at = pl.ds(pl.multiple_of(i * step, step), step)
        wait_rows(2 * i)
        wait_rows(2 * i + 1)
        pltpu.make_async_copy(rows_buf.at[at], rows_out.at[at], out_sems.at[0]).start()
        for j in range(cols // wide):
            across = pl.ds(j * wide, wide)
            s = dot_t(rows_buf[at, :], cols_buf[across, :])
            if j == 0:
                col = iota((step, wide), 1)
                s = jnp.where((iota((step, wide), 0) + i * step == col) & (col < size), NEG, s)
            s = jnp.exp2(s)
            if live is not None:
                s = s * jnp.concatenate([live[at, :]] * (wide // 128), axis=1)
            tile[at, across] = s
            if acc is not None:
                acc[:, across] += jnp.sum(s.reshape(step // 8, 8, wide), axis=0)
            if sums is not None:
                part = s[:, 0:128]
                for k in range(1, wide // 128):
                    part = part + s[:, k * 128:(k + 1) * 128]
                sums[at, :] = part if j == 0 else sums[at, :] + part
        return 0

    lax.fori_loop(0, rows // step, body, 0)
    pltpu.make_async_copy(rows_buf, rows_out, out_sems.at[0]).wait()
    save_cols.wait()


def coarse_tile_kernel(own, x1, x2, x3, y1, y2, y3, s0, s1, s2, s3, plog, tile, payload, peak, rows_out, cols_out,
                       rows_buf, cols_buf, row_sems, col_sems, out_sems, sums, wide, a_buf, b_buf, sem):
    n = own.shape[0]
    waits = fetch(
        [own, y1, y2, y3, s0, s1, s2, s3], [own, x1, x2, x3], rows_buf, cols_buf, row_sems, col_sems
    )
    fill_tile(tile, n, waits, rows_buf, cols_buf, rows_out, cols_out, out_sems, None, None, sums)
    rows, cols = tile.shape
    payload[...] = jnp.zeros(payload.shape, F32)
    lane, sub = iota((8, 128), 1), iota((8, 128), 0)

    def body(r, _):
        acc = jnp.zeros((8, 128), F32)
        for g in range(16):
            s = sums[pl.ds(pl.multiple_of(r * 128 + g * 8, 8), 8), :]
            acc = acc + jnp.where(lane == sub + 8 * g, jnp.sum(s, axis=1, keepdims=True), 0.0)
        payload[pl.ds(r, 1), :] = jnp.sum(acc, axis=0, keepdims=True)
        return 0

    lax.fori_loop(0, rows // 128, body, 0, unroll=4)
    total = payload[0:rows // 128, :]
    most = jnp.max(total)
    peak[...] = jnp.full(peak.shape, most, F32)
    store_lse(
        total, 0.0, most, payload,
        lambda: safe_columns(
            (rows_out, cols_out, n, a_buf, b_buf, sem), jnp.zeros((cols // 128, 128), F32), payload, wide
        ),
    )
    payload[rows // 128:rows // 128 + 2, :] = plog[0:2, :]


def fine_tile_kernel(info, live_rows, own, x1, x2, x3, y1, y2, y3, s0, s1, s2, s3, tile, part, peak, rows_out,
                     cols_out, rows_buf, cols_buf, row_sems, col_sems, out_sems, tall, acc, a_buf, b_buf, sem):
    n = own.shape[0]
    waits = fetch(
        [own, y1, y2, y3, s0, s1, s2, s3], [own, x1, x2, x3], rows_buf, cols_buf, row_sems, col_sems
    )
    for b, count in enumerate(row_counts(info, info_place(info))):
        tall[b * n:(b + 1) * n, :] = jnp.where(iota((n, 128), 0) < count, 1.0, 0.0)
    fill_tile(tile, n, waits, rows_buf, cols_buf, rows_out, cols_out, out_sems, acc, tall, None)
    rows, cols = tile.shape
    total = jnp.sum(acc[...], axis=0, keepdims=True)
    for k in range(cols // 128):
        part[k:k + 1, :] = total[:, k * 128:(k + 1) * 128]
    h = jnp.where(live_rows[...] > 0.0, 0.0, NEG)
    most = jnp.max(total)
    peak[...] = jnp.full(peak.shape, most, F32)
    store_lse(
        part[...], 0.0, most, part,
        lambda: safe_rows((rows_out, cols_out, n, a_buf, b_buf, sem), h, part, tall),
    )


def fold_y_kernel(plan, *refs):
    parts, out = refs[0:Y], refs[Y]
    out[...] = jnp.zeros(out.shape, F32)
    for first, per in plan["lse"]:
        n = 2 * Y * per
        out[first:first + n, :] = fold_y(parts, first, per)
    if plan["plog"] is not None:
        first, into = plan["plog"]
        out[into:into + 2 * Y, :] = jnp.concatenate(
            [p[first:first + 2, :] for p in parts], axis=0
        )


def coarse2_kernel(mine, other, part, plog, seat, tile, peak, rows_hbm, cols_hbm, payload, plog_rows, tall, *bufs):
    plog_rows[0:8, :] = mine[16:24, :]
    plog_rows[8:16, :] = other[16:24, :]
    h = plog_rows[...] + SC - fold_core(mine, other, 0, 2)
    payload[...] = jnp.zeros(payload.shape, F32)
    reduce_rows(tile, h, peak, payload, tall, (rows_hbm, cols_hbm, PROTO_BLOCK, *bufs))
    payload[8:20, :] = part[...]
    payload[20:22, :] = plog[0:2, :]
    payload[22:25, :] = seat[...]


def fine_h(lse, logs, live, boost=0.0):
    return jnp.where(live[...] > 0.0, SC - logs[0:1, :] - lse + boost, NEG)


def step3_kernel(logs, live_rows, live_cols, p0, p1, p2, p3, ktile, kpeak, krows, kcols, tile, peak, rows_hbm, cols_hbm,
                 payload, plog_cols, seats, wide, kwide, *bufs):
    parts = (p0, p1, p2, p3)
    plog_cols[...] = gather_columns(parts, 20, 2)
    seats[...] = gather_columns(parts, 22, 3)
    payload[...] = jnp.zeros(payload.shape, F32)
    h = fine_h(from_columns(parts, 8, 3), logs, live_cols)
    backup = (rows_hbm, cols_hbm, tile.shape[1] // X, *bufs)
    reduce_columns(tile, h, peak, payload.at[16:40, :], wide, backup, live_rows)
    h = plog_cols[...] + SC - from_columns(parts, 0, 2)
    reduce_columns(ktile, h, kpeak, payload.at[0:16, :], kwide, (krows, kcols, PROTO_BLOCK, *bufs))


def step4_kernel(logs, live_rows, mine, other, plog_rows, ktile, kpeak, krows, kcols, tile, peak, rows_hbm, cols_hbm,
                 payload, tall, ktall, *bufs):
    payload[...] = jnp.zeros(payload.shape, F32)
    h = plog_rows[...] + SC - fold_core(mine, other, 0, 2)
    reduce_rows(ktile, h, kpeak, payload.at[0:8, :], ktall, (krows, kcols, PROTO_BLOCK, *bufs))
    h = fine_h(fold_core(mine, other, 16, 3), logs, live_rows)
    backup = (rows_hbm, cols_hbm, tile.shape[1] // X, *bufs)
    reduce_rows(tile, h, peak, payload.at[8:20, :], tall, backup)


def step5_kernel(logs, live_rows, live_cols, p0, p1, p2, p3, plog_cols, seats, tile, peak, rows_hbm, cols_hbm,
                 payload, coarse, tall, wide, *bufs):
    parts = (p0, p1, p2, p3)
    v = plog_cols[...] + SC - from_columns(parts, 0, 2)
    coarse[...] = v[0:1, :] * (1.0 / SC)
    to_rows(v, tall)
    local = seats[...].astype(jnp.int32)
    boost = []
    for k in range(X * 3):
        vals = tall[(k // 3) * PROTO_BLOCK:(k // 3 + 1) * PROTO_BLOCK, :]
        pick = iota((PROTO_BLOCK, 128), 0) == local[k:k + 1, :]
        boost.append(jnp.sum(jnp.where(pick, vals, 0.0), axis=0, keepdims=True))
    h = fine_h(from_columns(parts, 8, 3), logs, live_cols, jnp.concatenate(boost, axis=0))
    payload[...] = jnp.zeros(payload.shape, F32)
    reduce_columns(tile, h, peak, payload, wide, (rows_hbm, cols_hbm, tile.shape[1] // X, *bufs), live_rows)


def potential(h):
    return jnp.where(h == NEG, 0.0, h)[0:3, :] * (1.0 / SC)


def step6_kernel(logs, live_rows, mine, other, tile, peak, rows_hbm, cols_hbm, payload, out, tall, *bufs):
    h = fine_h(fold_core(mine, other, 0, 3), logs, live_rows)
    out[...] = potential(h)
    payload[...] = jnp.zeros(payload.shape, F32)
    backup = (rows_hbm, cols_hbm, tile.shape[1] // X, *bufs)
    reduce_rows(tile, h, peak, payload, tall, backup)


def last_kernel(logs, live_cols, p0, p1, p2, p3, out):
    out[...] = potential(fine_h(from_columns((p0, p1, p2, p3), 0, 3), logs, live_cols))


def swap(v, axis, bit):
    n = {"z": Z, "c": 2}[axis]
    return lax.ppermute(v, axis, [(i, i ^ bit) for i in range(n)])


def turn(v, axis, k):
    n = {"x": X, "y": Y}[axis]
    return lax.ppermute(
        v, (axis, "c"), [(i * 2 + c, (i + (k if c == 0 else n - k)) % n * 2 + c) for i in range(n) for c in range(2)]
    )


def spread_over(v, axis):
    return [v] + [turn(v, axis, k) for k in (1, 2, 3)]


def vmem(v):
    return pltpu.with_memory_space_constraint(v, pltpu.VMEM)


def held(tile, peak, rows, cols):
    return [vmem(tile), peak, *[pltpu.with_memory_space_constraint(v, HBM) for v in (rows, cols)]]


def local(embeddings, members, counts):
    rows, d = embeddings.shape
    here = jnp.stack([lax.axis_index(a) for a in ("z", "x", "y", "c")]).astype(jnp.int32)
    info = jnp.concatenate([counts, jnp.pad(here[None], ((0, 0), (0, counts.shape[1] - 4)))], axis=0)
    per = rows // 128
    n_rows, n_cols = rows * Y * 2, rows * X
    k_rows, k_cols = PROTO_BLOCK * Y * 2, PROTO_BLOCK * X
    quarter = PROTO_BLOCK // Z
    width = d + PAD

    def first(own):
        return turn(own, "x", 1), turn(own, "x", 3), turn(own, "y", 1), turn(own, "y", 3)

    x1, x3, y1, y3 = first(embeddings)
    keep, send, live_rows, live_cols, seat, logs = call(
        pool_kernel,
        [
            sds((2 * quarter, width)), sds((2 * quarter, width)), sds((n_rows // 128, 128)),
            sds((n_cols // 128, 128)), sds((per, 128)), sds((8, 128)),
        ],
        [SMEM, VMEM, VMEM],
        name="pool",
    )(info, embeddings, members.reshape(per, 128))
    keep, send = call(
        pool2_kernel, [sds((quarter, width)), sds((quarter, width))], [VMEM] * 2, name="pool2"
    )(keep, swap(send, "z", 1))
    got = swap(send, "z", 3)
    x1, x3, y1, y3, got = lax.optimization_barrier((x1, x3, y1, y3, got))
    x2, y2 = turn(x1, "x", 1), turn(y1, "y", 1)
    part = call(means_kernel, sds((quarter, width), BF16), [VMEM] * 2, name="means")(keep, got)
    far = [swap(part, "z", k) for k in (1, 2, 3)]
    x1, y1, y3, x2, y2, embeddings, far = lax.optimization_barrier((x1, y1, y3, x2, y2, embeddings, far))
    means, plog = call(
        join_kernel, [sds((PROTO_BLOCK, d), BF16), sds((8, 128))], [VMEM] * 5, name="join"
    )(logs, part, *far)
    s0, s1, s2, s3 = [swap(v, "c", 1) for v in (embeddings, y1, y2, y3)]
    vectors = [embeddings, x1, x2, x3, y1, y2, y3, s0, s1, s2, s3]

    bufs = [pltpu.VMEM((STEP, d), BF16), pltpu.VMEM((STEP, d), BF16), pltpu.SemaphoreType.DMA]

    def tile_call(body, n, m, part_rows, specs, extra, name):
        out = [pltpu.VMEM((n, m), F32), sds((part_rows, 128)), sds((8, 128)), HBM((n, d), BF16), HBM((m, d), BF16)]
        return call(
            body,
            out,
            specs,
            scratch=[
                pltpu.VMEM((n, d), BF16),
                pltpu.VMEM((m, d), BF16),
                pltpu.SemaphoreType.DMA((2 * Y,)),
                pltpu.SemaphoreType.DMA((X,)),
                pltpu.SemaphoreType.DMA((2,)),
                *extra,
                *bufs,
            ],
            out_specs=[VMEM, VMEM, VMEM, IN_HBM, IN_HBM],
            limit=18,
            name=name,
            flops=2 * n * m * d,
        )

    tall = pltpu.VMEM((n_rows, 128), F32)
    wide = pltpu.VMEM((8, n_cols), F32)
    mx1, mx3, my1, my3 = first(means)
    tile, upart, *back = tile_call(
        fine_tile_kernel, n_rows, n_cols, n_cols // 128, [SMEM, VMEM] + [ANY] * 11, [tall, wide], "fine_tile"
    )(info, live_rows, *vectors)
    upart, means, mx1, mx3, my1, my3 = lax.optimization_barrier((upart, means, mx1, mx3, my1, my3))
    mx2, my2 = turn(mx1, "x", 1), turn(my1, "y", 1)
    t0, t1, t3, t2 = swap(means, "c", 1), swap(my1, "c", 1), swap(my3, "c", 1), swap(my2, "c", 1)
    back = held(tile, *back)

    ktile, part, *kback = tile_call(
        coarse_tile_kernel, k_rows, k_cols, 24, [ANY] * 11 + [VMEM],
        [pltpu.VMEM((k_rows, 128), F32), pltpu.VMEM((8, k_cols), F32)], "coarse_tile"
    )(means, mx1, mx2, mx3, my1, my2, my3, t0, t1, t2, t3, plog)
    kback = held(ktile, *kback)
    kspecs = [VMEM, VMEM, IN_HBM, IN_HBM]
    mine = call(
        lambda *r: fold_y_kernel({"lse": [(0, 2)], "plog": (16, 16)}, *r),
        sds((24, 128)),
        [VMEM] * 4,
        name="fold_y1",
    )(*spread_over(part, "y"))
    other = swap(mine, "c", 1)

    part, plog_rows = call(
        coarse2_kernel,
        [sds((32, 128)), sds((16, 128))],
        [VMEM] * 5 + kspecs,
        scratch=[pltpu.VMEM((k_rows, 128), F32), *bufs],
        name="coarse2",
    )(mine, other, upart, plog, seat, *kback)

    part, plog_cols, seats = call(
        step3_kernel,
        [sds((40, 128)), sds((8, 128)), sds((12, 128))],
        [VMEM] * 7 + kspecs * 2,
        scratch=[wide, pltpu.VMEM((8, k_cols), F32), *bufs],
        name="step3",
    )(logs, live_rows, live_cols, *spread_over(part, "x"), *kback, *back)
    mine = call(
        lambda *r: fold_y_kernel({"lse": [(0, 2), (16, 3)], "plog": None}, *r),
        sds((40, 128)),
        [VMEM] * 4,
        name="fold_y2",
    )(*spread_over(part, "y"))
    other = swap(mine, "c", 1)

    part = call(
        step4_kernel,
        sds((24, 128)),
        [VMEM, VMEM] + [VMEM] * 3 + kspecs * 2,
        scratch=[tall, pltpu.VMEM((k_rows, 128), F32), *bufs],
        name="step4",
    )(logs, live_rows, mine, other, plog_rows, *kback, *back)

    part, coarse = call(
        step5_kernel,
        [sds((24, 128)), sds((1, 128))],
        [VMEM] * 9 + kspecs,
        scratch=[pltpu.VMEM((k_cols, 128), F32), wide, *bufs],
        name="step5",
    )(logs, live_rows, live_cols, *spread_over(part, "x"), plog_cols, seats, *back)
    mine = call(
        lambda *r: fold_y_kernel({"lse": [(0, 3)], "plog": None}, *r),
        sds((24, 128)),
        [VMEM] * 4,
        name="fold_y3",
    )(*spread_over(part, "y"))
    other = swap(mine, "c", 1)

    part, col = call(
        step6_kernel,
        [sds((16, 128)), sds((3, 128))],
        [VMEM, VMEM] + [VMEM] * 2 + kspecs,
        scratch=[tall, *bufs],
        name="step6",
    )(logs, live_rows, mine, other, *back)
    row = call(last_kernel, sds((3, 128)), [VMEM, VMEM] + [VMEM] * 4, name="last")(
        logs, live_cols, *spread_over(part, "x")
    )
    return row.reshape(rows), col.reshape(rows), coarse[0, :quarter]


def solution(mesh):
    split = Mesh(mesh.devices.reshape(Z, X, Y, 2), ("z", "x", "y", "c"))
    every = P(("z", "x", "y", "c"))
    return jax.shard_map(
        local,
        mesh=split,
        in_specs=(P(("z", "x", "y", "c"), None), every, P()),
        out_specs=(every, every, every),
        check_vma=False,
    )
```

```python
import math

import jax
import jax.numpy as jnp
from jax import lax
from jax.experimental import pallas as pl
from jax.experimental.pallas import tpu as pltpu
from jax.sharding import Mesh, PartitionSpec as P


PROTO_BLOCK = 256
EPS = 0.01
SC = math.log2(math.e) / EPS
NEG = -1e30
LOW, HIGH, PEAK = 2.0 ** -25, 2.0 ** 120, 2.0 ** 64
STEP = 256
F32 = jnp.float32
BF16 = jnp.bfloat16
MIB = 2 ** 20
X, Y, Z = 4, 4, 4
PAD = 128

VMEM = pl.BlockSpec(memory_space=pltpu.VMEM)
SMEM = pl.BlockSpec(memory_space=pltpu.SMEM)
ANY = pl.BlockSpec(memory_space=pl.ANY)


HBM = pltpu.MemorySpace.HBM
IN_HBM = pl.BlockSpec(memory_space=HBM)


def call(body, out_shape, in_specs, scratch=(), out_specs=None, limit=6, name=None, flops=0, nbytes=0):
    return pl.pallas_call(
        body,
        out_shape=out_shape,
        in_specs=in_specs,
        out_specs=out_specs or jax.tree.map(lambda _: VMEM, out_shape),
        scratch_shapes=list(scratch),
        compiler_params=pltpu.CompilerParams(vmem_limit_bytes=limit * MIB),
        cost_estimate=pl.CostEstimate(flops=flops, bytes_accessed=nbytes, transcendentals=0),
        name=name,
    )


def sds(shape, dtype=F32):
    return jax.ShapeDtypeStruct(shape, dtype)


def iota(shape, dim):
    return lax.broadcasted_iota(jnp.int32, shape, dim)


def to_lanes(col):
    n = col.shape[0]
    eye = iota((128, 128), 0) == iota((128, 128), 1)
    return jnp.concatenate(
        [
            jnp.sum(jnp.where(eye, col[k * 128:(k + 1) * 128], 0.0), axis=0, keepdims=True)
            for k in range(n // 128)
        ],
        axis=0,
    )


def to_rows(vals, out_ref):
    for k in range(vals.shape[0]):
        out_ref[k * 128:(k + 1) * 128, :] = jnp.transpose(
            jnp.broadcast_to(vals[k:k + 1, :], (128, 128))
        )


def lse2(parts):
    top = parts[0]
    for p in parts[1:]:
        top = jnp.maximum(top, p)
    total = jnp.exp2(parts[0] - top)
    for p in parts[1:]:
        total = total + jnp.exp2(p - top)
    return top + jnp.log2(total)


def in_range(total, peak):
    outside = jnp.sum(jnp.where((total > LOW) & (total < HIGH), 0.0, 1.0))
    return (outside == 0.0) & (peak <= PEAK)


def spread(vals, wide_ref):
    for k in range(vals.shape[0]):
        wide_ref[:, k * 128:(k + 1) * 128] = jnp.broadcast_to(vals[k:k + 1, :], (8, 128))


def store_lse(total, shift, peak, out_ref, safe):
    n = total.shape[0]
    good = in_range(total, peak)

    @pl.when(good)
    def _():
        out_ref[0:n, :] = jnp.log2(total) + shift

    @pl.when(jnp.logical_not(good))
    def _():
        safe()


def reduce_columns(tile, h, guard, out_ref, wide_ref, backup, live=None):
    rows, cols = tile.shape
    shift = jnp.max(h)
    spread(jnp.exp2(h - shift), wide_ref)
    lane, sub = iota((8, 128), 1), iota((8, 128), 0)

    def body(r, _):
        acc = jnp.zeros((8, 128), F32)
        for g in range(16):
            s = tile[pl.ds(pl.multiple_of(r * 128 + g * 8, 8), 8), :] * wide_ref[...]
            part = jnp.sum(s, axis=1, keepdims=True)
            acc = acc + jnp.where(lane == sub + 8 * g, part, 0.0)
        out_ref[pl.ds(r, 1), :] = jnp.sum(acc, axis=0, keepdims=True)
        return 0

    lax.fori_loop(0, rows // 128, body, 0, unroll=4)
    total = out_ref[0:rows // 128, :]
    if live is not None:
        total = jnp.where(live[...] > 0.0, total, 1.0)
    store_lse(total, shift, jnp.max(guard[...]), out_ref, lambda: safe_columns(backup, h, out_ref, wide_ref))


def reduce_rows(tile, h, guard, out_ref, tall_ref, backup):
    rows, cols = tile.shape
    shift = jnp.max(h)
    to_rows(jnp.exp2(h - shift), tall_ref)
    width, chunk = 512, 64
    groups = width // 128
    for strip in range(cols // width):
        at = pl.ds(strip * width, width)

        def body(c, acc):
            part = pl.ds(pl.multiple_of(c * chunk, chunk), chunk)
            s = tile[part, at] * jnp.concatenate([tall_ref[part, :]] * groups, axis=1)
            return acc + jnp.sum(s.reshape(chunk // 8, 8, width), axis=0)

        acc = lax.fori_loop(0, rows // chunk, body, jnp.zeros((8, width), F32), unroll=2)
        acc = jnp.sum(acc, axis=0, keepdims=True)
        for k in range(groups):
            row = strip * groups + k
            out_ref[row:row + 1, :] = acc[:, k * 128:(k + 1) * 128]
    store_lse(
        out_ref[0:cols // 128, :], shift, jnp.max(guard[...]), out_ref,
        lambda: safe_rows(backup, h, out_ref, tall_ref),
    )


def block_scores(backup, ci, cj):
    rows_hbm, cols_hbm, own, a_buf, b_buf, sem = backup
    for src, at, buf in ((rows_hbm, ci, a_buf), (cols_hbm, cj, b_buf)):
        copy = pltpu.make_async_copy(src.at[pl.ds(pl.multiple_of(at * STEP, STEP), STEP)], buf, sem)
        copy.start()
        copy.wait()
    s = dot_t(a_buf[...], b_buf[...])
    i, j = iota((STEP, STEP), 0) + ci * STEP, iota((STEP, STEP), 1) + cj * STEP
    return jnp.where((i == j) & (j < own), NEG, s)


def safe_columns(backup, h, out_ref, wide_ref):
    n, m = backup[0].shape[0] // STEP, backup[1].shape[0] // STEP
    spread(h, wide_ref)

    def by_rows(ci, _):
        def by_cols(cj, carry):
            top, total = carry
            s = block_scores(backup, ci, cj)
            s = s + wide_ref[0:1, pl.ds(pl.multiple_of(cj * STEP, STEP), STEP)]
            now = jnp.maximum(top, jnp.max(s, axis=1, keepdims=True))
            return now, total * jnp.exp2(top - now) + jnp.sum(jnp.exp2(s - now), axis=1, keepdims=True)

        top, total = lax.fori_loop(
            0, m, by_cols, (jnp.full((STEP, 1), NEG, F32), jnp.zeros((STEP, 1), F32))
        )
        lanes = to_lanes(jnp.broadcast_to(top + jnp.log2(total), (STEP, 128)))
        for k in range(STEP // 128):
            out_ref[pl.ds(ci * (STEP // 128) + k, 1), :] = lanes[k:k + 1, :]
        return 0

    lax.fori_loop(0, n, by_rows, 0)


def safe_rows(backup, h, out_ref, tall_ref):
    n, m = backup[0].shape[0] // STEP, backup[1].shape[0] // STEP
    to_rows(h, tall_ref)

    def by_cols(cj, _):
        def by_rows(ci, carry):
            top, total = carry
            add = tall_ref[pl.ds(pl.multiple_of(ci * STEP, STEP), STEP), :]
            s = block_scores(backup, ci, cj) + jnp.concatenate([add] * (STEP // 128), axis=1)
            now = jnp.maximum(top, jnp.max(s, axis=0, keepdims=True))
            return now, total * jnp.exp2(top - now) + jnp.sum(jnp.exp2(s - now), axis=0, keepdims=True)

        top, total = lax.fori_loop(
            0, n, by_rows, (jnp.full((1, STEP), NEG, F32), jnp.zeros((1, STEP), F32))
        )
        lse = top + jnp.log2(total)
        for k in range(STEP // 128):
            out_ref[pl.ds(cj * (STEP // 128) + k, 1), :] = lse[:, k * 128:(k + 1) * 128]
        return 0

    lax.fori_loop(0, m, by_cols, 0)


def info_place(info):
    return info[Z, 0], info[Z, 1], info[Z, 2], info[Z, 3]


def count_at(counts, z, x, y, c):
    return counts[z, (x * Y + y) * 2 + c]


def behind(at, c, k, n):
    return lax.rem(at + jnp.where(c == 0, n - k, k), n)


def row_counts(counts, idx):
    z, x, y, c = idx
    return [
        count_at(counts, z, x, behind(y, (c + dc) % 2, k, Y), (c + dc) % 2) for dc in range(2) for k in range(Y)
    ]


def col_counts(counts, idx):
    z, x, y, c = idx
    return [count_at(counts, z, behind(x, c, k, X), y, c) for k in range(X)]


def live_mask(block_counts, per):
    at = iota((per, 128), 0) * 128 + iota((per, 128), 1)
    return jnp.concatenate([jnp.where(at < n, 1.0, 0.0) for n in block_counts], axis=0)


def log2_of(n):
    return jnp.log2(jnp.full((1, 128), n, jnp.int32).astype(F32))


def from_columns(parts, first, per):
    blocks = []
    for j in range(X):
        rows = [first + (j - k) % X * per for k in range(X)]
        blocks.append(lse2([p[r:r + per, :] for p, r in zip(parts, rows)]))
    return jnp.concatenate(blocks, axis=0)


def gather_columns(parts, first, per):
    return jnp.concatenate([p[first:first + per, :] for p in parts], axis=0)


def fold_y(parts, first, per):
    blocks = []
    for dc in range(2):
        for j in range(Y):
            rows = [first + (dc * Y + (j - k if dc == 0 else j + k) % Y) * per for k in range(Y)]
            blocks.append(lse2([p[r:r + per, :] for p, r in zip(parts, rows)]))
    return jnp.concatenate(blocks, axis=0)


def fold_core(mine, other, first, per):
    half = Y * per
    return jnp.concatenate(
        [
            lse2([mine[first:first + half, :], other[first + half:first + 2 * half, :]]),
            lse2([mine[first + half:first + 2 * half, :], other[first:first + half, :]]),
        ],
        axis=0,
    )


def pool_kernel(info, emb, table, keep, send, live_rows, live_cols, seat, logs):
    idx = info_place(info)
    z, x, y, c = idx
    quarter = PROTO_BLOCK // Z
    per = seat.shape[0]
    ids = table[Z + 1:Z + 1 + per, :]
    which = lax.shift_right_logical(ids, 11)
    within = jnp.bitwise_and(ids, quarter - 1)
    turn = jnp.bitwise_xor(which, z)
    seat[...] = (turn * quarter + within).astype(F32)
    slot = jnp.where(turn == 0, 0, jnp.where(turn == 3, 1, turn + 1)) * quarter + within
    local = jnp.concatenate([slot[k:k + 1, :] for k in range(per)], axis=1)
    rows, d = emb.shape
    live = iota((1, rows), 1) < count_at(info, z, x, y, c)
    hot = ((iota((PROTO_BLOCK, rows), 0) == local) & live).astype(BF16)
    sums = jnp.dot(hot, emb[...], preferred_element_type=F32)
    sizes = lax.dot_general(
        jnp.ones((8, rows), BF16), hot, (((1,), (1,)), ((), ())), preferred_element_type=F32
    )
    half = 2 * quarter
    keep[0:half, :] = sums[0:half]
    keep[half:, :] = size_rows(sizes[:, 0:half], d)
    send[0:half, :] = sums[half:]
    send[half:, :] = size_rows(sizes[:, half:], d)
    live_rows[...] = live_mask(row_counts(info, idx), per)
    live_cols[...] = live_mask(col_counts(info, idx), per)
    mine, total = 0, 0
    for g in range(Z):
        n = info[g, 0]
        for s in range(1, X * Y * 2):
            n = n + info[g, s]
        mine = mine + jnp.where(g == z, n, 0)
        total = total + n
    logs[...] = jnp.concatenate([log2_of(mine), log2_of(total), jnp.zeros((6, 128), F32)], axis=0)


def size_rows(sizes, d):
    return jnp.concatenate([sizes, jnp.zeros((sizes.shape[0], d - sizes.shape[1]), F32)], axis=1)


def code_sizes(sizes):
    high = jnp.floor(sizes * (1.0 / 256.0))
    low = sizes - 256.0 * high
    return jnp.where(iota(sizes.shape, 1) < 64, high, low).astype(BF16)


def read_sizes(block, d):
    coded = block[:, d:].astype(F32)
    return coded[:, 0:1] * 256.0 + coded[:, 64:65]


def pool2_kernel(mine, got, keep, send):
    half, d = mine.shape[0] - 8, mine.shape[1]
    quarter = half // 2
    keep[0:quarter, :] = mine[0:quarter, :] + got[0:quarter, :]
    send[0:quarter, :] = mine[quarter:half, :] + got[quarter:half, :]
    sizes = mine[half:, 0:half] + got[half:, 0:half]
    keep[quarter:, :] = size_rows(sizes, d)
    send[quarter:, :] = size_rows(jnp.concatenate([sizes[:, quarter:], sizes[:, 0:quarter]], axis=1), d)


def means_kernel(mine, got, out):
    quarter, d = mine.shape[0] - 8, mine.shape[1]
    lanes = mine[quarter:, 0:128] + got[quarter:, 0:128]
    sizes = jnp.transpose(jnp.broadcast_to(lanes[0:1, :], (128, 128)))[0:quarter, :]
    out[:, 0:d] = ((mine[0:quarter, :] + got[0:quarter, :]) / sizes[:, 0:1]).astype(BF16)
    out[:, d:] = code_sizes(sizes)


def join_kernel(logs, p0, p1, p2, p3, means, plog):
    quarter, width = p0.shape
    d = width - PAD
    sizes = []
    for k, ref in enumerate((p0, p1, p2, p3)):
        block = ref[...]
        means[k * quarter:(k + 1) * quarter, :] = block[:, 0:d]
        sizes.append(jnp.broadcast_to(read_sizes(block, d), (quarter, 128)))
    plog[...] = jnp.zeros(plog.shape, F32)
    plog[0:2, :] = jnp.log2(to_lanes(jnp.concatenate(sizes, axis=0))) - logs[1:2, :]


def fetch(row_blocks, col_blocks, rows_buf, cols_buf, row_sems, col_sems):
    size = row_blocks[0].shape[0]

    def start(blocks, buf, sems, b):
        pltpu.make_async_copy(blocks[b], buf.at[pl.ds(b * size, size)], sems.at[b]).start()

    for b in range(X):
        start(col_blocks, cols_buf, col_sems, b)
    for b in range(2 * Y):
        start(row_blocks, rows_buf, row_sems, b)

    def wait(buf, sems, b):
        into = buf.at[pl.ds(pl.multiple_of(b * size, size), size)]
        pltpu.make_async_copy(into, into, sems.at[b]).wait()

    return lambda b: wait(rows_buf, row_sems, b), lambda b: wait(cols_buf, col_sems, b)


def dot_t(a, b):
    return lax.dot_general(a, b, (((1,), (1,)), ((), ())), preferred_element_type=F32) * SC


def fill_tile(tile, size, waits, rows_buf, cols_buf, rows_out, cols_out, out_sems, acc, live, sums):
    rows, cols = tile.shape
    wait_rows, wait_cols = waits
    step, wide = 2 * size, 512
    for b in range(X):
        wait_cols(b)
    save_cols = pltpu.make_async_copy(cols_buf, cols_out, out_sems.at[1])
    save_cols.start()
    if acc is not None:
        acc[...] = jnp.zeros(acc.shape, F32)

    def body(i, _):
        at = pl.ds(pl.multiple_of(i * step, step), step)
        wait_rows(2 * i)
        wait_rows(2 * i + 1)
        pltpu.make_async_copy(rows_buf.at[at], rows_out.at[at], out_sems.at[0]).start()
        for j in range(cols // wide):
            across = pl.ds(j * wide, wide)
            s = dot_t(rows_buf[at, :], cols_buf[across, :])
            if j == 0:
                col = iota((step, wide), 1)
                s = jnp.where((iota((step, wide), 0) + i * step == col) & (col < size), NEG, s)
            s = jnp.exp2(s)
            if live is not None:
                s = s * jnp.concatenate([live[at, :]] * (wide // 128), axis=1)
            tile[at, across] = s
            if acc is not None:
                acc[:, across] += jnp.sum(s.reshape(step // 8, 8, wide), axis=0)
            if sums is not None:
                part = s[:, 0:128]
                for k in range(1, wide // 128):
                    part = part + s[:, k * 128:(k + 1) * 128]
                sums[at, :] = part if j == 0 else sums[at, :] + part
        return 0

    lax.fori_loop(0, rows // step, body, 0)
    pltpu.make_async_copy(rows_buf, rows_out, out_sems.at[0]).wait()
    save_cols.wait()


def coarse_tile_kernel(own, x1, x2, x3, y1, y2, y3, s0, s1, s2, s3, plog, tile, payload, peak, rows_out, cols_out,
                       rows_buf, cols_buf, row_sems, col_sems, out_sems, sums, wide, a_buf, b_buf, sem):
    n = own.shape[0]
    waits = fetch(
        [own, y1, y2, y3, s0, s1, s2, s3], [own, x1, x2, x3], rows_buf, cols_buf, row_sems, col_sems
    )
    fill_tile(tile, n, waits, rows_buf, cols_buf, rows_out, cols_out, out_sems, None, None, sums)
    rows, cols = tile.shape
    payload[...] = jnp.zeros(payload.shape, F32)
    lane, sub = iota((8, 128), 1), iota((8, 128), 0)

    def body(r, _):
        acc = jnp.zeros((8, 128), F32)
        for g in range(16):
            s = sums[pl.ds(pl.multiple_of(r * 128 + g * 8, 8), 8), :]
            acc = acc + jnp.where(lane == sub + 8 * g, jnp.sum(s, axis=1, keepdims=True), 0.0)
        payload[pl.ds(r, 1), :] = jnp.sum(acc, axis=0, keepdims=True)
        return 0

    lax.fori_loop(0, rows // 128, body, 0, unroll=4)
    total = payload[0:rows // 128, :]
    most = jnp.max(total)
    peak[...] = jnp.full(peak.shape, most, F32)
    store_lse(
        total, 0.0, most, payload,
        lambda: safe_columns(
            (rows_out, cols_out, n, a_buf, b_buf, sem), jnp.zeros((cols // 128, 128), F32), payload, wide
        ),
    )
    payload[rows // 128:rows // 128 + 2, :] = plog[0:2, :]


def fine_tile_kernel(info, live_rows, own, x1, x2, x3, y1, y2, y3, s0, s1, s2, s3, tile, part, peak, rows_out,
                     cols_out, rows_buf, cols_buf, row_sems, col_sems, out_sems, tall, acc, a_buf, b_buf, sem):
    n = own.shape[0]
    waits = fetch(
        [own, y1, y2, y3, s0, s1, s2, s3], [own, x1, x2, x3], rows_buf, cols_buf, row_sems, col_sems
    )
    for b, count in enumerate(row_counts(info, info_place(info))):
        tall[b * n:(b + 1) * n, :] = jnp.where(iota((n, 128), 0) < count, 1.0, 0.0)
    fill_tile(tile, n, waits, rows_buf, cols_buf, rows_out, cols_out, out_sems, acc, tall, None)
    rows, cols = tile.shape
    total = jnp.sum(acc[...], axis=0, keepdims=True)
    for k in range(cols // 128):
        part[k:k + 1, :] = total[:, k * 128:(k + 1) * 128]
    h = jnp.where(live_rows[...] > 0.0, 0.0, NEG)
    most = jnp.max(total)
    peak[...] = jnp.full(peak.shape, most, F32)
    store_lse(
        part[...], 0.0, most, part,
        lambda: safe_rows((rows_out, cols_out, n, a_buf, b_buf, sem), h, part, tall),
    )


def fold_y_kernel(plan, *refs):
    parts, out = refs[0:Y], refs[Y]
    out[...] = jnp.zeros(out.shape, F32)
    for first, per in plan["lse"]:
        n = 2 * Y * per
        out[first:first + n, :] = fold_y(parts, first, per)
    if plan["plog"] is not None:
        first, into = plan["plog"]
        out[into:into + 2 * Y, :] = jnp.concatenate(
            [p[first:first + 2, :] for p in parts], axis=0
        )


def coarse2_kernel(mine, other, part, plog, seat, tile, peak, rows_hbm, cols_hbm, payload, plog_rows, tall, *bufs):
    plog_rows[0:8, :] = mine[16:24, :]
    plog_rows[8:16, :] = other[16:24, :]
    h = plog_rows[...] + SC - fold_core(mine, other, 0, 2)
    payload[...] = jnp.zeros(payload.shape, F32)
    reduce_rows(tile, h, peak, payload, tall, (rows_hbm, cols_hbm, PROTO_BLOCK, *bufs))
    payload[8:20, :] = part[...]
    payload[20:22, :] = plog[0:2, :]
    payload[22:25, :] = seat[...]


def fine_h(lse, logs, live, boost=0.0):
    return jnp.where(live[...] > 0.0, SC - logs[0:1, :] - lse + boost, NEG)


def step3_kernel(logs, live_rows, live_cols, p0, p1, p2, p3, ktile, kpeak, krows, kcols, tile, peak, rows_hbm, cols_hbm,
                 payload, plog_cols, seats, wide, kwide, *bufs):
    parts = (p0, p1, p2, p3)
    plog_cols[...] = gather_columns(parts, 20, 2)
    seats[...] = gather_columns(parts, 22, 3)
    payload[...] = jnp.zeros(payload.shape, F32)
    h = fine_h(from_columns(parts, 8, 3), logs, live_cols)
    backup = (rows_hbm, cols_hbm, tile.shape[1] // X, *bufs)
    reduce_columns(tile, h, peak, payload.at[16:40, :], wide, backup, live_rows)
    h = plog_cols[...] + SC - from_columns(parts, 0, 2)
    reduce_columns(ktile, h, kpeak, payload.at[0:16, :], kwide, (krows, kcols, PROTO_BLOCK, *bufs))


def step4_kernel(logs, live_rows, mine, other, plog_rows, ktile, kpeak, krows, kcols, tile, peak, rows_hbm, cols_hbm,
                 payload, tall, ktall, *bufs):
    payload[...] = jnp.zeros(payload.shape, F32)
    h = plog_rows[...] + SC - fold_core(mine, other, 0, 2)
    reduce_rows(ktile, h, kpeak, payload.at[0:8, :], ktall, (krows, kcols, PROTO_BLOCK, *bufs))
    h = fine_h(fold_core(mine, other, 16, 3), logs, live_rows)
    backup = (rows_hbm, cols_hbm, tile.shape[1] // X, *bufs)
    reduce_rows(tile, h, peak, payload.at[8:20, :], tall, backup)


def step5_kernel(logs, live_rows, live_cols, p0, p1, p2, p3, plog_cols, seats, tile, peak, rows_hbm, cols_hbm,
                 payload, coarse, tall, wide, *bufs):
    parts = (p0, p1, p2, p3)
    v = plog_cols[...] + SC - from_columns(parts, 0, 2)
    coarse[...] = v[0:1, :] * (1.0 / SC)
    to_rows(v, tall)
    local = seats[...].astype(jnp.int32)
    boost = []
    for k in range(X * 3):
        vals = tall[(k // 3) * PROTO_BLOCK:(k // 3 + 1) * PROTO_BLOCK, :]
        pick = iota((PROTO_BLOCK, 128), 0) == local[k:k + 1, :]
        boost.append(jnp.sum(jnp.where(pick, vals, 0.0), axis=0, keepdims=True))
    h = fine_h(from_columns(parts, 8, 3), logs, live_cols, jnp.concatenate(boost, axis=0))
    payload[...] = jnp.zeros(payload.shape, F32)
    reduce_columns(tile, h, peak, payload, wide, (rows_hbm, cols_hbm, tile.shape[1] // X, *bufs), live_rows)


def potential(h):
    return jnp.where(h == NEG, 0.0, h)[0:3, :] * (1.0 / SC)


def step6_kernel(logs, live_rows, mine, other, tile, peak, rows_hbm, cols_hbm, payload, out, tall, *bufs):
    h = fine_h(fold_core(mine, other, 0, 3), logs, live_rows)
    out[...] = potential(h)
    payload[...] = jnp.zeros(payload.shape, F32)
    backup = (rows_hbm, cols_hbm, tile.shape[1] // X, *bufs)
    reduce_rows(tile, h, peak, payload, tall, backup)


def last_kernel(logs, live_cols, p0, p1, p2, p3, out):
    out[...] = potential(fine_h(from_columns((p0, p1, p2, p3), 0, 3), logs, live_cols))


def swap(v, axis, bit):
    n = {"z": Z, "c": 2}[axis]
    return lax.ppermute(v, axis, [(i, i ^ bit) for i in range(n)])


def turn(v, axis, k):
    n = {"x": X, "y": Y}[axis]
    return lax.ppermute(
        v, (axis, "c"), [(i * 2 + c, (i + (k if c == 0 else n - k)) % n * 2 + c) for i in range(n) for c in range(2)]
    )


def spread_over(v, axis):
    return [v] + [turn(v, axis, k) for k in (1, 2, 3)]


def vmem(v):
    return pltpu.with_memory_space_constraint(v, pltpu.VMEM)


def held(tile, peak, rows, cols):
    return [vmem(tile), peak, *[pltpu.with_memory_space_constraint(v, HBM) for v in (rows, cols)]]


def local(embeddings, members, counts):
    rows, d = embeddings.shape
    here = jnp.stack([lax.axis_index(a) for a in ("z", "x", "y", "c")]).astype(jnp.int32)
    info = jnp.concatenate(
        [
            jnp.pad(counts, ((0, 0), (0, 128 - counts.shape[1]))),
            jnp.pad(here[None], ((0, 0), (0, 124))),
            members.reshape(rows // 128, 128),
        ],
        axis=0,
    )
    per = rows // 128
    n_rows, n_cols = rows * Y * 2, rows * X
    k_rows, k_cols = PROTO_BLOCK * Y * 2, PROTO_BLOCK * X
    quarter = PROTO_BLOCK // Z
    width = d + PAD

    def first(own):
        return turn(own, "x", 1), turn(own, "x", 3), turn(own, "y", 1), turn(own, "y", 3)

    x1, x3, y1, y3 = first(embeddings)
    keep, send, live_rows, live_cols, seat, logs = call(
        pool_kernel,
        [
            sds((2 * quarter + 8, d)), sds((2 * quarter + 8, d)), sds((n_rows // 128, 128)),
            sds((n_cols // 128, 128)), sds((per, 128)), sds((8, 128)),
        ],
        [SMEM, VMEM, VMEM],
        name="pool",
    )(info, embeddings, info)
    keep, send = call(
        pool2_kernel, [sds((quarter + 8, d)), sds((quarter + 8, d))], [VMEM] * 2, name="pool2"
    )(keep, swap(send, "z", 1))
    got = swap(send, "z", 3)
    x1, x3, y1, y3, got = lax.optimization_barrier((x1, x3, y1, y3, got))
    x2, y2 = turn(x1, "x", 1), turn(y1, "y", 1)
    part = call(means_kernel, sds((quarter, width), BF16), [VMEM] * 2, name="means")(keep, got)
    far = [swap(part, "z", k) for k in (1, 2, 3)]
    x1, y1, y3, x2, y2, embeddings, far = lax.optimization_barrier((x1, y1, y3, x2, y2, embeddings, far))
    means, plog = call(
        join_kernel, [sds((PROTO_BLOCK, d), BF16), sds((8, 128))], [VMEM] * 5, name="join"
    )(logs, part, *far)
    s0, s1, s2, s3 = [swap(v, "c", 1) for v in (embeddings, y1, y2, y3)]
    vectors = [embeddings, x1, x2, x3, y1, y2, y3, s0, s1, s2, s3]

    bufs = [pltpu.VMEM((STEP, d), BF16), pltpu.VMEM((STEP, d), BF16), pltpu.SemaphoreType.DMA]

    def tile_call(body, n, m, part_rows, specs, extra, name):
        out = [pltpu.VMEM((n, m), F32), sds((part_rows, 128)), sds((8, 128)), HBM((n, d), BF16), HBM((m, d), BF16)]
        return call(
            body,
            out,
            specs,
            scratch=[
                pltpu.VMEM((n, d), BF16),
                pltpu.VMEM((m, d), BF16),
                pltpu.SemaphoreType.DMA((2 * Y,)),
                pltpu.SemaphoreType.DMA((X,)),
                pltpu.SemaphoreType.DMA((2,)),
                *extra,
                *bufs,
            ],
            out_specs=[VMEM, VMEM, VMEM, IN_HBM, IN_HBM],
            limit=18,
            name=name,
            flops=2 * n * m * d,
        )

    tall = pltpu.VMEM((n_rows, 128), F32)
    wide = pltpu.VMEM((8, n_cols), F32)
    mx1, mx3, my1, my3 = first(means)
    tile, upart, *back = tile_call(
        fine_tile_kernel, n_rows, n_cols, n_cols // 128, [SMEM, VMEM] + [ANY] * 11, [tall, wide], "fine_tile"
    )(info, live_rows, *vectors)
    upart, means, mx1, mx3, my1, my3 = lax.optimization_barrier((upart, means, mx1, mx3, my1, my3))
    mx2, my2 = turn(mx1, "x", 1), turn(my1, "y", 1)
    t0, t1, t3, t2 = swap(means, "c", 1), swap(my1, "c", 1), swap(my3, "c", 1), swap(my2, "c", 1)
    back = held(tile, *back)

    ktile, part, *kback = tile_call(
        coarse_tile_kernel, k_rows, k_cols, 24, [ANY] * 11 + [VMEM],
        [pltpu.VMEM((k_rows, 128), F32), pltpu.VMEM((8, k_cols), F32)], "coarse_tile"
    )(means, mx1, mx2, mx3, my1, my2, my3, t0, t1, t2, t3, plog)
    kback = held(ktile, *kback)
    kspecs = [VMEM, VMEM, IN_HBM, IN_HBM]
    mine = call(
        lambda *r: fold_y_kernel({"lse": [(0, 2)], "plog": (16, 16)}, *r),
        sds((24, 128)),
        [VMEM] * 4,
        name="fold_y1",
    )(*spread_over(part, "y"))
    other = swap(mine, "c", 1)

    part, plog_rows = call(
        coarse2_kernel,
        [sds((32, 128)), sds((16, 128))],
        [VMEM] * 5 + kspecs,
        scratch=[pltpu.VMEM((k_rows, 128), F32), *bufs],
        name="coarse2",
    )(mine, other, upart, plog, seat, *kback)

    part, plog_cols, seats = call(
        step3_kernel,
        [sds((40, 128)), sds((8, 128)), sds((12, 128))],
        [VMEM] * 7 + kspecs * 2,
        scratch=[wide, pltpu.VMEM((8, k_cols), F32), *bufs],
        name="step3",
    )(logs, live_rows, live_cols, *spread_over(part, "x"), *kback, *back)
    mine = call(
        lambda *r: fold_y_kernel({"lse": [(0, 2), (16, 3)], "plog": None}, *r),
        sds((40, 128)),
        [VMEM] * 4,
        name="fold_y2",
    )(*spread_over(part, "y"))
    other = swap(mine, "c", 1)

    part = call(
        step4_kernel,
        sds((24, 128)),
        [VMEM, VMEM] + [VMEM] * 3 + kspecs * 2,
        scratch=[tall, pltpu.VMEM((k_rows, 128), F32), *bufs],
        name="step4",
    )(logs, live_rows, mine, other, plog_rows, *kback, *back)

    part, coarse = call(
        step5_kernel,
        [sds((24, 128)), sds((1, 128))],
        [VMEM] * 9 + kspecs,
        scratch=[pltpu.VMEM((k_cols, 128), F32), wide, *bufs],
        name="step5",
    )(logs, live_rows, live_cols, *spread_over(part, "x"), plog_cols, seats, *back)
    mine = call(
        lambda *r: fold_y_kernel({"lse": [(0, 3)], "plog": None}, *r),
        sds((24, 128)),
        [VMEM] * 4,
        name="fold_y3",
    )(*spread_over(part, "y"))
    other = swap(mine, "c", 1)

    part, col = call(
        step6_kernel,
        [sds((16, 128)), sds((3, 128))],
        [VMEM, VMEM] + [VMEM] * 2 + kspecs,
        scratch=[tall, *bufs],
        name="step6",
    )(logs, live_rows, mine, other, *back)
    row = call(last_kernel, sds((3, 128)), [VMEM, VMEM] + [VMEM] * 4, name="last")(
        logs, live_cols, *spread_over(part, "x")
    )
    return row.reshape(rows), col.reshape(rows), coarse[0, :quarter]


def solution(mesh):
    split = Mesh(mesh.devices.reshape(Z, X, Y, 2), ("z", "x", "y", "c"))
    every = P(("z", "x", "y", "c"))
    return jax.shard_map(
        local,
        mesh=split,
        in_specs=(P(("z", "x", "y", "c"), None), every, P()),
        out_specs=(every, every, every),
        check_vma=False,
    )
```

```python
import math

import jax
import jax.numpy as jnp
from jax import lax
from jax.experimental import pallas as pl
from jax.experimental.pallas import tpu as pltpu
from jax.sharding import Mesh, PartitionSpec as P


PROTO_BLOCK = 256
EPS = 0.01
SC = math.log2(math.e) / EPS
NEG = -1e30
LOW, HIGH, PEAK = 2.0 ** -25, 2.0 ** 120, 2.0 ** 64
STEP = 256
F32 = jnp.float32
BF16 = jnp.bfloat16
MIB = 2 ** 20
X, Y, Z = 4, 4, 4
PAD = 128

VMEM = pl.BlockSpec(memory_space=pltpu.VMEM)
SMEM = pl.BlockSpec(memory_space=pltpu.SMEM)
ANY = pl.BlockSpec(memory_space=pl.ANY)


HBM = pltpu.MemorySpace.HBM
IN_HBM = pl.BlockSpec(memory_space=HBM)


def call(body, out_shape, in_specs, scratch=(), out_specs=None, limit=6, name=None, flops=0, nbytes=0):
    return pl.pallas_call(
        body,
        out_shape=out_shape,
        in_specs=in_specs,
        out_specs=out_specs or jax.tree.map(lambda _: VMEM, out_shape),
        scratch_shapes=list(scratch),
        compiler_params=pltpu.CompilerParams(vmem_limit_bytes=limit * MIB),
        cost_estimate=pl.CostEstimate(flops=flops, bytes_accessed=nbytes, transcendentals=0),
        name=name,
    )


def sds(shape, dtype=F32):
    return jax.ShapeDtypeStruct(shape, dtype)


def iota(shape, dim):
    return lax.broadcasted_iota(jnp.int32, shape, dim)


def to_lanes(col):
    n = col.shape[0]
    eye = iota((128, 128), 0) == iota((128, 128), 1)
    return jnp.concatenate(
        [
            jnp.sum(jnp.where(eye, col[k * 128:(k + 1) * 128], 0.0), axis=0, keepdims=True)
            for k in range(n // 128)
        ],
        axis=0,
    )


def to_rows(vals, out_ref):
    for k in range(vals.shape[0]):
        out_ref[k * 128:(k + 1) * 128, :] = jnp.transpose(
            jnp.broadcast_to(vals[k:k + 1, :], (128, 128))
        )


def to_rows_by_product(vals, out_ref):
    k = vals.shape[0]
    parts, rest = [], jnp.concatenate([vals, jnp.zeros((32 - k, 128), F32)], axis=0)
    for _ in range(3):
        part = rest.astype(BF16).astype(F32)
        parts.append(part)
        rest = rest - part
    cols = jnp.transpose(jnp.concatenate([*parts, jnp.zeros((32, 128), F32)], axis=0)).astype(BF16)
    which = jnp.bitwise_and(iota((128, 128), 0), 31)
    step = 8
    for j in range(0, k, step):
        pick = jnp.concatenate([jnp.where(which == j + i, 1.0, 0.0).astype(BF16) for i in range(step)], axis=1)
        wide = jnp.dot(cols, pick, preferred_element_type=F32)
        for i in range(step):
            out_ref[(j + i) * 128:(j + i + 1) * 128, :] = wide[:, i * 128:(i + 1) * 128]


def lse2(parts):
    top = parts[0]
    for p in parts[1:]:
        top = jnp.maximum(top, p)
    total = jnp.exp2(parts[0] - top)
    for p in parts[1:]:
        total = total + jnp.exp2(p - top)
    return top + jnp.log2(total)


def most_of(x):
    return jnp.max(jnp.max(x, axis=0, keepdims=True), axis=1, keepdims=True)


def out_of_range(total, peak):
    bad = jnp.sum(jnp.where((total > LOW) & (total < HIGH), 0.0, 1.0), axis=0, keepdims=True)
    bad = bad + jnp.sum(jnp.where(peak <= PEAK, 0.0, 1.0), axis=0, keepdims=True)
    return jnp.sum(bad) > 0.0


def spread(vals, wide_ref):
    for k in range(vals.shape[0]):
        wide_ref[:, k * 128:(k + 1) * 128] = jnp.broadcast_to(vals[k:k + 1, :], (8, 128))


def store_lse(total, shift, peak, out_ref, safe):
    n = total.shape[0]
    bad = out_of_range(total, peak)
    out_ref[0:n, :] = jnp.log2(total) + shift

    @pl.when(bad)
    def _():
        safe()


def reduce_columns(tile, h, guard, out_ref, wide_ref, backup, live=None):
    rows, cols = tile.shape
    shift = most_of(h)
    spread(jnp.exp2(h - shift), wide_ref)
    lane, sub = iota((8, 128), 1), iota((8, 128), 0)

    def body(r, _):
        acc = jnp.zeros((8, 128), F32)
        for g in range(16):
            s = tile[pl.ds(pl.multiple_of(r * 128 + g * 8, 8), 8), :] * wide_ref[...]
            part = jnp.sum(s, axis=1, keepdims=True)
            acc = acc + jnp.where(lane == sub + 8 * g, part, 0.0)
        out_ref[pl.ds(r, 1), :] = jnp.sum(acc, axis=0, keepdims=True)
        return 0

    lax.fori_loop(0, rows // 128, body, 0, unroll=4)
    total = out_ref[0:rows // 128, :]
    if live is not None:
        total = jnp.where(live[...] > 0.0, total, 1.0)
    store_lse(total, shift, guard[...], out_ref, lambda: safe_columns(backup, h, out_ref, wide_ref))


def reduce_rows(tile, h, guard, out_ref, tall_ref, backup):
    rows, cols = tile.shape
    shift = most_of(h)
    to_rows_by_product(jnp.exp2(h - shift), tall_ref)
    width, chunk = cols // 2, 64
    groups = width // 128
    for strip in range(cols // width):
        at = pl.ds(strip * width, width)

        def body(c, acc):
            part = pl.ds(pl.multiple_of(c * chunk, chunk), chunk)
            s = tile[part, at] * jnp.concatenate([tall_ref[part, :]] * groups, axis=1)
            return acc + jnp.sum(s.reshape(chunk // 8, 8, width), axis=0)

        acc = lax.fori_loop(0, rows // chunk, body, jnp.zeros((8, width), F32), unroll=2)
        acc = jnp.sum(acc, axis=0, keepdims=True)
        for k in range(groups):
            row = strip * groups + k
            out_ref[row:row + 1, :] = acc[:, k * 128:(k + 1) * 128]
    store_lse(
        out_ref[0:cols // 128, :], shift, guard[...], out_ref,
        lambda: safe_rows(backup, h, out_ref, tall_ref),
    )


def block_scores(backup, ci, cj):
    rows_hbm, cols_hbm, own, a_buf, b_buf, sem = backup
    for src, at, buf in ((rows_hbm, ci, a_buf), (cols_hbm, cj, b_buf)):
        copy = pltpu.make_async_copy(src.at[pl.ds(pl.multiple_of(at * STEP, STEP), STEP)], buf, sem)
        copy.start()
        copy.wait()
    s = dot_t(a_buf[...], b_buf[...])
    i, j = iota((STEP, STEP), 0) + ci * STEP, iota((STEP, STEP), 1) + cj * STEP
    return jnp.where((i == j) & (j < own), NEG, s)


def safe_columns(backup, h, out_ref, wide_ref):
    n, m = backup[0].shape[0] // STEP, backup[1].shape[0] // STEP
    spread(h, wide_ref)

    def by_rows(ci, _):
        def by_cols(cj, carry):
            top, total = carry
            s = block_scores(backup, ci, cj)
            s = s + wide_ref[0:1, pl.ds(pl.multiple_of(cj * STEP, STEP), STEP)]
            now = jnp.maximum(top, jnp.max(s, axis=1, keepdims=True))
            return now, total * jnp.exp2(top - now) + jnp.sum(jnp.exp2(s - now), axis=1, keepdims=True)

        top, total = lax.fori_loop(
            0, m, by_cols, (jnp.full((STEP, 1), NEG, F32), jnp.zeros((STEP, 1), F32))
        )
        lanes = to_lanes(jnp.broadcast_to(top + jnp.log2(total), (STEP, 128)))
        for k in range(STEP // 128):
            out_ref[pl.ds(ci * (STEP // 128) + k, 1), :] = lanes[k:k + 1, :]
        return 0

    lax.fori_loop(0, n, by_rows, 0)


def safe_rows(backup, h, out_ref, tall_ref):
    n, m = backup[0].shape[0] // STEP, backup[1].shape[0] // STEP
    to_rows(h, tall_ref)

    def by_cols(cj, _):
        def by_rows(ci, carry):
            top, total = carry
            add = tall_ref[pl.ds(pl.multiple_of(ci * STEP, STEP), STEP), :]
            s = block_scores(backup, ci, cj) + jnp.concatenate([add] * (STEP // 128), axis=1)
            now = jnp.maximum(top, jnp.max(s, axis=0, keepdims=True))
            return now, total * jnp.exp2(top - now) + jnp.sum(jnp.exp2(s - now), axis=0, keepdims=True)

        top, total = lax.fori_loop(
            0, n, by_rows, (jnp.full((1, STEP), NEG, F32), jnp.zeros((1, STEP), F32))
        )
        lse = top + jnp.log2(total)
        for k in range(STEP // 128):
            out_ref[pl.ds(cj * (STEP // 128) + k, 1), :] = lse[:, k * 128:(k + 1) * 128]
        return 0

    lax.fori_loop(0, m, by_cols, 0)


def info_place(info):
    return info[Z, 0], info[Z, 1], info[Z, 2], info[Z, 3]


def count_at(counts, z, x, y, c):
    return counts[z, (x * Y + y) * 2 + c]


def behind(at, c, k, n):
    return lax.rem(at + jnp.where(c == 0, n - k, k), n)


def row_counts(counts, idx):
    z, x, y, c = idx
    return [
        count_at(counts, z, x, behind(y, (c + dc) % 2, k, Y), (c + dc) % 2) for dc in range(2) for k in range(Y)
    ]


def col_counts(counts, idx):
    z, x, y, c = idx
    return [count_at(counts, z, behind(x, c, k, X), y, c) for k in range(X)]


def live_mask(block_counts, per):
    at = iota((per, 128), 0) * 128 + iota((per, 128), 1)
    return jnp.concatenate([jnp.where(at < n, 1.0, 0.0) for n in block_counts], axis=0)


def log2_of(n):
    return jnp.log2(jnp.full((1, 128), n, jnp.int32).astype(F32))


def from_columns(parts, first, per):
    blocks = []
    for j in range(X):
        rows = [first + (j - k) % X * per for k in range(X)]
        blocks.append(lse2([p[r:r + per, :] for p, r in zip(parts, rows)]))
    return jnp.concatenate(blocks, axis=0)


def gather_columns(parts, first, per):
    return jnp.concatenate([p[first:first + per, :] for p in parts], axis=0)


def fold_y(parts, first, per):
    blocks = []
    for dc in range(2):
        for j in range(Y):
            rows = [first + (dc * Y + (j - k if dc == 0 else j + k) % Y) * per for k in range(Y)]
            blocks.append(lse2([p[r:r + per, :] for p, r in zip(parts, rows)]))
    return jnp.concatenate(blocks, axis=0)


def fold_core(mine, other, first, per):
    half = Y * per
    return jnp.concatenate(
        [
            lse2([mine[first:first + half, :], other[first + half:first + 2 * half, :]]),
            lse2([mine[first + half:first + 2 * half, :], other[first:first + half, :]]),
        ],
        axis=0,
    )


def pool_kernel(info, emb, table, keep, send, live_rows, live_cols, seat, logs):
    idx = info_place(info)
    z, x, y, c = idx
    quarter = PROTO_BLOCK // Z
    per = seat.shape[0]
    ids = table[Z + 1:Z + 1 + per, :]
    which = lax.shift_right_logical(ids, 11)
    within = jnp.bitwise_and(ids, quarter - 1)
    turn = jnp.bitwise_xor(which, z)
    seat[...] = (turn * quarter + within).astype(F32)
    slot = jnp.where(turn == 0, 0, jnp.where(turn == 3, 1, turn + 1)) * quarter + within
    local = jnp.concatenate([slot[k:k + 1, :] for k in range(per)], axis=1)
    rows, d = emb.shape
    live = iota((1, rows), 1) < count_at(info, z, x, y, c)
    hot = ((iota((PROTO_BLOCK, rows), 0) == local) & live).astype(BF16)
    sums = jnp.dot(hot, emb[...], preferred_element_type=F32)
    sizes = lax.dot_general(
        jnp.ones((8, rows), BF16), hot, (((1,), (1,)), ((), ())), preferred_element_type=F32
    )
    half = 2 * quarter
    keep[0:half, :] = sums[0:half]
    keep[half:, :] = size_rows(sizes[:, 0:half], d)
    send[0:half, :] = sums[half:]
    send[half:, :] = size_rows(sizes[:, half:], d)
    live_rows[...] = live_mask(row_counts(info, idx), per)
    live_cols[...] = live_mask(col_counts(info, idx), per)
    mine, total = 0, 0
    for g in range(Z):
        n = info[g, 0]
        for s in range(1, X * Y * 2):
            n = n + info[g, s]
        mine = mine + jnp.where(g == z, n, 0)
        total = total + n
    logs[...] = jnp.concatenate([log2_of(mine), log2_of(total), jnp.zeros((6, 128), F32)], axis=0)


def size_rows(sizes, d):
    return jnp.concatenate([sizes, jnp.zeros((sizes.shape[0], d - sizes.shape[1]), F32)], axis=1)


def code_sizes(sizes):
    high = jnp.floor(sizes * (1.0 / 256.0))
    low = sizes - 256.0 * high
    return jnp.where(iota(sizes.shape, 1) < 64, high, low).astype(BF16)


def read_sizes(block, d):
    coded = block[:, d:].astype(F32)
    return coded[:, 0:1] * 256.0 + coded[:, 64:65]


def pool2_kernel(mine, got, keep, send):
    half, d = mine.shape[0] - 8, mine.shape[1]
    quarter = half // 2
    keep[0:quarter, :] = mine[0:quarter, :] + got[0:quarter, :]
    send[0:quarter, :] = mine[quarter:half, :] + got[quarter:half, :]
    sizes = mine[half:, 0:half] + got[half:, 0:half]
    keep[quarter:, :] = size_rows(sizes, d)
    send[quarter:, :] = size_rows(jnp.concatenate([sizes[:, quarter:], sizes[:, 0:quarter]], axis=1), d)


def means_kernel(mine, got, out):
    quarter, d = mine.shape[0] - 8, mine.shape[1]
    lanes = mine[quarter:, 0:128] + got[quarter:, 0:128]
    sizes = jnp.transpose(jnp.broadcast_to(lanes[0:1, :], (128, 128)))[0:quarter, :]
    out[:, 0:d] = ((mine[0:quarter, :] + got[0:quarter, :]) / sizes[:, 0:1]).astype(BF16)
    out[:, d:] = code_sizes(sizes)


def join_kernel(logs, p0, p1, p2, p3, means, plog):
    quarter, width = p0.shape
    d = width - PAD
    sizes = []
    for k, ref in enumerate((p0, p1, p2, p3)):
        block = ref[...]
        means[k * quarter:(k + 1) * quarter, :] = block[:, 0:d]
        sizes.append(jnp.broadcast_to(read_sizes(block, d), (quarter, 128)))
    plog[...] = jnp.zeros(plog.shape, F32)
    plog[0:2, :] = jnp.log2(to_lanes(jnp.concatenate(sizes, axis=0))) - logs[1:2, :]


def fetch(row_blocks, col_blocks, rows_buf, cols_buf, row_sems, col_sems):
    size = row_blocks[0].shape[0]

    def start(blocks, buf, sems, b):
        pltpu.make_async_copy(blocks[b], buf.at[pl.ds(b * size, size)], sems.at[b]).start()

    for b in range(X):
        start(col_blocks, cols_buf, col_sems, b)
    for b in range(2 * Y):
        start(row_blocks, rows_buf, row_sems, b)

    def wait(buf, sems, b):
        into = buf.at[pl.ds(pl.multiple_of(b * size, size), size)]
        pltpu.make_async_copy(into, into, sems.at[b]).wait()

    return lambda b: wait(rows_buf, row_sems, b), lambda b: wait(cols_buf, col_sems, b)


def dot_t(a, b):
    return lax.dot_general(a, b, (((1,), (1,)), ((), ())), preferred_element_type=F32) * SC


def fill_tile(tile, size, waits, rows_buf, cols_buf, rows_out, cols_out, out_sems, acc, live, sums):
    rows, cols = tile.shape
    wait_rows, wait_cols = waits
    step, wide = 2 * size, 512
    for b in range(X):
        wait_cols(b)
    save_cols = pltpu.make_async_copy(cols_buf, cols_out, out_sems.at[1])
    save_cols.start()
    if acc is not None:
        acc[...] = jnp.zeros(acc.shape, F32)

    def body(i, _):
        at = pl.ds(pl.multiple_of(i * step, step), step)
        wait_rows(2 * i)
        wait_rows(2 * i + 1)
        pltpu.make_async_copy(rows_buf.at[at], rows_out.at[at], out_sems.at[0]).start()
        for j in range(cols // wide):
            across = pl.ds(j * wide, wide)
            s = dot_t(rows_buf[at, :], cols_buf[across, :])
            if j == 0:
                col = iota((step, wide), 1)
                s = jnp.where((iota((step, wide), 0) + i * step == col) & (col < size), NEG, s)
            s = jnp.exp2(s)
            if live is not None:
                s = s * jnp.concatenate([live[at, :]] * (wide // 128), axis=1)
            tile[at, across] = s
            if acc is not None:
                acc[:, across] += jnp.sum(s.reshape(step // 8, 8, wide), axis=0)
            if sums is not None:
                part = s[:, 0:128]
                for k in range(1, wide // 128):
                    part = part + s[:, k * 128:(k + 1) * 128]
                sums[at, :] = part if j == 0 else sums[at, :] + part
        return 0

    lax.fori_loop(0, rows // step, body, 0)
    pltpu.make_async_copy(rows_buf, rows_out, out_sems.at[0]).wait()
    save_cols.wait()


def coarse_tile_kernel(own, x1, x2, x3, y1, y2, y3, s0, s1, s2, s3, plog, tile, payload, peak, rows_out, cols_out,
                       rows_buf, cols_buf, row_sems, col_sems, out_sems, sums, wide, a_buf, b_buf, sem):
    n = own.shape[0]
    waits = fetch(
        [own, y1, y2, y3, s0, s1, s2, s3], [own, x1, x2, x3], rows_buf, cols_buf, row_sems, col_sems
    )
    fill_tile(tile, n, waits, rows_buf, cols_buf, rows_out, cols_out, out_sems, None, None, sums)
    rows, cols = tile.shape
    payload[...] = jnp.zeros(payload.shape, F32)
    lane, sub = iota((8, 128), 1), iota((8, 128), 0)

    def body(r, _):
        acc = jnp.zeros((8, 128), F32)
        for g in range(16):
            s = sums[pl.ds(pl.multiple_of(r * 128 + g * 8, 8), 8), :]
            acc = acc + jnp.where(lane == sub + 8 * g, jnp.sum(s, axis=1, keepdims=True), 0.0)
        payload[pl.ds(r, 1), :] = jnp.sum(acc, axis=0, keepdims=True)
        return 0

    lax.fori_loop(0, rows // 128, body, 0, unroll=4)
    total = payload[0:rows // 128, :]
    peak[...] = jnp.broadcast_to(most_of(total), peak.shape)
    store_lse(
        total, 0.0, peak[...], payload,
        lambda: safe_columns(
            (rows_out, cols_out, n, a_buf, b_buf, sem), jnp.zeros((cols // 128, 128), F32), payload, wide
        ),
    )
    payload[rows // 128:rows // 128 + 2, :] = plog[0:2, :]


def fine_tile_kernel(info, live_rows, own, x1, x2, x3, y1, y2, y3, s0, s1, s2, s3, tile, part, peak, rows_out,
                     cols_out, rows_buf, cols_buf, row_sems, col_sems, out_sems, tall, acc, a_buf, b_buf, sem):
    n = own.shape[0]
    waits = fetch(
        [own, y1, y2, y3, s0, s1, s2, s3], [own, x1, x2, x3], rows_buf, cols_buf, row_sems, col_sems
    )
    for b, count in enumerate(row_counts(info, info_place(info))):
        tall[b * n:(b + 1) * n, :] = jnp.where(iota((n, 128), 0) < count, 1.0, 0.0)
    fill_tile(tile, n, waits, rows_buf, cols_buf, rows_out, cols_out, out_sems, acc, tall, None)
    rows, cols = tile.shape
    total = jnp.sum(acc[...], axis=0, keepdims=True)
    for k in range(cols // 128):
        part[k:k + 1, :] = total[:, k * 128:(k + 1) * 128]
    h = jnp.where(live_rows[...] > 0.0, 0.0, NEG)
    peak[...] = jnp.broadcast_to(most_of(total), peak.shape)
    store_lse(
        part[...], 0.0, peak[...], part,
        lambda: safe_rows((rows_out, cols_out, n, a_buf, b_buf, sem), h, part, tall),
    )


def fold_y_kernel(plan, *refs):
    parts, out = refs[0:Y], refs[Y]
    out[...] = jnp.zeros(out.shape, F32)
    for first, per in plan["lse"]:
        n = 2 * Y * per
        out[first:first + n, :] = fold_y(parts, first, per)
    if plan["plog"] is not None:
        first, into = plan["plog"]
        out[into:into + 2 * Y, :] = jnp.concatenate(
            [p[first:first + 2, :] for p in parts], axis=0
        )


def coarse2_kernel(mine, other, part, plog, seat, tile, peak, rows_hbm, cols_hbm, payload, plog_rows, tall, *bufs):
    plog_rows[0:8, :] = mine[16:24, :]
    plog_rows[8:16, :] = other[16:24, :]
    h = plog_rows[...] + SC - fold_core(mine, other, 0, 2)
    payload[...] = jnp.zeros(payload.shape, F32)
    reduce_rows(tile, h, peak, payload, tall, (rows_hbm, cols_hbm, PROTO_BLOCK, *bufs))
    payload[8:20, :] = part[...]
    payload[20:22, :] = plog[0:2, :]
    payload[22:25, :] = seat[...]


def fine_h(lse, logs, live, boost=0.0):
    return jnp.where(live[...] > 0.0, SC - logs[0:1, :] - lse + boost, NEG)


def step3_kernel(logs, live_rows, live_cols, p0, p1, p2, p3, ktile, kpeak, krows, kcols, tile, peak, rows_hbm, cols_hbm,
                 payload, plog_cols, seats, wide, kwide, *bufs):
    parts = (p0, p1, p2, p3)
    plog_cols[...] = gather_columns(parts, 20, 2)
    seats[...] = gather_columns(parts, 22, 3)
    payload[...] = jnp.zeros(payload.shape, F32)
    h = fine_h(from_columns(parts, 8, 3), logs, live_cols)
    backup = (rows_hbm, cols_hbm, tile.shape[1] // X, *bufs)
    reduce_columns(tile, h, peak, payload.at[16:40, :], wide, backup, live_rows)
    h = plog_cols[...] + SC - from_columns(parts, 0, 2)
    reduce_columns(ktile, h, kpeak, payload.at[0:16, :], kwide, (krows, kcols, PROTO_BLOCK, *bufs))


def step4_kernel(logs, live_rows, mine, other, plog_rows, ktile, kpeak, krows, kcols, tile, peak, rows_hbm, cols_hbm,
                 payload, tall, ktall, *bufs):
    payload[...] = jnp.zeros(payload.shape, F32)
    h = plog_rows[...] + SC - fold_core(mine, other, 0, 2)
    reduce_rows(ktile, h, kpeak, payload.at[0:8, :], ktall, (krows, kcols, PROTO_BLOCK, *bufs))
    h = fine_h(fold_core(mine, other, 16, 3), logs, live_rows)
    backup = (rows_hbm, cols_hbm, tile.shape[1] // X, *bufs)
    reduce_rows(tile, h, peak, payload.at[8:20, :], tall, backup)


def step5_kernel(logs, live_rows, live_cols, p0, p1, p2, p3, plog_cols, seats, tile, peak, rows_hbm, cols_hbm,
                 payload, coarse, tall, wide, *bufs):
    parts = (p0, p1, p2, p3)
    v = plog_cols[...] + SC - from_columns(parts, 0, 2)
    coarse[...] = v[0:1, :] * (1.0 / SC)
    to_rows(v, tall)
    local = seats[...].astype(jnp.int32)
    boost = []
    for k in range(X * 3):
        vals = tall[(k // 3) * PROTO_BLOCK:(k // 3 + 1) * PROTO_BLOCK, :]
        pick = iota((PROTO_BLOCK, 128), 0) == local[k:k + 1, :]
        boost.append(jnp.sum(jnp.where(pick, vals, 0.0), axis=0, keepdims=True))
    h = fine_h(from_columns(parts, 8, 3), logs, live_cols, jnp.concatenate(boost, axis=0))
    payload[...] = jnp.zeros(payload.shape, F32)
    reduce_columns(tile, h, peak, payload, wide, (rows_hbm, cols_hbm, tile.shape[1] // X, *bufs), live_rows)


def potential(h):
    return jnp.where(h == NEG, 0.0, h)[0:3, :] * (1.0 / SC)


def step6_kernel(logs, live_rows, mine, other, tile, peak, rows_hbm, cols_hbm, payload, out, tall, *bufs):
    h = fine_h(fold_core(mine, other, 0, 3), logs, live_rows)
    out[...] = potential(h)
    payload[...] = jnp.zeros(payload.shape, F32)
    backup = (rows_hbm, cols_hbm, tile.shape[1] // X, *bufs)
    reduce_rows(tile, h, peak, payload, tall, backup)


def last_kernel(logs, live_cols, p0, p1, p2, p3, out):
    out[...] = potential(fine_h(from_columns((p0, p1, p2, p3), 0, 3), logs, live_cols))


def swap(v, axis, bit):
    n = {"z": Z, "c": 2}[axis]
    return lax.ppermute(v, axis, [(i, i ^ bit) for i in range(n)])


def turn(v, axis, k):
    n = {"x": X, "y": Y}[axis]
    return lax.ppermute(
        v, (axis, "c"), [(i * 2 + c, (i + (k if c == 0 else n - k)) % n * 2 + c) for i in range(n) for c in range(2)]
    )


def spread_over(v, axis):
    return [v] + [turn(v, axis, k) for k in (1, 2, 3)]


def vmem(v):
    return pltpu.with_memory_space_constraint(v, pltpu.VMEM)


def held(tile, peak, rows, cols):
    return [vmem(tile), peak, *[pltpu.with_memory_space_constraint(v, HBM) for v in (rows, cols)]]


def local(embeddings, members, counts):
    rows, d = embeddings.shape
    here = jnp.stack([lax.axis_index(a) for a in ("z", "x", "y", "c")]).astype(jnp.int32)
    info = jnp.concatenate(
        [
            jnp.pad(counts, ((0, 0), (0, 128 - counts.shape[1]))),
            jnp.pad(here[None], ((0, 0), (0, 124))),
            members.reshape(rows // 128, 128),
        ],
        axis=0,
    )
    per = rows // 128
    n_rows, n_cols = rows * Y * 2, rows * X
    k_rows, k_cols = PROTO_BLOCK * Y * 2, PROTO_BLOCK * X
    quarter = PROTO_BLOCK // Z
    width = d + PAD

    def first(own):
        return turn(own, "x", 1), turn(own, "x", 3), turn(own, "y", 1), turn(own, "y", 3)

    x1, x3, y1, y3 = first(embeddings)
    keep, send, live_rows, live_cols, seat, logs = call(
        pool_kernel,
        [
            sds((2 * quarter + 8, d)), sds((2 * quarter + 8, d)), sds((n_rows // 128, 128)),
            sds((n_cols // 128, 128)), sds((per, 128)), sds((8, 128)),
        ],
        [SMEM, VMEM, VMEM],
        name="pool",
    )(info, embeddings, info)
    keep, send = call(
        pool2_kernel, [sds((quarter + 8, d)), sds((quarter + 8, d))], [VMEM] * 2, name="pool2"
    )(keep, swap(send, "z", 1))
    got = swap(send, "z", 3)
    x1, x3, y1, y3, got = lax.optimization_barrier((x1, x3, y1, y3, got))
    x2, y2 = turn(x1, "x", 1), turn(y1, "y", 1)
    part = call(means_kernel, sds((quarter, width), BF16), [VMEM] * 2, name="means")(keep, got)
    far = [swap(part, "z", k) for k in (1, 2, 3)]
    x1, y1, y3, x2, y2, embeddings, far = lax.optimization_barrier((x1, y1, y3, x2, y2, embeddings, far))
    means, plog = call(
        join_kernel, [sds((PROTO_BLOCK, d), BF16), sds((8, 128))], [VMEM] * 5, name="join"
    )(logs, part, *far)
    s0, s1, s2, s3 = [swap(v, "c", 1) for v in (embeddings, y1, y2, y3)]
    vectors = [embeddings, x1, x2, x3, y1, y2, y3, s0, s1, s2, s3]

    bufs = [pltpu.VMEM((STEP, d), BF16), pltpu.VMEM((STEP, d), BF16), pltpu.SemaphoreType.DMA]

    def tile_call(body, n, m, part_rows, specs, extra, name):
        out = [pltpu.VMEM((n, m), F32), sds((part_rows, 128)), sds((8, 128)), HBM((n, d), BF16), HBM((m, d), BF16)]
        return call(
            body,
            out,
            specs,
            scratch=[
                pltpu.VMEM((n, d), BF16),
                pltpu.VMEM((m, d), BF16),
                pltpu.SemaphoreType.DMA((2 * Y,)),
                pltpu.SemaphoreType.DMA((X,)),
                pltpu.SemaphoreType.DMA((2,)),
                *extra,
                *bufs,
            ],
            out_specs=[VMEM, VMEM, VMEM, IN_HBM, IN_HBM],
            limit=18,
            name=name,
            flops=2 * n * m * d,
        )

    tall = pltpu.VMEM((n_rows, 128), F32)
    wide = pltpu.VMEM((8, n_cols), F32)
    mx1, mx3, my1, my3 = first(means)
    tile, upart, *back = tile_call(
        fine_tile_kernel, n_rows, n_cols, n_cols // 128, [SMEM, VMEM] + [ANY] * 11, [tall, wide], "fine_tile"
    )(info, live_rows, *vectors)
    upart, means, mx1, mx3, my1, my3 = lax.optimization_barrier((upart, means, mx1, mx3, my1, my3))
    mx2, my2 = turn(mx1, "x", 1), turn(my1, "y", 1)
    t0, t1, t3, t2 = swap(means, "c", 1), swap(my1, "c", 1), swap(my3, "c", 1), swap(my2, "c", 1)
    back = held(tile, *back)

    ktile, part, *kback = tile_call(
        coarse_tile_kernel, k_rows, k_cols, 24, [ANY] * 11 + [VMEM],
        [pltpu.VMEM((k_rows, 128), F32), pltpu.VMEM((8, k_cols), F32)], "coarse_tile"
    )(means, mx1, mx2, mx3, my1, my2, my3, t0, t1, t2, t3, plog)
    kback = held(ktile, *kback)
    kspecs = [VMEM, VMEM, IN_HBM, IN_HBM]
    mine = call(
        lambda *r: fold_y_kernel({"lse": [(0, 2)], "plog": (16, 16)}, *r),
        sds((24, 128)),
        [VMEM] * 4,
        name="fold_y1",
    )(*spread_over(part, "y"))
    other = swap(mine, "c", 1)

    part, plog_rows = call(
        coarse2_kernel,
        [sds((32, 128)), sds((16, 128))],
        [VMEM] * 5 + kspecs,
        scratch=[pltpu.VMEM((k_rows, 128), F32), *bufs],
        name="coarse2",
    )(mine, other, upart, plog, seat, *kback)

    part, plog_cols, seats = call(
        step3_kernel,
        [sds((40, 128)), sds((8, 128)), sds((12, 128))],
        [VMEM] * 7 + kspecs * 2,
        scratch=[wide, pltpu.VMEM((8, k_cols), F32), *bufs],
        name="step3",
    )(logs, live_rows, live_cols, *spread_over(part, "x"), *kback, *back)
    mine = call(
        lambda *r: fold_y_kernel({"lse": [(0, 2), (16, 3)], "plog": None}, *r),
        sds((40, 128)),
        [VMEM] * 4,
        name="fold_y2",
    )(*spread_over(part, "y"))
    other = swap(mine, "c", 1)

    part = call(
        step4_kernel,
        sds((24, 128)),
        [VMEM, VMEM] + [VMEM] * 3 + kspecs * 2,
        scratch=[tall, pltpu.VMEM((k_rows, 128), F32), *bufs],
        name="step4",
    )(logs, live_rows, mine, other, plog_rows, *kback, *back)

    part, coarse = call(
        step5_kernel,
        [sds((24, 128)), sds((1, 128))],
        [VMEM] * 9 + kspecs,
        scratch=[pltpu.VMEM((k_cols, 128), F32), wide, *bufs],
        name="step5",
    )(logs, live_rows, live_cols, *spread_over(part, "x"), plog_cols, seats, *back)
    mine = call(
        lambda *r: fold_y_kernel({"lse": [(0, 3)], "plog": None}, *r),
        sds((24, 128)),
        [VMEM] * 4,
        name="fold_y3",
    )(*spread_over(part, "y"))
    other = swap(mine, "c", 1)

    part, col = call(
        step6_kernel,
        [sds((16, 128)), sds((3, 128))],
        [VMEM, VMEM] + [VMEM] * 2 + kspecs,
        scratch=[tall, *bufs],
        name="step6",
    )(logs, live_rows, mine, other, *back)
    row = call(last_kernel, sds((3, 128)), [VMEM, VMEM] + [VMEM] * 4, name="last")(
        logs, live_cols, *spread_over(part, "x")
    )
    return row.reshape(rows), col.reshape(rows), coarse[0, :quarter]


def solution(mesh):
    split = Mesh(mesh.devices.reshape(Z, X, Y, 2), ("z", "x", "y", "c"))
    every = P(("z", "x", "y", "c"))
    return jax.shard_map(
        local,
        mesh=split,
        in_specs=(P(("z", "x", "y", "c"), None), every, P()),
        out_specs=(every, every, every),
        check_vma=False,
    )
```

```python
import math

import jax
import jax.numpy as jnp
from jax import lax
from jax.experimental import pallas as pl
from jax.experimental.pallas import tpu as pltpu
from jax.sharding import Mesh, PartitionSpec as P


PROTO_BLOCK = 256
EPS = 0.01
SC = math.log2(math.e) / EPS
NEG = -1e30
LOW, HIGH, PEAK = 2.0 ** -25, 2.0 ** 120, 2.0 ** 64
STEP = 256
F32 = jnp.float32
BF16 = jnp.bfloat16
MIB = 2 ** 20
X, Y, Z = 4, 4, 4
PAD = 128

VMEM = pl.BlockSpec(memory_space=pltpu.VMEM)
SMEM = pl.BlockSpec(memory_space=pltpu.SMEM)
ANY = pl.BlockSpec(memory_space=pl.ANY)


HBM = pltpu.MemorySpace.HBM
IN_HBM = pl.BlockSpec(memory_space=HBM)


def call(body, out_shape, in_specs, scratch=(), out_specs=None, limit=6, name=None, flops=0, nbytes=0):
    return pl.pallas_call(
        body,
        out_shape=out_shape,
        in_specs=in_specs,
        out_specs=out_specs or jax.tree.map(lambda _: VMEM, out_shape),
        scratch_shapes=list(scratch),
        compiler_params=pltpu.CompilerParams(vmem_limit_bytes=limit * MIB),
        cost_estimate=pl.CostEstimate(flops=flops, bytes_accessed=nbytes, transcendentals=0),
        name=name,
    )


def sds(shape, dtype=F32):
    return jax.ShapeDtypeStruct(shape, dtype)


def iota(shape, dim):
    return lax.broadcasted_iota(jnp.int32, shape, dim)


def to_lanes(col):
    n = col.shape[0]
    eye = iota((128, 128), 0) == iota((128, 128), 1)
    return jnp.concatenate(
        [
            jnp.sum(jnp.where(eye, col[k * 128:(k + 1) * 128], 0.0), axis=0, keepdims=True)
            for k in range(n // 128)
        ],
        axis=0,
    )


def to_rows(vals, out_ref):
    for k in range(vals.shape[0]):
        out_ref[k * 128:(k + 1) * 128, :] = jnp.transpose(
            jnp.broadcast_to(vals[k:k + 1, :], (128, 128))
        )


def to_rows_by_product(vals, out_ref):
    k = vals.shape[0]
    parts, rest = [], jnp.concatenate([vals, jnp.zeros((32 - k, 128), F32)], axis=0)
    for _ in range(3):
        part = rest.astype(BF16).astype(F32)
        parts.append(part)
        rest = rest - part
    cols = jnp.transpose(jnp.concatenate([*parts, jnp.zeros((32, 128), F32)], axis=0)).astype(BF16)
    which = jnp.bitwise_and(iota((128, 128), 0), 31)
    step = 8
    for j in range(0, k, step):
        pick = jnp.concatenate([jnp.where(which == j + i, 1.0, 0.0).astype(BF16) for i in range(step)], axis=1)
        wide = jnp.dot(cols, pick, preferred_element_type=F32)
        for i in range(step):
            out_ref[(j + i) * 128:(j + i + 1) * 128, :] = wide[:, i * 128:(i + 1) * 128]


def lse2(parts):
    top = parts[0]
    for p in parts[1:]:
        top = jnp.maximum(top, p)
    total = jnp.exp2(parts[0] - top)
    for p in parts[1:]:
        total = total + jnp.exp2(p - top)
    return top + jnp.log2(total)


def most_of(x):
    return jnp.max(jnp.max(x, axis=0, keepdims=True), axis=1, keepdims=True)


def out_of_range(total, peak):
    bad = jnp.sum(jnp.where((total > LOW) & (total < HIGH), 0.0, 1.0), axis=0, keepdims=True)
    bad = bad + jnp.sum(jnp.where(peak <= PEAK, 0.0, 1.0), axis=0, keepdims=True)
    return jnp.sum(bad) > 0.0


def spread(vals, wide_ref):
    for k in range(vals.shape[0]):
        wide_ref[:, k * 128:(k + 1) * 128] = jnp.broadcast_to(vals[k:k + 1, :], (8, 128))


def store_lse(total, shift, peak, out_ref, safe):
    n = total.shape[0]
    bad = out_of_range(total, peak)
    out_ref[0:n, :] = jnp.log2(total) + shift

    @pl.when(bad)
    def _():
        safe()


def reduce_columns(tile, h, guard, out_ref, wide_ref, backup, live=None):
    rows, cols = tile.shape
    shift = most_of(h)
    spread(jnp.exp2(h - shift), wide_ref)
    lane, sub = iota((8, 128), 1), iota((8, 128), 0)

    def body(r, _):
        acc = jnp.zeros((8, 128), F32)
        for g in range(16):
            s = tile[pl.ds(pl.multiple_of(r * 128 + g * 8, 8), 8), :] * wide_ref[...]
            part = jnp.sum(s, axis=1, keepdims=True)
            acc = acc + jnp.where(lane == sub + 8 * g, part, 0.0)
        out_ref[pl.ds(r, 1), :] = jnp.sum(acc, axis=0, keepdims=True)
        return 0

    lax.fori_loop(0, rows // 128, body, 0, unroll=4)
    total = out_ref[0:rows // 128, :]
    if live is not None:
        total = jnp.where(live[...] > 0.0, total, 1.0)
    store_lse(total, shift, guard[...], out_ref, lambda: safe_columns(backup, h, out_ref, wide_ref))


def reduce_rows(tile, h, guard, out_ref, tall_ref, backup):
    rows, cols = tile.shape
    shift = most_of(h)
    to_rows_by_product(jnp.exp2(h - shift), tall_ref)
    width, chunk = cols // 2, 64
    groups = width // 128
    for strip in range(cols // width):
        at = pl.ds(strip * width, width)

        def body(c, acc):
            part = pl.ds(pl.multiple_of(c * chunk, chunk), chunk)
            s = tile[part, at] * jnp.concatenate([tall_ref[part, :]] * groups, axis=1)
            return acc + jnp.sum(s.reshape(chunk // 8, 8, width), axis=0)

        acc = lax.fori_loop(0, rows // chunk, body, jnp.zeros((8, width), F32), unroll=2)
        acc = jnp.sum(acc, axis=0, keepdims=True)
        for k in range(groups):
            row = strip * groups + k
            out_ref[row:row + 1, :] = acc[:, k * 128:(k + 1) * 128]
    store_lse(
        out_ref[0:cols // 128, :], shift, guard[...], out_ref,
        lambda: safe_rows(backup, h, out_ref, tall_ref),
    )


def block_scores(backup, ci, cj):
    rows_hbm, cols_hbm, own, a_buf, b_buf, sem = backup
    for src, at, buf in ((rows_hbm, ci, a_buf), (cols_hbm, cj, b_buf)):
        copy = pltpu.make_async_copy(src.at[pl.ds(pl.multiple_of(at * STEP, STEP), STEP)], buf, sem)
        copy.start()
        copy.wait()
    s = dot_t(a_buf[...], b_buf[...])
    i, j = iota((STEP, STEP), 0) + ci * STEP, iota((STEP, STEP), 1) + cj * STEP
    return jnp.where((i == j) & (j < own), NEG, s)


def safe_columns(backup, h, out_ref, wide_ref):
    n, m = backup[0].shape[0] // STEP, backup[1].shape[0] // STEP
    spread(h, wide_ref)

    def by_rows(ci, _):
        def by_cols(cj, carry):
            top, total = carry
            s = block_scores(backup, ci, cj)
            s = s + wide_ref[0:1, pl.ds(pl.multiple_of(cj * STEP, STEP), STEP)]
            now = jnp.maximum(top, jnp.max(s, axis=1, keepdims=True))
            return now, total * jnp.exp2(top - now) + jnp.sum(jnp.exp2(s - now), axis=1, keepdims=True)

        top, total = lax.fori_loop(
            0, m, by_cols, (jnp.full((STEP, 1), NEG, F32), jnp.zeros((STEP, 1), F32))
        )
        lanes = to_lanes(jnp.broadcast_to(top + jnp.log2(total), (STEP, 128)))
        for k in range(STEP // 128):
            out_ref[pl.ds(ci * (STEP // 128) + k, 1), :] = lanes[k:k + 1, :]
        return 0

    lax.fori_loop(0, n, by_rows, 0)


def safe_rows(backup, h, out_ref, tall_ref):
    n, m = backup[0].shape[0] // STEP, backup[1].shape[0] // STEP
    to_rows(h, tall_ref)

    def by_cols(cj, _):
        def by_rows(ci, carry):
            top, total = carry
            add = tall_ref[pl.ds(pl.multiple_of(ci * STEP, STEP), STEP), :]
            s = block_scores(backup, ci, cj) + jnp.concatenate([add] * (STEP // 128), axis=1)
            now = jnp.maximum(top, jnp.max(s, axis=0, keepdims=True))
            return now, total * jnp.exp2(top - now) + jnp.sum(jnp.exp2(s - now), axis=0, keepdims=True)

        top, total = lax.fori_loop(
            0, n, by_rows, (jnp.full((1, STEP), NEG, F32), jnp.zeros((1, STEP), F32))
        )
        lse = top + jnp.log2(total)
        for k in range(STEP // 128):
            out_ref[pl.ds(cj * (STEP // 128) + k, 1), :] = lse[:, k * 128:(k + 1) * 128]
        return 0

    lax.fori_loop(0, m, by_cols, 0)


def info_place(info):
    return info[Z, 0], info[Z, 1], info[Z, 2], info[Z, 3]


def count_at(counts, z, x, y, c):
    return counts[z, (x * Y + y) * 2 + c]


def behind(at, c, k, n):
    return lax.rem(at + jnp.where(c == 0, n - k, k), n)


def row_counts(counts, idx):
    z, x, y, c = idx
    return [
        count_at(counts, z, x, behind(y, (c + dc) % 2, k, Y), (c + dc) % 2) for dc in range(2) for k in range(Y)
    ]


def col_counts(counts, idx):
    z, x, y, c = idx
    return [count_at(counts, z, behind(x, c, k, X), y, c) for k in range(X)]


def live_mask(block_counts, per):
    at = iota((per, 128), 0) * 128 + iota((per, 128), 1)
    return jnp.concatenate([jnp.where(at < n, 1.0, 0.0) for n in block_counts], axis=0)


def log2_of(n):
    return jnp.log2(jnp.full((1, 128), n, jnp.int32).astype(F32))


def from_columns(parts, first, per):
    blocks = []
    for j in range(X):
        rows = [first + (j - k) % X * per for k in range(X)]
        blocks.append(lse2([p[r:r + per, :] for p, r in zip(parts, rows)]))
    return jnp.concatenate(blocks, axis=0)


def gather_columns(parts, first, per):
    return jnp.concatenate([p[first:first + per, :] for p in parts], axis=0)


def fold_y(parts, first, per):
    blocks = []
    for dc in range(2):
        for j in range(Y):
            rows = [first + (dc * Y + (j - k if dc == 0 else j + k) % Y) * per for k in range(Y)]
            blocks.append(lse2([p[r:r + per, :] for p, r in zip(parts, rows)]))
    return jnp.concatenate(blocks, axis=0)


def fold_core(mine, other, first, per):
    half = Y * per
    return jnp.concatenate(
        [
            lse2([mine[first:first + half, :], other[first + half:first + 2 * half, :]]),
            lse2([mine[first + half:first + 2 * half, :], other[first:first + half, :]]),
        ],
        axis=0,
    )


def pool_kernel(info, emb, table, keep, send, live_rows, live_cols, seat, logs):
    idx = info_place(info)
    z, x, y, c = idx
    quarter = PROTO_BLOCK // Z
    per = seat.shape[0]
    ids = table[Z + 1:Z + 1 + per, :]
    which = lax.shift_right_logical(ids, 11)
    within = jnp.bitwise_and(ids, quarter - 1)
    turn = jnp.bitwise_xor(which, z)
    seat[...] = (turn * quarter + within).astype(F32)
    slot = jnp.where(turn == 0, 0, jnp.where(turn == 3, 1, turn + 1)) * quarter + within
    local = jnp.concatenate([slot[k:k + 1, :] for k in range(per)], axis=1)
    rows, d = emb.shape
    live = iota((1, rows), 1) < count_at(info, z, x, y, c)
    hot = ((iota((PROTO_BLOCK, rows), 0) == local) & live).astype(BF16)
    sums = jnp.dot(hot, emb[...], preferred_element_type=F32)
    sizes = lax.dot_general(
        jnp.ones((8, rows), BF16), hot, (((1,), (1,)), ((), ())), preferred_element_type=F32
    )
    half = 2 * quarter
    keep[0:half, :] = sums[0:half]
    keep[half:, :] = size_rows(sizes[:, 0:half], d)
    send[0:half, :] = sums[half:]
    send[half:, :] = size_rows(sizes[:, half:], d)
    live_rows[...] = live_mask(row_counts(info, idx), per)
    live_cols[...] = live_mask(col_counts(info, idx), per)
    mine, total = 0, 0
    for g in range(Z):
        n = info[g, 0]
        for s in range(1, X * Y * 2):
            n = n + info[g, s]
        mine = mine + jnp.where(g == z, n, 0)
        total = total + n
    logs[...] = jnp.concatenate([log2_of(mine), log2_of(total), jnp.zeros((6, 128), F32)], axis=0)


def size_rows(sizes, d):
    return jnp.concatenate([sizes, jnp.zeros((sizes.shape[0], d - sizes.shape[1]), F32)], axis=1)


def code_sizes(sizes):
    high = jnp.floor(sizes * (1.0 / 256.0))
    low = sizes - 256.0 * high
    return jnp.where(iota(sizes.shape, 1) < 64, high, low).astype(BF16)


def read_sizes(block, d):
    coded = block[:, d:].astype(F32)
    return coded[:, 0:1] * 256.0 + coded[:, 64:65]


def pool2_kernel(mine, got, keep, send):
    half, d = mine.shape[0] - 8, mine.shape[1]
    quarter = half // 2
    keep[0:quarter, :] = mine[0:quarter, :] + got[0:quarter, :]
    send[0:quarter, :] = mine[quarter:half, :] + got[quarter:half, :]
    sizes = mine[half:, 0:half] + got[half:, 0:half]
    keep[quarter:, :] = size_rows(sizes, d)
    send[quarter:, :] = size_rows(jnp.concatenate([sizes[:, quarter:], sizes[:, 0:quarter]], axis=1), d)


def means_kernel(mine, got, out):
    quarter, d = mine.shape[0] - 8, mine.shape[1]
    lanes = mine[quarter:, 0:128] + got[quarter:, 0:128]
    sizes = jnp.transpose(jnp.broadcast_to(lanes[0:1, :], (128, 128)))[0:quarter, :]
    out[:, 0:d] = ((mine[0:quarter, :] + got[0:quarter, :]) / sizes[:, 0:1]).astype(BF16)
    out[:, d:] = code_sizes(sizes)


def join_kernel(logs, p0, p1, p2, p3, means, plog):
    quarter, width = p0.shape
    d = width - PAD
    sizes = []
    for k, ref in enumerate((p0, p1, p2, p3)):
        block = ref[...]
        means[k * quarter:(k + 1) * quarter, :] = block[:, 0:d]
        sizes.append(jnp.broadcast_to(read_sizes(block, d), (quarter, 128)))
    plog[...] = jnp.zeros(plog.shape, F32)
    plog[0:2, :] = jnp.log2(to_lanes(jnp.concatenate(sizes, axis=0))) - logs[1:2, :]


def fetch(row_blocks, col_blocks, rows_buf, cols_buf, row_sems, col_sems):
    size = row_blocks[0].shape[0]

    def start(blocks, buf, sems, b):
        pltpu.make_async_copy(blocks[b], buf.at[pl.ds(b * size, size)], sems.at[b]).start()

    for b in range(X):
        start(col_blocks, cols_buf, col_sems, b)
    for b in range(2 * Y):
        start(row_blocks, rows_buf, row_sems, b)

    def wait(buf, sems, b):
        into = buf.at[pl.ds(pl.multiple_of(b * size, size), size)]
        pltpu.make_async_copy(into, into, sems.at[b]).wait()

    return lambda b: wait(rows_buf, row_sems, b), lambda b: wait(cols_buf, col_sems, b)


def dot_t(a, b):
    return lax.dot_general(a, b, (((1,), (1,)), ((), ())), preferred_element_type=F32) * SC


def fill_tile(tile, size, waits, rows_buf, cols_buf, rows_out, cols_out, out_sems, acc, live, sums):
    rows, cols = tile.shape
    wait_rows, wait_cols = waits
    step, wide = 2 * size, 512
    for b in range(X):
        wait_cols(b)
    save_cols = pltpu.make_async_copy(cols_buf, cols_out, out_sems.at[1])
    save_cols.start()
    if acc is not None:
        acc[...] = jnp.zeros(acc.shape, F32)

    def body(i, _):
        at = pl.ds(pl.multiple_of(i * step, step), step)
        wait_rows(2 * i)
        wait_rows(2 * i + 1)
        pltpu.make_async_copy(rows_buf.at[at], rows_out.at[at], out_sems.at[0]).start()
        for j in range(cols // wide):
            across = pl.ds(j * wide, wide)
            s = dot_t(rows_buf[at, :], cols_buf[across, :])
            if j == 0:
                col = iota((step, wide), 1)
                s = jnp.where((iota((step, wide), 0) + i * step == col) & (col < size), NEG, s)
            s = jnp.exp2(s)
            if live is not None:
                s = s * jnp.concatenate([live[at, :]] * (wide // 128), axis=1)
            tile[at, across] = s
            if acc is not None:
                acc[:, across] += jnp.sum(s.reshape(step // 8, 8, wide), axis=0)
            if sums is not None:
                part = s[:, 0:128]
                for k in range(1, wide // 128):
                    part = part + s[:, k * 128:(k + 1) * 128]
                sums[at, :] = part if j == 0 else sums[at, :] + part
        return 0

    lax.fori_loop(0, rows // step, body, 0)
    pltpu.make_async_copy(rows_buf, rows_out, out_sems.at[0]).wait()
    save_cols.wait()


def coarse_tile_kernel(own, x1, x2, x3, y1, y2, y3, s0, s1, s2, s3, plog, tile, payload, peak, rows_out, cols_out,
                       rows_buf, cols_buf, row_sems, col_sems, out_sems, sums, wide, a_buf, b_buf, sem):
    n = own.shape[0]
    waits = fetch(
        [own, y1, y2, y3, s0, s1, s2, s3], [own, x1, x2, x3], rows_buf, cols_buf, row_sems, col_sems
    )
    fill_tile(tile, n, waits, rows_buf, cols_buf, rows_out, cols_out, out_sems, None, None, sums)
    rows, cols = tile.shape
    payload[...] = jnp.zeros(payload.shape, F32)
    lane, sub = iota((8, 128), 1), iota((8, 128), 0)

    def body(r, _):
        acc = jnp.zeros((8, 128), F32)
        for g in range(16):
            s = sums[pl.ds(pl.multiple_of(r * 128 + g * 8, 8), 8), :]
            acc = acc + jnp.where(lane == sub + 8 * g, jnp.sum(s, axis=1, keepdims=True), 0.0)
        payload[pl.ds(r, 1), :] = jnp.sum(acc, axis=0, keepdims=True)
        return 0

    lax.fori_loop(0, rows // 128, body, 0, unroll=8)
    total = payload[0:rows // 128, :]
    peak[...] = jnp.broadcast_to(most_of(total), peak.shape)
    store_lse(
        total, 0.0, peak[...], payload,
        lambda: safe_columns(
            (rows_out, cols_out, n, a_buf, b_buf, sem), jnp.zeros((cols // 128, 128), F32), payload, wide
        ),
    )
    payload[rows // 128:rows // 128 + 2, :] = plog[0:2, :]


def fine_tile_kernel(info, live_rows, own, x1, x2, x3, y1, y2, y3, s0, s1, s2, s3, tile, part, peak, rows_out,
                     cols_out, rows_buf, cols_buf, row_sems, col_sems, out_sems, tall, acc, a_buf, b_buf, sem):
    n = own.shape[0]
    waits = fetch(
        [own, y1, y2, y3, s0, s1, s2, s3], [own, x1, x2, x3], rows_buf, cols_buf, row_sems, col_sems
    )
    for b, count in enumerate(row_counts(info, info_place(info))):
        tall[b * n:(b + 1) * n, :] = jnp.where(iota((n, 128), 0) < count, 1.0, 0.0)
    fill_tile(tile, n, waits, rows_buf, cols_buf, rows_out, cols_out, out_sems, acc, tall, None)
    rows, cols = tile.shape
    total = jnp.sum(acc[...], axis=0, keepdims=True)
    for k in range(cols // 128):
        part[k:k + 1, :] = total[:, k * 128:(k + 1) * 128]
    h = jnp.where(live_rows[...] > 0.0, 0.0, NEG)
    peak[...] = jnp.broadcast_to(most_of(total), peak.shape)
    store_lse(
        part[...], 0.0, peak[...], part,
        lambda: safe_rows((rows_out, cols_out, n, a_buf, b_buf, sem), h, part, tall),
    )


def fold_y_kernel(plan, *refs):
    parts, out = refs[0:Y], refs[Y]
    out[...] = jnp.zeros(out.shape, F32)
    for first, per in plan["lse"]:
        n = 2 * Y * per
        out[first:first + n, :] = fold_y(parts, first, per)
    if plan["plog"] is not None:
        first, into = plan["plog"]
        out[into:into + 2 * Y, :] = jnp.concatenate(
            [p[first:first + 2, :] for p in parts], axis=0
        )


def coarse2_kernel(mine, other, part, plog, seat, tile, peak, rows_hbm, cols_hbm, payload, plog_rows, tall, *bufs):
    plog_rows[0:8, :] = mine[16:24, :]
    plog_rows[8:16, :] = other[16:24, :]
    h = plog_rows[...] + SC - fold_core(mine, other, 0, 2)
    payload[...] = jnp.zeros(payload.shape, F32)
    reduce_rows(tile, h, peak, payload, tall, (rows_hbm, cols_hbm, PROTO_BLOCK, *bufs))
    payload[8:20, :] = part[...]
    payload[20:22, :] = plog[0:2, :]
    payload[22:25, :] = seat[...]


def fine_h(lse, logs, live, boost=0.0):
    return jnp.where(live[...] > 0.0, SC - logs[0:1, :] - lse + boost, NEG)


def step3_kernel(logs, live_rows, live_cols, p0, p1, p2, p3, ktile, kpeak, krows, kcols, tile, peak, rows_hbm, cols_hbm,
                 payload, plog_cols, seats, wide, kwide, *bufs):
    parts = (p0, p1, p2, p3)
    plog_cols[...] = gather_columns(parts, 20, 2)
    seats[...] = gather_columns(parts, 22, 3)
    payload[...] = jnp.zeros(payload.shape, F32)
    h = fine_h(from_columns(parts, 8, 3), logs, live_cols)
    backup = (rows_hbm, cols_hbm, tile.shape[1] // X, *bufs)
    reduce_columns(tile, h, peak, payload.at[16:40, :], wide, backup, live_rows)
    h = plog_cols[...] + SC - from_columns(parts, 0, 2)
    reduce_columns(ktile, h, kpeak, payload.at[0:16, :], kwide, (krows, kcols, PROTO_BLOCK, *bufs))


def step4_kernel(logs, live_rows, mine, other, plog_rows, ktile, kpeak, krows, kcols, tile, peak, rows_hbm, cols_hbm,
                 payload, tall, ktall, *bufs):
    payload[...] = jnp.zeros(payload.shape, F32)
    h = plog_rows[...] + SC - fold_core(mine, other, 0, 2)
    reduce_rows(ktile, h, kpeak, payload.at[0:8, :], ktall, (krows, kcols, PROTO_BLOCK, *bufs))
    h = fine_h(fold_core(mine, other, 16, 3), logs, live_rows)
    backup = (rows_hbm, cols_hbm, tile.shape[1] // X, *bufs)
    reduce_rows(tile, h, peak, payload.at[8:20, :], tall, backup)


def step5_kernel(logs, live_rows, live_cols, p0, p1, p2, p3, plog_cols, seats, tile, peak, rows_hbm, cols_hbm,
                 payload, coarse, tall, wide, *bufs):
    parts = (p0, p1, p2, p3)
    v = plog_cols[...] + SC - from_columns(parts, 0, 2)
    coarse[...] = v[0:1, :] * (1.0 / SC)
    to_rows(v, tall)
    local = seats[...].astype(jnp.int32)
    boost = []
    for k in range(X * 3):
        vals = tall[(k // 3) * PROTO_BLOCK:(k // 3 + 1) * PROTO_BLOCK, :]
        pick = iota((PROTO_BLOCK, 128), 0) == local[k:k + 1, :]
        boost.append(jnp.sum(jnp.where(pick, vals, 0.0), axis=0, keepdims=True))
    h = fine_h(from_columns(parts, 8, 3), logs, live_cols, jnp.concatenate(boost, axis=0))
    payload[...] = jnp.zeros(payload.shape, F32)
    reduce_columns(tile, h, peak, payload, wide, (rows_hbm, cols_hbm, tile.shape[1] // X, *bufs), live_rows)


def potential(h):
    return jnp.where(h == NEG, 0.0, h)[0:3, :] * (1.0 / SC)


def step6_kernel(logs, live_rows, mine, other, tile, peak, rows_hbm, cols_hbm, payload, out, tall, *bufs):
    h = fine_h(fold_core(mine, other, 0, 3), logs, live_rows)
    out[...] = potential(h)
    payload[...] = jnp.zeros(payload.shape, F32)
    backup = (rows_hbm, cols_hbm, tile.shape[1] // X, *bufs)
    reduce_rows(tile, h, peak, payload, tall, backup)


def last_kernel(logs, live_cols, p0, p1, p2, p3, out):
    out[...] = potential(fine_h(from_columns((p0, p1, p2, p3), 0, 3), logs, live_cols))


def swap(v, axis, bit):
    n = {"z": Z, "c": 2}[axis]
    return lax.ppermute(v, axis, [(i, i ^ bit) for i in range(n)])


def turn(v, axis, k):
    n = {"x": X, "y": Y}[axis]
    return lax.ppermute(
        v, (axis, "c"), [(i * 2 + c, (i + (k if c == 0 else n - k)) % n * 2 + c) for i in range(n) for c in range(2)]
    )


def spread_over(v, axis):
    return [v] + [turn(v, axis, k) for k in (1, 2, 3)]


def vmem(v):
    return pltpu.with_memory_space_constraint(v, pltpu.VMEM)


def held(tile, peak, rows, cols):
    return [vmem(tile), peak, *[pltpu.with_memory_space_constraint(v, HBM) for v in (rows, cols)]]


def local(embeddings, members, counts):
    rows, d = embeddings.shape
    here = jnp.stack([lax.axis_index(a) for a in ("z", "x", "y", "c")]).astype(jnp.int32)
    info = jnp.concatenate(
        [
            jnp.pad(counts, ((0, 0), (0, 128 - counts.shape[1]))),
            jnp.pad(here[None], ((0, 0), (0, 124))),
            members.reshape(rows // 128, 128),
        ],
        axis=0,
    )
    per = rows // 128
    n_rows, n_cols = rows * Y * 2, rows * X
    k_rows, k_cols = PROTO_BLOCK * Y * 2, PROTO_BLOCK * X
    quarter = PROTO_BLOCK // Z
    width = d + PAD

    def first(own):
        return turn(own, "x", 1), turn(own, "x", 3), turn(own, "y", 1), turn(own, "y", 3)

    x1, x3, y1, y3 = first(embeddings)
    keep, send, live_rows, live_cols, seat, logs = call(
        pool_kernel,
        [
            sds((2 * quarter + 8, d)), sds((2 * quarter + 8, d)), sds((n_rows // 128, 128)),
            sds((n_cols // 128, 128)), sds((per, 128)), sds((8, 128)),
        ],
        [SMEM, VMEM, VMEM],
        name="pool",
    )(info, embeddings, info)
    keep, send = call(
        pool2_kernel, [sds((quarter + 8, d)), sds((quarter + 8, d))], [VMEM] * 2, name="pool2"
    )(keep, swap(send, "z", 1))
    got = swap(send, "z", 3)
    x1, x3, y1, y3, got = lax.optimization_barrier((x1, x3, y1, y3, got))
    x2, y2 = turn(x1, "x", 1), turn(y1, "y", 1)
    part = call(means_kernel, sds((quarter, width), BF16), [VMEM] * 2, name="means")(keep, got)
    far = [swap(part, "z", k) for k in (1, 2, 3)]
    x1, y1, y3, x2, y2, embeddings, far = lax.optimization_barrier((x1, y1, y3, x2, y2, embeddings, far))
    means, plog = call(
        join_kernel, [sds((PROTO_BLOCK, d), BF16), sds((8, 128))], [VMEM] * 5, name="join"
    )(logs, part, *far)
    s0, s1, s2, s3 = [swap(v, "c", 1) for v in (embeddings, y1, y2, y3)]
    vectors = [embeddings, x1, x2, x3, y1, y2, y3, s0, s1, s2, s3]

    bufs = [pltpu.VMEM((STEP, d), BF16), pltpu.VMEM((STEP, d), BF16), pltpu.SemaphoreType.DMA]

    def tile_call(body, n, m, part_rows, specs, extra, name):
        out = [pltpu.VMEM((n, m), F32), sds((part_rows, 128)), sds((8, 128)), HBM((n, d), BF16), HBM((m, d), BF16)]
        return call(
            body,
            out,
            specs,
            scratch=[
                pltpu.VMEM((n, d), BF16),
                pltpu.VMEM((m, d), BF16),
                pltpu.SemaphoreType.DMA((2 * Y,)),
                pltpu.SemaphoreType.DMA((X,)),
                pltpu.SemaphoreType.DMA((2,)),
                *extra,
                *bufs,
            ],
            out_specs=[VMEM, VMEM, VMEM, IN_HBM, IN_HBM],
            limit=18,
            name=name,
            flops=2 * n * m * d,
        )

    tall = pltpu.VMEM((n_rows, 128), F32)
    wide = pltpu.VMEM((8, n_cols), F32)
    mx1, mx3, my1, my3 = first(means)
    tile, upart, *back = tile_call(
        fine_tile_kernel, n_rows, n_cols, n_cols // 128, [SMEM, VMEM] + [ANY] * 11, [tall, wide], "fine_tile"
    )(info, live_rows, *vectors)
    upart, means, mx1, mx3, my1, my3 = lax.optimization_barrier((upart, means, mx1, mx3, my1, my3))
    mx2, my2 = turn(mx1, "x", 1), turn(my1, "y", 1)
    t0, t1, t3, t2 = swap(means, "c", 1), swap(my1, "c", 1), swap(my3, "c", 1), swap(my2, "c", 1)
    back = held(tile, *back)

    ktile, part, *kback = tile_call(
        coarse_tile_kernel, k_rows, k_cols, 24, [ANY] * 11 + [VMEM],
        [pltpu.VMEM((k_rows, 128), F32), pltpu.VMEM((8, k_cols), F32)], "coarse_tile"
    )(means, mx1, mx2, mx3, my1, my2, my3, t0, t1, t2, t3, plog)
    kback = held(ktile, *kback)
    kspecs = [VMEM, VMEM, IN_HBM, IN_HBM]
    mine = call(
        lambda *r: fold_y_kernel({"lse": [(0, 2)], "plog": (16, 16)}, *r),
        sds((24, 128)),
        [VMEM] * 4,
        name="fold_y1",
    )(*spread_over(part, "y"))
    other = swap(mine, "c", 1)

    part, plog_rows = call(
        coarse2_kernel,
        [sds((32, 128)), sds((16, 128))],
        [VMEM] * 5 + kspecs,
        scratch=[pltpu.VMEM((k_rows, 128), F32), *bufs],
        name="coarse2",
    )(mine, other, upart, plog, seat, *kback)

    part, plog_cols, seats = call(
        step3_kernel,
        [sds((40, 128)), sds((8, 128)), sds((12, 128))],
        [VMEM] * 7 + kspecs * 2,
        scratch=[wide, pltpu.VMEM((8, k_cols), F32), *bufs],
        name="step3",
    )(logs, live_rows, live_cols, *spread_over(part, "x"), *kback, *back)
    mine = call(
        lambda *r: fold_y_kernel({"lse": [(0, 2), (16, 3)], "plog": None}, *r),
        sds((40, 128)),
        [VMEM] * 4,
        name="fold_y2",
    )(*spread_over(part, "y"))
    other = swap(mine, "c", 1)

    part = call(
        step4_kernel,
        sds((24, 128)),
        [VMEM, VMEM] + [VMEM] * 3 + kspecs * 2,
        scratch=[tall, pltpu.VMEM((k_rows, 128), F32), *bufs],
        name="step4",
    )(logs, live_rows, mine, other, plog_rows, *kback, *back)

    part, coarse = call(
        step5_kernel,
        [sds((24, 128)), sds((1, 128))],
        [VMEM] * 9 + kspecs,
        scratch=[pltpu.VMEM((k_cols, 128), F32), wide, *bufs],
        name="step5",
    )(logs, live_rows, live_cols, *spread_over(part, "x"), plog_cols, seats, *back)
    mine = call(
        lambda *r: fold_y_kernel({"lse": [(0, 3)], "plog": None}, *r),
        sds((24, 128)),
        [VMEM] * 4,
        name="fold_y3",
    )(*spread_over(part, "y"))
    other = swap(mine, "c", 1)

    part, col = call(
        step6_kernel,
        [sds((16, 128)), sds((3, 128))],
        [VMEM, VMEM] + [VMEM] * 2 + kspecs,
        scratch=[tall, *bufs],
        name="step6",
    )(logs, live_rows, mine, other, *back)
    row = call(last_kernel, sds((3, 128)), [VMEM, VMEM] + [VMEM] * 4, name="last")(
        logs, live_cols, *spread_over(part, "x")
    )
    return row.reshape(rows), col.reshape(rows), coarse[0, :quarter]


def solution(mesh):
    split = Mesh(mesh.devices.reshape(Z, X, Y, 2), ("z", "x", "y", "c"))
    every = P(("z", "x", "y", "c"))
    return jax.shard_map(
        local,
        mesh=split,
        in_specs=(P(("z", "x", "y", "c"), None), every, P()),
        out_specs=(every, every, every),
        check_vma=False,
    )
```
